128 devices in a mesh: seq: 32 (over y, z, core), copy: 4 (over x).
Axes of the slice: x: 4, y: 4, z: 4, core: 2. Of those that a mesh axis runs over, the one named last changes fastest.
Arguments:
- frames: bfloat16 [8192, 1280], P('seq'), may hold values from -30 to 30
- utt_lengths: int32 [64], replicated, may hold values from 1 to 256, 8192 in all
- vis_frames: int32 [8, 32, 128], P('copy'), may hold values from 0 to 255, as said below
- vis_count: int32 [8, 32], P('copy'), may hold values from 32 to 128, as said below
- teacher_qkv: bfloat16 [3, 1280, 1280], P(None, None, 'copy'), may hold values from -1 to 1
- teacher_out: bfloat16 [1280, 1280], P('copy'), may hold values from -0.15625 to 0.15625
- student_weights: bfloat16 [5120, 1280], replicated, may hold values from -1 to 1
Outputs:
- grad_weights: float32 [5120, 1280], P(('seq', 'copy'))
The draws below stay inside these ranges and needn't reach their ends.
Inputs may be any that keep to these rules, and one draw needn't show every extreme that they name: `utt_lengths`: the utterances lie end to end and fill all 8192 frames; the longest has exactly 256 frames. `vis_count`: in every copy some block holds exactly 128 visible frames. `vis_frames`: entries below the block's count are distinct and ascending; the others are 0.
All inputs are finite; a program needn't handle non-finite values.
Results may differ from the reference program's by a relative error of at most 0.0045.
The reference program's roundings to bfloat16 on the way count: a program that leaves them out, or rounds other values in their place, can miss the bound.
Values may be sent and summed in bfloat16 or wider, within the bound.
No kernel may reach another device: no remote copies, remote signals or barrier semaphores. Data moves between devices by JAX's collectives and lax.ppermute only.
A program may use at most 192 MiB of HBM per device.

```python
import math
import jax
import jax.numpy as jnp
import numpy as np
from jax import lax

D = 1280
HEADS = 16
HEAD_DIM = 80
TOK_DEV = 256
UMAX = 256
SHARDS = 32
TOKENS = 8192
COPIES = 8
VIS_CAP = 128
UTTS = 64


def visible_sets(base_key):
    count_key, pick_key, full_key = jax.random.split(jax.random.fold_in(base_key, 17), 3)
    counts = jax.random.randint(count_key, (COPIES, SHARDS), VIS_CAP // 4, VIS_CAP + 1)
    full_block = jax.random.randint(full_key, (COPIES, 1), 0, SHARDS)
    counts = jnp.where(jnp.arange(SHARDS)[None, :] == full_block, VIS_CAP, counts)
    perm_keys = jax.random.split(pick_key, COPIES * SHARDS)
    orders = jax.vmap(lambda one_key: jax.random.permutation(one_key, TOK_DEV))(perm_keys).reshape(COPIES, SHARDS, TOK_DEV)
    rank_of = jnp.argsort(orders, axis=-1)
    frame_ids = jnp.arange(TOK_DEV, dtype=jnp.int32)
    chosen = rank_of < counts[..., None]
    listed = jnp.argsort(jnp.where(chosen, frame_ids, TOK_DEV + frame_ids), axis=-1)[..., :VIS_CAP]
    slot_ids = jnp.arange(VIS_CAP, dtype=jnp.int32)
    listed = jnp.where(slot_ids < counts[..., None], listed, 0)
    return (listed.astype(jnp.int32), counts.astype(jnp.int32))


def draw_vis_frames(key, part):
    return visible_sets(key)[0]


def draw_vis_count(key, part):
    return visible_sets(key)[1]


def draw_frames(key, part):
    key = jax.random.fold_in(key, 3)
    noise_key = jax.random.fold_in(key, 0)
    values = jax.random.normal(noise_key, (TOKENS, D), jnp.float32)
    values = jnp.clip(values, -6.0, 6.0)
    return values.astype(jnp.bfloat16)


def draw_teacher_qkv(key, part):
    key = jax.random.fold_in(key, 5)
    main_key = jax.random.fold_in(key, 0)
    values = jnp.clip(jax.random.normal(main_key, (3, D, D), jnp.float32), -6.0, 6.0) * D ** (-0.5)
    return values.astype(jnp.bfloat16)


def draw_student_weights(key, part):
    key = jax.random.fold_in(key, 7)
    main_key = jax.random.fold_in(key, 0)
    values = jnp.clip(jax.random.normal(main_key, (4, D, D), jnp.float32), -6.0, 6.0) * D ** (-0.5)
    return values.reshape(4 * D, D).astype(jnp.bfloat16)


def shard_levels(key, dims, cuts, least, high):
    gain, own = 1.0, jax.random.fold_in(key, 6)
    for position, shards_of in cuts:
        steps = jnp.exp(jax.random.uniform(jax.random.fold_in(own, position), (shards_of,), jnp.float32, least / len(cuts), high / len(cuts)))
        gain = gain * jnp.repeat(steps, dims[position] // shards_of).reshape([-1 if axis == position else 1 for axis in range(len(dims))])
    return gain


def split_up(amount, total, most, lean):
    portions = [(1 << 20) // math.isqrt(rank ** lean) + 1 for rank in range(2, amount + 1)]
    rest, given = total - most - (amount - 1), [1] * (amount - 1)
    while rest > 0:
        candidates = [i for i in range(amount - 1) if given[i] < most]
        pool, left = sum([portions[i] for i in candidates]), rest
        for i in candidates:
            more = min(most - given[i], max(1, left * portions[i] // pool), rest)
            given[i] = given[i] + more
            rest = rest - more
    return np.array([most] + given)


def uneven_parts(stream_key, count, total, reach, lean):
    if count == 2:
        one = jax.random.randint(stream_key, (), max(1, total - reach), min(reach, total - 1) + 1)
        return jnp.stack([one, total - one])
    lengths = jnp.asarray(split_up(count, total, reach, lean), jnp.int32)
    twos = (count - 1) // 2
    source_of, receiver = lengths[1:1 + 2 * twos:2], lengths[2:2 + 2 * twos:2]
    slack = jnp.minimum(source_of - 1, reach - receiver)
    moved = jax.random.randint(jax.random.fold_in(stream_key, 1), (twos,), 0, 1 << 20) % (slack + 1)
    lengths = lengths.at[1:1 + 2 * twos:2].set(source_of - moved).at[2:2 + 2 * twos:2].set(receiver + moved)
    return lengths[jax.random.permutation(jax.random.fold_in(stream_key, 2), count)]


def normal_values(stream_key, dims, deviation, limit, shards=(), kind=jnp.bfloat16):
    level = shard_levels(stream_key, dims, shards, -0.22, 0.18) if shards else 1.0
    result = jax.random.normal(stream_key, dims, jnp.float32) * deviation * level
    return jnp.minimum(jnp.maximum(result, -limit), limit).astype(kind)


def setup_inputs(seed: int = 0) -> dict:
    key_list = jax.random.split(jax.random.key(seed), 8)
    return {
        "frames": draw_frames(jax.random.fold_in(key_list[7], 71), 0),
        "utt_lengths": uneven_parts(key_list[1], UTTS, TOKENS, UMAX, 1).astype(jnp.int32),
        "vis_frames": draw_vis_frames(jax.random.fold_in(key_list[7], 71), 0),
        "vis_count": draw_vis_count(jax.random.fold_in(key_list[7], 71), 0),
        "teacher_qkv": draw_teacher_qkv(jax.random.fold_in(key_list[7], 71), 0),
        "teacher_out": normal_values(key_list[5], (D, D), D ** -0.5, 0.15625, ((0, 4),)),
        "student_weights": draw_student_weights(jax.random.fold_in(key_list[7], 71), 0),
    }


norm_eps = 1e-05
mask_fill = -1e+30

def narrowed(values):
    return lax.optimization_barrier(values.astype(jnp.bfloat16)).astype(jnp.float32)

def layer_norm(values):
    centre = values - lax.optimization_barrier(jnp.mean(values, axis=-1, keepdims=True))
    spread = lax.optimization_barrier(jnp.mean(centre * centre, axis=-1, keepdims=True))
    return centre * lax.rsqrt(spread + norm_eps)

def norm_backward(upstream, normed, values):
    centre = values - lax.optimization_barrier(jnp.mean(values, axis=-1, keepdims=True))
    factor = lax.rsqrt(lax.optimization_barrier(jnp.mean(centre * centre, axis=-1, keepdims=True)) + norm_eps)
    inner_part = upstream - lax.optimization_barrier(jnp.mean(upstream, axis=-1, keepdims=True)) - normed * lax.optimization_barrier(jnp.mean(upstream * normed, axis=-1, keepdims=True))
    return inner_part * factor

def utterance_of(positions, utt_ends):
    return lax.optimization_barrier(jnp.sum((utt_ends[None, :] <= positions[:, None]).astype(jnp.int32), axis=1))

def softmax_rows(scores, allowed):
    masked = jnp.where(allowed, scores, mask_fill)
    row_top = lax.optimization_barrier(jnp.max(masked, axis=-1, keepdims=True))
    expo_vals = jnp.exp(masked - row_top)
    return expo_vals / lax.optimization_barrier(jnp.sum(expo_vals, axis=-1, keepdims=True))

def finish_targets(frames_wide, mixing):
    return layer_norm(0.5 * (frames_wide + layer_norm(frames_wide + mixing))).astype(jnp.bfloat16)

def pick_rows(source_rows, row_index):
    return jax.vmap(lambda one_table, one_index: jnp.take(one_table, one_index, axis=0))(source_rows, row_index)

def teacher_targets(frames, utt_ends, teacher_qkv, teacher_out):
    frame_total = frames.shape[0]
    block_count = frame_total // TOK_DEV
    reach_rows = TOK_DEV + 2 * UMAX
    score_scale = HEAD_DIM ** (-0.5)
    frames_wide = frames.astype(jnp.float32)
    projected = narrowed(jnp.einsum('td,kde->tke', frames_wide, teacher_qkv.astype(jnp.float32)))
    queries = projected[:, 0].reshape(frame_total, HEADS, HEAD_DIM)
    padded = jnp.pad(projected[:, 1:], ((UMAX, UMAX), (0, 0), (0, 0)))
    frame_utt = utterance_of(jnp.arange(frame_total, dtype=jnp.int32), utt_ends)

    def teacher_block(block_id):
        first_row = block_id * TOK_DEV
        query_rows = lax.dynamic_slice_in_dim(queries, first_row, TOK_DEV, 0)
        beside_all = lax.dynamic_slice_in_dim(padded, first_row, reach_rows, 0).reshape(reach_rows, 2, HEADS, HEAD_DIM)
        positions = first_row - UMAX + jnp.arange(reach_rows, dtype=jnp.int32)
        in_range = (positions >= 0) & (positions < frame_total)
        query_utt = lax.dynamic_slice_in_dim(frame_utt, first_row, TOK_DEV, 0)
        allowed = in_range[None, :] & (query_utt[:, None] == utterance_of(positions, utt_ends)[None, :])
        scores = jnp.einsum('qhd,khd->hqk', query_rows, beside_all[:, 0]) * score_scale
        weights_half = narrowed(softmax_rows(scores, allowed[None]))
        mixed_heads = jnp.einsum('hqk,khd->qhd', weights_half, beside_all[:, 1])
        return narrowed(mixed_heads).reshape(TOK_DEV, D)
    attended = lax.map(teacher_block, jnp.arange(block_count, dtype=jnp.int32))
    attended = attended.reshape(frame_total, D).astype(jnp.bfloat16)
    mixing = jnp.dot(attended, teacher_out, preferred_element_type=jnp.float32)
    return finish_targets(frames_wide, mixing)

def student_copy(frame_blocks, goal_blocks, vis_list, vis_live_count, w_in, w_out, utt_ends, loss_coef):
    block_count, vis_cap = vis_list.shape
    score_scale = HEAD_DIM ** (-0.5)
    visible = pick_rows(frame_blocks, vis_list).astype(jnp.float32)
    goals_all = pick_rows(goal_blocks, vis_list).astype(jnp.float32)
    slot_ids = jnp.arange(vis_cap, dtype=jnp.int32)
    is_live = slot_ids[None, :] < vis_live_count[:, None]
    positions = jnp.arange(block_count, dtype=jnp.int32)[:, None] * TOK_DEV + vis_list
    row_utt = utterance_of(positions.reshape(-1), utt_ends).reshape(block_count, vis_cap)
    projected = narrowed(jnp.einsum('svd,kde->svke', visible, w_in))
    proj_pad = jnp.pad(projected, ((1, 1), (0, 0), (0, 0), (0, 0)))
    live_pad = jnp.pad(is_live, ((1, 1), (0, 0)))
    utt_pad = jnp.pad(row_utt, ((1, 1), (0, 0)), constant_values=-1)
    term_init = jnp.zeros((block_count + 2, vis_cap, 2 * D), jnp.float32)

    def student_block(term_sums, block_id):
        beside_all = lax.dynamic_slice_in_dim(proj_pad, block_id, 3, 0).reshape(3 * vis_cap, 3, HEADS, HEAD_DIM)
        key_live = lax.dynamic_slice_in_dim(live_pad, block_id, 3, 0).reshape(-1)
        key_utt = lax.dynamic_slice_in_dim(utt_pad, block_id, 3, 0).reshape(-1)
        queries = projected[block_id, :, 0].reshape(vis_cap, HEADS, HEAD_DIM)
        allowed = key_live[None, :] & (row_utt[block_id][:, None] == key_utt[None, :])
        scores = jnp.einsum('qhd,khd->hqk', queries, beside_all[:, 1]) * score_scale
        probs = softmax_rows(scores, allowed[None])
        probs_half = narrowed(probs)
        attended = narrowed(jnp.einsum('hqk,khd->qhd', probs_half, beside_all[:, 2])).reshape(vis_cap, D)
        summed_in = visible[block_id] + jnp.dot(attended.astype(jnp.bfloat16), w_out, preferred_element_type=jnp.float32)
        normed = layer_norm(summed_in)
        upstream = jnp.where(is_live[block_id][:, None], (normed - goals_all[block_id]) * loss_coef, 0.0)
        norm_grad = narrowed(norm_backward(upstream, normed, summed_in))
        attn_grad = narrowed(jnp.dot(norm_grad.astype(jnp.bfloat16), w_out.T, preferred_element_type=jnp.float32))
        grad_heads = attn_grad.reshape(vis_cap, HEADS, HEAD_DIM)
        prob_grad = jnp.einsum('qhd,khd->hqk', grad_heads, beside_all[:, 2])
        score_grad = narrowed(probs * (prob_grad - lax.optimization_barrier(jnp.sum(probs * prob_grad, axis=-1, keepdims=True))) * score_scale)
        query_grad = narrowed(jnp.einsum('hqk,khd->qhd', score_grad, beside_all[:, 1])).reshape(vis_cap, D)
        key_grad = narrowed(jnp.einsum('hqk,qhd->khd', score_grad, queries)).reshape(3, vis_cap, D)
        value_grad = narrowed(jnp.einsum('hqk,qhd->khd', probs_half, grad_heads)).reshape(3, vis_cap, D)
        current = lax.dynamic_slice_in_dim(term_sums, block_id, 3, 0)
        term_sums = lax.dynamic_update_slice_in_dim(term_sums, current + jnp.concatenate([key_grad, value_grad], axis=-1), block_id, 0)
        return (term_sums, (query_grad, attended, norm_grad))
    term_sums, outputs = lax.scan(student_block, term_init, jnp.arange(block_count, dtype=jnp.int32))
    query_grads, attended_all, norm_grads = outputs
    grad_q = jnp.einsum('svd,sve->de', visible, query_grads)
    grad_kv = jnp.einsum('svd,sve->de', visible, term_sums[1:-1])
    grad_o = jnp.einsum('svd,sve->de', attended_all, norm_grads)
    return (grad_q, grad_kv, grad_o)

def reference(frames, utt_lengths, vis_frames, vis_count, teacher_qkv, teacher_out, student_weights):
    utt_ends = jnp.cumsum(utt_lengths)
    targets = teacher_targets(frames, utt_ends, teacher_qkv, teacher_out)
    block_count = frames.shape[0] // TOK_DEV
    frame_blocks = frames.reshape(block_count, TOK_DEV, D)
    goal_blocks = targets.reshape(block_count, TOK_DEV, D)
    w_in = student_weights[:3 * D].reshape(3, D, D).astype(jnp.float32)
    w_out = student_weights[3 * D:]
    loss_coef = 2.0 / (D ** 0.5 * COPIES)

    def one_copy(carried, inputs):
        vis_list, vis_live_count = inputs
        part_q, part_kv, part_o = student_copy(frame_blocks, goal_blocks, vis_list, vis_live_count, w_in, w_out, utt_ends, loss_coef)
        return ((carried[0] + part_q, carried[1] + part_kv, carried[2] + part_o), None)
    start_sums = (jnp.zeros((D, D), jnp.float32), jnp.zeros((D, 2 * D), jnp.float32), jnp.zeros((D, D), jnp.float32))
    sums, unused = lax.scan(one_copy, start_sums, (vis_frames, vis_count))
    grad_q, grad_kv, grad_o = sums
    return jnp.concatenate([grad_q, grad_kv[:, :D], grad_kv[:, D:], grad_o], axis=0)
```

```python
import functools

import jax
import jax.numpy as jnp
from jax import lax
from jax.experimental import pallas as pl
from jax.experimental.pallas import tpu as pltpu
from jax.sharding import PartitionSpec as P

HEADS = 16
HEAD_DIM = 80
LANES = 128
CHUNKS = 2
CORES = 2
RING = 4

norm_eps = 1e-05
mask_fill = -1e30
score_scale = HEAD_DIM ** (-0.5)
bf16 = jnp.bfloat16
f32 = jnp.float32
VMEM = pl.BlockSpec(memory_space=pltpu.VMEM)
SMEM = pl.BlockSpec(memory_space=pltpu.SMEM)


def dot(a, b):
    return lax.dot_general(a, b, (((1,), (0,)), ((), ())), preferred_element_type=f32)


def dot_nt(a, b):
    return lax.dot_general(a, b, (((1,), (1,)), ((), ())), preferred_element_type=f32)


def dot_tn(a, b):
    return lax.dot_general(a, b, (((0,), (0,)), ((), ())), preferred_element_type=f32)


def widen_heads(x):
    rows, cols = x.shape
    gap = jnp.zeros((rows, LANES - HEAD_DIM), x.dtype)
    parts = []
    for h in range(cols // HEAD_DIM):
        parts += [x[:, h * HEAD_DIM : (h + 1) * HEAD_DIM], gap]
    return jnp.concatenate(parts, axis=1)


def narrow_heads(x):
    return jnp.concatenate(
        [x[:, h * LANES : h * LANES + HEAD_DIM] for h in range(x.shape[1] // LANES)], axis=1
    )


def softmax_rows(scores, allowed):
    masked = jnp.where(allowed, scores, mask_fill)
    expo = jnp.exp(masked - jnp.max(masked, axis=-1, keepdims=True))
    return expo * (1.0 / jnp.sum(expo, axis=-1, keepdims=True))


def layer_norm(values):
    centre = values - jnp.mean(values, axis=-1, keepdims=True)
    spread = jnp.mean(centre * centre, axis=-1, keepdims=True)
    return centre * lax.rsqrt(spread + norm_eps)


def params(mib=48):
    return pltpu.CompilerParams(vmem_limit_bytes=mib << 20)


def teacher_kernel(own_ref, beside_ref, utt_col_ref, utt_row_ref, out_ref):
    rows = own_ref.shape[0]
    cols = own_ref.shape[1] // 3
    own = own_ref[...]
    query = widen_heads(own[:, :cols])
    key_own, value_own = widen_heads(own[:, cols : 2 * cols]), widen_heads(own[:, 2 * cols :])
    key_side = widen_heads(beside_ref[:, :cols])
    value_side = widen_heads(beside_ref[:, cols:])
    allowed = utt_col_ref[...] == utt_row_ref[...]
    parts = []
    for h in range(cols // HEAD_DIM):
        sl = slice(h * LANES, (h + 1) * LANES)
        keys = jnp.concatenate([key_side[:rows, sl], key_own[:, sl], key_side[rows:, sl]], axis=0)
        vals = jnp.concatenate(
            [value_side[:rows, sl], value_own[:, sl], value_side[rows:, sl]], axis=0
        )
        probs = softmax_rows(dot_nt(query[:, sl], keys) * score_scale, allowed).astype(bf16)
        parts.append(dot(probs, vals).astype(bf16)[:, :HEAD_DIM])
    attn = jnp.concatenate(parts, axis=1)
    out_ref[...] = jnp.concatenate([attn[: rows // 2], attn[rows // 2 :]], axis=1)


def targets_kernel(parity_ref, attn_ref, mine_ref, other_ref, frames_ref, out_ref):
    groups, half_rows, wide = attn_ref.shape
    cols = wide // 2
    part = cols // 2
    even = parity_ref[0] == 0
    low, high = [], []
    for g in range(groups):
        block = attn_ref[g]
        rows = jnp.concatenate([block[:, :cols], block[:, cols:]], axis=0)
        low.append(rows[:, :part])
        high.append(rows[:, part:])
    low, high = jnp.concatenate(low, axis=1), jnp.concatenate(high, axis=1)
    depth, width = groups * part, mine_ref.shape[-1]
    mine = mine_ref[...].reshape(depth, width)
    other = other_ref[...].reshape(depth, width)
    lhs_mine = jnp.where(even, low, high)
    lhs_other = jnp.where(even, high, low)
    wide_frames = frames_ref[...].astype(f32)
    mixing = dot(lhs_mine, mine) + dot(lhs_other, other)
    out_ref[...] = layer_norm(0.5 * (wide_frames + layer_norm(wide_frames + mixing))).astype(bf16)


def select_rows(index_col, count):
    rows = index_col.shape[0]
    return (lax.broadcasted_iota(jnp.int32, (rows, count), 1) == index_col).astype(bf16)


def select_rows_t(index_row, count):
    rows = index_row.shape[1]
    return (lax.broadcasted_iota(jnp.int32, (count, rows), 0) == index_row).astype(bf16)


def forward_kernel(
    own_ref, beside_ref, pick_ref, utt_col_ref, utt_row_ref,
    attn_ref, prob_ref, query_ref, kv_ref, proj_scr, side_scr,
):
    step = pl.program_id(0)
    tok = own_ref.shape[0]
    cols = own_ref.shape[1] // 3
    heads = cols // HEAD_DIM
    wide = heads * LANES
    slots = pick_ref.shape[1] // 3

    @pl.when(step == 0)
    def _():
        proj_scr[...] = widen_heads(own_ref[...])
        side_scr[...] = widen_heads(beside_ref[...])

    picks = [select_rows(pick_ref[0, j * slots : (j + 1) * slots, :], tok) for j in range(3)]
    tables = [side_scr[:tok, :], proj_scr[:, wide:], side_scr[tok:, :]]
    kv = jnp.concatenate([dot(p, t).astype(bf16) for p, t in zip(picks, tables)], axis=0)
    query = dot(picks[1], proj_scr[:, :wide]).astype(bf16)
    query_ref[0] = query
    kv_ref[0] = kv
    allowed = utt_col_ref[0, slots : 2 * slots, :] == utt_row_ref[0]
    parts = []
    for h in range(heads):
        sl = slice(h * LANES, (h + 1) * LANES)
        probs = softmax_rows(dot_nt(query[:, sl], kv[:, sl]) * score_scale, allowed)
        prob_ref[0, h] = probs
        vals = kv[:, wide + h * LANES : wide + (h + 1) * LANES]
        parts.append(dot(probs.astype(bf16), vals).astype(bf16)[:, :HEAD_DIM])
    attn = jnp.concatenate(parts, axis=1)

    @pl.when(lax.rem(step, 2) == 0)
    def _():
        attn_ref[0, :, :cols] = attn

    @pl.when(lax.rem(step, 2) == 1)
    def _():
        attn_ref[0, :, cols:] = attn


def backward_kernel(
    place_ref, attn_ref, wout_ref, frames_ref, goal_ref, pick_col_ref, pick_row_ref,
    prob_ref, query_ref, kv_ref,
    gq_ref, gkv_ref, go_ref, full_scr, attn_scr, ng_scr, dq_scr, dkv_scr, *, coef,
):
    step = pl.program_id(0)
    last = pl.num_programs(0) - 1
    tok, width = frames_ref.shape
    groups = attn_ref.shape[0]
    cols = attn_ref.shape[3] // 2
    heads = cols // HEAD_DIM
    wide = heads * LANES
    slots = attn_ref.shape[2]
    place = place_ref[0]

    for half in range(2):
        @pl.when(lax.rem(step, 2) == half)
        def _():
            for g in range(groups):
                full_scr[:, g * cols : (g + 1) * cols] = attn_ref[
                    g, 0, :, half * cols : (half + 1) * cols
                ]

    attn = full_scr[...]
    here = pl.ds(pl.multiple_of(step * slots, slots), slots)
    attn_scr[here, :] = attn
    pick_col = pick_col_ref[0, slots : 2 * slots, :]
    pick = select_rows(pick_col, tok)
    live = pick_col >= 0
    summed = dot(pick, frames_ref[...]) + dot(attn, wout_ref[...])
    goal = dot(pick, goal_ref[...])
    centre = summed - jnp.mean(summed, axis=-1, keepdims=True)
    factor = lax.rsqrt(jnp.mean(centre * centre, axis=-1, keepdims=True) + norm_eps)
    normed = centre * factor
    upstream = jnp.where(live, (normed - goal) * coef, 0.0)
    norm_grad = (
        (
            upstream
            - jnp.mean(upstream, axis=-1, keepdims=True)
            - normed * jnp.mean(upstream * normed, axis=-1, keepdims=True)
        )
        * factor
    ).astype(bf16)
    for g in range(groups):
        @pl.when(place == g)
        def _():
            ng_scr[here, :] = norm_grad[:, g * cols : (g + 1) * cols]

    own_rows = wout_ref[pl.ds(pl.multiple_of(place * cols, cols), cols), :]
    attn_grad = widen_heads(dot_nt(norm_grad, own_rows).astype(bf16))
    for h in range(heads):
        sl = slice(h * LANES, (h + 1) * LANES)
        sv = slice(wide + h * LANES, wide + (h + 1) * LANES)
        probs = prob_ref[0, h]
        grad = attn_grad[:, sl]
        prob_grad = dot_nt(grad, kv_ref[0, :, sv])
        inner = jnp.sum(probs * prob_grad, axis=-1, keepdims=True)
        score_grad = (probs * (prob_grad - inner) * score_scale).astype(bf16)
        dq_scr[here, sl] = dot(score_grad, kv_ref[0, :, sl]).astype(bf16)
        dkv_scr[step, :, sl] = dot_tn(score_grad, query_ref[0, :, sl]).astype(bf16)
        dkv_scr[step, :, sv] = dot_tn(probs.astype(bf16), grad).astype(bf16)

    @pl.when(step == last)
    def _():
        members = dkv_scr.shape[0]
        for j in range(3):
            total = None
            sums = None
            for m in range(members):
                pick_t = select_rows_t(pick_row_ref[m, :, j * slots : (j + 1) * slots], tok)
                term = dot(pick_t, dkv_scr[m, j * slots : (j + 1) * slots, :])
                total = term if total is None else total + term
                if j == 1:
                    term = dot(pick_t, dq_scr[m * slots : (m + 1) * slots, :])
                    sums = term if sums is None else sums + term
            gkv_ref[j * tok : (j + 1) * tok, :] = total
            if j == 1:
                gq_ref[...] = sums
        go_ref[...] = dot_tn(attn_scr[...], ng_scr[...])


def weights_kernel(half_ref, left_ref, own_ref, right_ref, *refs):
    gq_refs, gkv_refs, go_refs = refs[:CHUNKS], refs[CHUNKS : 2 * CHUNKS], refs[2 * CHUNKS : 3 * CHUNKS]
    qk_ref, vo_ref, qk_scr, v_scr = refs[3 * CHUNKS :]
    tok = own_ref.shape[0]
    wide = gq_refs[0].shape[1]
    cols = wide // LANES * HEAD_DIM
    reach = 3 * tok

    @pl.when(pl.program_id(0) == 0)
    def _():
        total = gkv_refs[0][...]
        query = gq_refs[0][...]
        for c in range(1, CHUNKS):
            total = total + gkv_refs[c][...]
            query = query + gq_refs[c][...]
        gap = jnp.zeros((tok, cols), f32)
        query = jnp.concatenate([gap, narrow_heads(query), gap], axis=0)
        both = jnp.concatenate([query, narrow_heads(total[:, :wide])], axis=1)
        value = narrow_heads(total[:, wide:])
        for scr, full in ((qk_scr, both), (v_scr, value)):
            top = full.astype(bf16)
            scr[:reach] = top
            scr[reach:] = (full - top.astype(f32)).astype(bf16)

    lhs = jnp.concatenate([left_ref[...], own_ref[...], right_ref[...]], axis=0)
    lhs = jnp.concatenate([lhs, lhs], axis=0)
    qk_ref[...] = dot_tn(lhs, qk_scr[...])
    out = go_refs[0][...]
    for c in range(1, CHUNKS):
        out = out + go_refs[c][...]
    vo_ref[:, :cols] = dot_tn(lhs, v_scr[...])
    vo_ref[:, cols:] = out


def weight_grads(half, left, own, right, gq, gkv, go):
    tok, width = own.shape
    cols = go[0].shape[1]
    block = LANES
    steps = width // block // CORES
    row_block = lambda k, half: (half[0] * steps + k, 0)
    col_block = lambda k, half: (0, half[0] * steps + k)
    whole = lambda a: pl.BlockSpec(a.shape, lambda k, half: (0, 0))
    frames_spec = pl.BlockSpec((tok, block), col_block)
    return pl.pallas_call(
        weights_kernel,
        grid_spec=pltpu.PrefetchScalarGridSpec(
            num_scalar_prefetch=1,
            grid=(steps,),
            in_specs=[frames_spec] * 3
            + [whole(a) for a in gq]
            + [whole(a) for a in gkv]
            + [pl.BlockSpec((block, cols), row_block) for a in go],
            out_specs=[pl.BlockSpec((block, 2 * cols), lambda k, half: (k, 0))] * 2,
            scratch_shapes=[
                pltpu.VMEM((6 * tok, 2 * cols), bf16),
                pltpu.VMEM((6 * tok, cols), bf16),
            ],
        ),
        out_shape=[jax.ShapeDtypeStruct((steps * block, 2 * cols), f32)] * 2,
        compiler_params=params(),
        cost_estimate=pl.CostEstimate(
            flops=2 * 6 * tok * width // 2 * 3 * cols, bytes_accessed=16 << 20, transcendentals=0
        ),
        name="weight_grads",
    )(half, left, own, right, *gq, *gkv, *go)


def ring_sum(value, place, count, pairs_of):
    rows = value.shape[0] // count
    piece = lambda k: lax.dynamic_slice_in_dim(value, lax.rem(place + k, count) * rows, rows, 0)
    arrived = [lax.ppermute(piece(k), "seq", pairs_of(k)) for k in (2, 1, 3) if k < count]
    total = piece(0)
    for part in arrived:
        total = total + part
    return total


def utterance_of(positions, utt_ends):
    return jnp.sum((utt_ends <= positions[..., None]).astype(jnp.int32), axis=-1)


def per_device(
    frames, utt_lengths, vis_frames, vis_count, teacher_qkv, teacher_out, student_weights
):
    tok, width = frames.shape
    seq, seq_count = lax.axis_index("seq"), lax.axis_size("seq")
    place, groups = lax.axis_index("copy"), lax.axis_size("copy")
    cols = teacher_out.shape[0]
    heads = cols // HEAD_DIM
    wide = heads * LANES
    first_frame = seq * tok
    copies = vis_frames.shape[0] * groups
    slots = vis_frames.shape[2]
    members = copies // CHUNKS
    core = lax.rem(seq, CORES)
    swap = [(n, n ^ 1) for n in range(seq_count)]

    up = [(n, n + 1) for n in range(seq_count - 1)]
    left = lax.ppermute(frames, "seq", up)
    right = lax.ppermute(frames, "seq", [(j, n) for n, j in up])

    near = seq - 1 + jnp.arange(3, dtype=jnp.int32)
    inside = (near >= 0) & (near < seq_count)
    near_ids = jnp.clip(near, 0, seq_count - 1)
    near_lists = jnp.take(vis_frames, near_ids, axis=1)
    near_counts = jnp.where(inside, jnp.take(vis_count, near_ids, axis=1), 0)
    near_live = jnp.arange(slots, dtype=jnp.int32) < near_counts[..., None]
    picks = lax.all_gather(jnp.where(near_live, near_lists, -1), "copy", axis=0, tiled=True)

    half_rows = cols // CORES
    out_mine = lax.all_gather(
        lax.dynamic_slice_in_dim(teacher_out, core * half_rows, half_rows, 0), "copy", axis=0
    )
    out_other = lax.ppermute(out_mine, "seq", swap)

    utt_ends = jnp.cumsum(utt_lengths)
    reach_pos = first_frame - tok + jnp.arange(3 * tok, dtype=jnp.int32)
    reach_in = (reach_pos >= 0) & (reach_pos < seq_count * tok)
    reach_utt = jnp.where(reach_in, utterance_of(reach_pos, utt_ends), -1)
    slot_pos = (near * tok)[None, :, None] + picks
    slot_utt = jnp.where(picks >= 0, utterance_of(slot_pos, utt_ends), -1)
    pick_col = picks.reshape(copies, 3 * slots, 1)
    pick_row = picks.reshape(copies, 1, 3 * slots)
    utt_col = slot_utt.reshape(copies, 3 * slots, 1)
    utt_row = slot_utt.reshape(copies, 1, 3 * slots)

    w_in = lax.dynamic_slice_in_dim(student_weights[: 3 * width], place * cols, cols, 1)
    w_in = w_in.reshape(3, width, cols)
    w_out = student_weights[3 * width :]

    def project(rows, weights):
        return jnp.concatenate(
            [jnp.dot(rows, w, preferred_element_type=f32).astype(bf16) for w in weights], axis=1
        )

    beside = jnp.concatenate([left, right], axis=0)
    own_student = project(frames, w_in)
    own_teacher = project(frames, teacher_qkv)
    side_student = project(beside, w_in[1:])
    side_teacher = project(beside, teacher_qkv[1:])

    teacher_attn = pl.pallas_call(
        teacher_kernel,
        in_specs=[VMEM] * 4,
        out_specs=VMEM,
        out_shape=jax.ShapeDtypeStruct((tok // 2, 2 * cols), bf16),
        compiler_params=params(),
        cost_estimate=pl.CostEstimate(
            flops=4 * heads * tok * 3 * tok * LANES,
            bytes_accessed=2 << 20,
            transcendentals=heads * tok * 3 * tok,
        ),
        name="teacher_attn",
    )(own_teacher, side_teacher, reach_utt[tok : 2 * tok].reshape(tok, 1), reach_utt.reshape(1, 3 * tok))
    teacher_all = lax.all_gather(teacher_attn, "copy", axis=0)

    saved, gathered = [], []
    whole2 = lambda a: pl.BlockSpec(a.shape, lambda c: (0, 0))
    for chunk in range(CHUNKS):
        base = chunk * members
        per_copy = lambda shape: pl.BlockSpec(
            (1,) + shape, lambda c, base=base: (base + c,) + (0,) * len(shape)
        )
        out_copy = lambda shape: pl.BlockSpec((1,) + shape, lambda c: (c,) + (0,) * len(shape))
        attn, probs, query, kv = pl.pallas_call(
            forward_kernel,
            grid=(members,),
            in_specs=[
                whole2(own_student),
                whole2(side_student),
                per_copy((3 * slots, 1)),
                per_copy((3 * slots, 1)),
                per_copy((1, 3 * slots)),
            ],
            out_specs=[
                pl.BlockSpec((1, slots, 2 * cols), lambda c: (c // 2, 0, 0)),
                out_copy((heads, slots, 3 * slots)),
                out_copy((slots, wide)),
                out_copy((3 * slots, 2 * wide)),
            ],
            out_shape=[
                jax.ShapeDtypeStruct((members // 2, slots, 2 * cols), bf16),
                jax.ShapeDtypeStruct((members, heads, slots, 3 * slots), f32),
                jax.ShapeDtypeStruct((members, slots, wide), bf16),
                jax.ShapeDtypeStruct((members, 3 * slots, 2 * wide), bf16),
            ],
            scratch_shapes=[
                pltpu.VMEM((tok, 3 * wide), bf16),
                pltpu.VMEM((2 * tok, 2 * wide), bf16),
            ],
            compiler_params=params(),
            cost_estimate=pl.CostEstimate(
                flops=members * (4 * heads * slots * 3 * slots * LANES + 2 * slots * tok * 7 * wide),
                bytes_accessed=8 << 20,
                transcendentals=members * heads * slots * 3 * slots,
            ),
            name=f"student_forward{chunk}",
        )(own_student, side_student, pick_col, utt_col, utt_row)
        gathered.append(lax.all_gather(attn, "copy", axis=0))
        saved.append((probs, query, kv))

    targets = pl.pallas_call(
        targets_kernel,
        in_specs=[SMEM] + [VMEM] * 4,
        out_specs=VMEM,
        out_shape=jax.ShapeDtypeStruct((tok, width), bf16),
        compiler_params=params(),
        cost_estimate=pl.CostEstimate(
            flops=2 * tok * width * width, bytes_accessed=5 << 20, transcendentals=0
        ),
        name="teacher_targets",
    )(core.reshape(1), teacher_all, out_mine, out_other, frames)

    coef = 2.0 / (width**0.5 * copies)
    gq, gkv, go = [], [], []
    for chunk in range(CHUNKS):
        base = chunk * members
        per_copy = lambda shape: pl.BlockSpec(
            (1,) + shape, lambda c, base=base: (base + c,) + (0,) * len(shape)
        )
        in_copy = lambda shape: pl.BlockSpec((1,) + shape, lambda c: (c,) + (0,) * len(shape))
        probs, query, kv = saved[chunk]
        part_q, part_kv, part_o = pl.pallas_call(
            functools.partial(backward_kernel, coef=coef),
            grid=(members,),
            in_specs=[
                SMEM,
                pl.BlockSpec((groups, 1, slots, 2 * cols), lambda c: (0, c // 2, 0, 0)),
                whole2(w_out),
                whole2(frames),
                whole2(targets),
                per_copy((3 * slots, 1)),
                pl.BlockSpec((members, 1, 3 * slots), lambda c, chunk=chunk: (chunk, 0, 0)),
                in_copy((heads, slots, 3 * slots)),
                in_copy((slots, wide)),
                in_copy((3 * slots, 2 * wide)),
            ],
            out_specs=[
                pl.BlockSpec((tok, wide), lambda c: (0, 0)),
                pl.BlockSpec((3 * tok, 2 * wide), lambda c: (0, 0)),
                pl.BlockSpec((width, cols), lambda c: (0, 0)),
            ],
            out_shape=[
                jax.ShapeDtypeStruct((tok, wide), f32),
                jax.ShapeDtypeStruct((3 * tok, 2 * wide), f32),
                jax.ShapeDtypeStruct((width, cols), f32),
            ],
            scratch_shapes=[
                pltpu.VMEM((slots, width), bf16),
                pltpu.VMEM((members * slots, width), bf16),
                pltpu.VMEM((members * slots, cols), bf16),
                pltpu.VMEM((members * slots, wide), bf16),
                pltpu.VMEM((members, 3 * slots, 2 * wide), bf16),
            ],
            compiler_params=params(),
            cost_estimate=pl.CostEstimate(
                flops=members * slots * width * width * 4, bytes_accessed=16 << 20, transcendentals=0
            ),
            name=f"student_backward{chunk}",
        )(
            place.reshape(1), gathered[chunk], w_out, frames, targets, pick_col, pick_row,
            probs, query, kv,
        )
        gq.append(part_q)
        gkv.append(part_kv)
        go.append(part_o)

    away = weight_grads((1 - core).reshape(1), left, frames, right, gq, gkv, go)
    arrived = [lax.ppermute(a, "seq", swap) for a in away]
    kept = weight_grads(core.reshape(1), left, frames, right, gq, gkv, go)
    kept = [a + b for a, b in zip(kept, arrived)]

    ring = RING
    far = seq_count // CORES // ring
    z_place = lax.rem(seq // CORES, ring)
    y_place = seq // (CORES * ring)

    def z_pairs(k):
        return [
            (n, n // (CORES * ring) * (CORES * ring) + ((n // CORES + k) % ring) * CORES + n % CORES)
            for n in range(seq_count)
        ]

    def y_pairs(k):
        return [(n, (n + k * CORES * ring) % seq_count) for n in range(seq_count)]

    first_z = ring_sum(kept[0], z_place, ring, z_pairs)
    first_y = ring_sum(kept[1], y_place, far, y_pairs)
    sum_qk = ring_sum(first_z, y_place, far, y_pairs)
    sum_vo = ring_sum(first_y, z_place, ring, z_pairs)

    rows = width // seq_count
    per_row = groups
    mats = groups
    parts = jnp.stack(
        [sum_qk[:, :cols], sum_qk[:, cols:], sum_vo[:, :cols], sum_vo[:, cols:]]
    )

    def row_block(s, mat):
        c, z, y = s % CORES, s // CORES % ring, s // (CORES * ring)
        return (c * ring + z) * far + y if mat < 2 else (c * far + y) * ring + z

    def target(s, mat):
        return mat * seq_count + row_block(s, mat)

    received = []
    for turn in range(mats):
        mine = lax.dynamic_index_in_dim(parts, lax.rem(place + turn, mats), 0, keepdims=False)
        pairs = [
            (s * groups + g, target(s, (g + turn) % mats))
            for s in range(seq_count)
            for g in range(groups)
        ]
        received.append(lax.ppermute(mine, ("seq", "copy"), pairs))
    own_mat = (seq * groups + place) // seq_count
    received = jnp.stack(received)
    order = lax.rem(own_mat - jnp.arange(groups, dtype=jnp.int32) + groups, mats)
    blocks = jnp.take(received, order, axis=0)
    return jnp.transpose(blocks, (1, 0, 2)).reshape(rows, groups * cols)


def solution(mesh):
    placed = (
        P("seq", None),
        P(),
        P("copy", None, None),
        P("copy", None),
        P(None, None, "copy"),
        P("copy", None),
        P(),
    )
    return jax.shard_map(
        per_device, mesh=mesh, in_specs=placed, out_specs=P(("seq", "copy"), None), check_vma=False
    )
```

```python
import functools

import jax
import jax.numpy as jnp
from jax import lax
from jax.experimental import pallas as pl
from jax.experimental.pallas import tpu as pltpu
from jax.sharding import PartitionSpec as P

HEADS = 16
HEAD_DIM = 80
LANES = 128
CHUNKS = 2
CORES = 2
RING = 4

norm_eps = 1e-05
mask_fill = -1e30
score_scale = HEAD_DIM ** (-0.5)
bf16 = jnp.bfloat16
f32 = jnp.float32
VMEM = pl.BlockSpec(memory_space=pltpu.VMEM)
SMEM = pl.BlockSpec(memory_space=pltpu.SMEM)
HBM = pl.BlockSpec(memory_space=pl.ANY)


def dot(a, b):
    return lax.dot_general(a, b, (((1,), (0,)), ((), ())), preferred_element_type=f32)


def dot_nt(a, b):
    return lax.dot_general(a, b, (((1,), (1,)), ((), ())), preferred_element_type=f32)


def dot_tn(a, b):
    return lax.dot_general(a, b, (((0,), (0,)), ((), ())), preferred_element_type=f32)


def widen_heads(x):
    rows, cols = x.shape
    gap = jnp.zeros((rows, LANES - HEAD_DIM), x.dtype)
    parts = []
    for h in range(cols // HEAD_DIM):
        parts += [x[:, h * HEAD_DIM : (h + 1) * HEAD_DIM], gap]
    return jnp.concatenate(parts, axis=1)


def narrow_heads(x):
    return jnp.concatenate(
        [x[:, h * LANES : h * LANES + HEAD_DIM] for h in range(x.shape[1] // LANES)], axis=1
    )


def softmax_rows(scores, allowed):
    masked = jnp.where(allowed, scores, mask_fill)
    expo = jnp.exp(masked - jnp.max(masked, axis=-1, keepdims=True))
    return expo * (1.0 / jnp.sum(expo, axis=-1, keepdims=True))


def layer_norm(values):
    centre = values - jnp.mean(values, axis=-1, keepdims=True)
    spread = jnp.mean(centre * centre, axis=-1, keepdims=True)
    return centre * lax.rsqrt(spread + norm_eps)


def params(mib=60):
    return pltpu.CompilerParams(vmem_limit_bytes=mib << 20)


def column_of(row):
    count = row.shape[1]
    return jnp.transpose(jnp.broadcast_to(row, (count, count)))


def select_rows(row, count):
    slots = row.shape[1]
    column = column_of(row)
    column = jnp.concatenate([column] * (count // slots), axis=1)
    return (lax.broadcasted_iota(jnp.int32, (slots, count), 1) == column).astype(bf16)


def select_rows_t(row, count):
    slots = row.shape[1]
    return (lax.broadcasted_iota(jnp.int32, (count, slots), 0) == row).astype(bf16)


def split_pair(x):
    gap = jnp.zeros((x.shape[0], LANES), x.dtype)
    top = jnp.concatenate([x[:, :LANES], gap], axis=1)
    low = jnp.concatenate([gap, x[:, LANES:]], axis=1)
    return jnp.concatenate([top, low], axis=0)


def join_pair(x):
    rows = x.shape[0] // 2
    return jnp.concatenate([x[:rows, :LANES], x[rows:, LANES:]], axis=1)


def project_kernel(spot_ref, *refs, sides):
    rows_refs, (w0, w1, w2, wt, student_ref, teacher_ref) = refs[:sides], refs[sides:]
    cols = wt.shape[2]
    rows = jnp.concatenate([r[...] for r in rows_refs], axis=0)
    weights = jnp.concatenate([w0[...], w1[...], w2[...]], axis=1)
    student = dot(rows, weights).astype(bf16)
    teacher_ref[...] = widen_heads(dot(rows, wt[0]).astype(bf16))
    shift = LANES // 2
    for odd in range(2):
        @pl.when(spot_ref[1] == odd)
        def _():
            student_ref[...] = widen_heads(student[:, odd * shift : odd * shift + cols])


def project(spot, rows, student_weights, teacher_qkv, first, name):
    count = len(rows)
    tok, width = rows[0].shape
    cols = teacher_qkv.shape[2]
    wide = cols // HEAD_DIM * LANES
    mats = 3 - first
    window = lambda j: pl.BlockSpec((width, LANES), lambda m, spot, j=j: (m + first, spot[0] + j))
    out = jax.ShapeDtypeStruct((count * tok, mats * wide), bf16)
    return pl.pallas_call(
        functools.partial(project_kernel, sides=count),
        grid_spec=pltpu.PrefetchScalarGridSpec(
            num_scalar_prefetch=1,
            grid=(mats,),
            in_specs=[pl.BlockSpec((tok, width), lambda m, spot: (0, 0))] * count
            + [window(j) for j in range(3)]
            + [pl.BlockSpec((1, width, cols), lambda m, spot: (m + first, 0, 0))],
            out_specs=[pl.BlockSpec((count * tok, wide), lambda m, spot: (0, m))] * 2,
        ),
        out_shape=[out, out],
        compiler_params=params(),
        cost_estimate=pl.CostEstimate(
            flops=2 * count * tok * width * 768 * mats, bytes_accessed=6 << 20, transcendentals=0
        ),
        name=name,
    )(spot, *rows, student_weights, student_weights, student_weights, teacher_qkv)


def teacher_kernel(own_ref, side_ref, utt_col_ref, utt_row_ref, out_ref):
    rows = own_ref.shape[0]
    wide = own_ref.shape[1] // 3
    allowed = utt_col_ref[...] == utt_row_ref[...]
    parts = []
    for h in range(wide // LANES):
        sl = slice(h * LANES, (h + 1) * LANES)
        sk = slice(wide + h * LANES, wide + (h + 1) * LANES)
        sv = slice(2 * wide + h * LANES, 2 * wide + (h + 1) * LANES)
        keys = jnp.concatenate([side_ref[:rows, sl], own_ref[:, sk], side_ref[rows:, sl]], axis=0)
        vals = jnp.concatenate([side_ref[:rows, sk], own_ref[:, sv], side_ref[rows:, sk]], axis=0)
        probs = softmax_rows(dot_nt(own_ref[:, sl], keys) * score_scale, allowed).astype(bf16)
        parts.append(dot(probs, vals).astype(bf16)[:, :HEAD_DIM])
    attn = jnp.concatenate(parts, axis=1)
    out_ref[...] = jnp.concatenate([attn[: rows // 2], attn[rows // 2 :]], axis=1)


def targets_kernel(info_ref, a0, a1, a2, a3, mine_ref, other_ref, frames_ref, out_ref, attn_scr):
    groups = len((a0, a1, a2, a3))
    cols = a0.shape[1] // 2
    part = cols // 2
    even = info_ref[0] == 0
    for k, ref in enumerate((a0, a1, a2, a3)):
        attn_scr[lax.rem(info_ref[1] + k, groups)] = ref[...]
    low, high = [], []
    for g in range(groups):
        block = attn_scr[g]
        rows = jnp.concatenate([block[:, :cols], block[:, cols:]], axis=0)
        low.append(rows[:, :part])
        high.append(rows[:, part:])
    low, high = jnp.concatenate(low, axis=1), jnp.concatenate(high, axis=1)
    depth, width = groups * part, mine_ref.shape[-1]
    mine = mine_ref[...].reshape(depth, width)
    other = other_ref[...].reshape(depth, width)
    lhs_mine = jnp.where(even, low, high)
    lhs_other = jnp.where(even, high, low)
    wide_frames = frames_ref[...].astype(f32)
    mixing = dot(lhs_mine, mine) + dot(lhs_other, other)
    out_ref[...] = layer_norm(0.5 * (wide_frames + layer_norm(wide_frames + mixing))).astype(bf16)


def forward_kernel(
    own_ref, side_ref, pick_ref, utt_ref, attn_ref, prob_ref, query_ref, kv_ref, *, base
):
    step = pl.program_id(0)
    tok = own_ref.shape[0]
    wide = own_ref.shape[1] // 3
    pairs = wide // (2 * LANES)
    slots = pick_ref.shape[2]
    first = base + 2 * step
    tables = [side_ref[:tok, :], own_ref[:, wide:], side_ref[tok:, :]]
    kv_parts, query = [], None
    for j in range(3):
        pick = jnp.concatenate(
            [select_rows(pick_ref[first + c, j : j + 1, :], tok) for c in range(2)], axis=0
        )
        kv_parts.append(dot(pick, tables[j]).astype(bf16))
        if j == 1:
            query = dot(pick, own_ref[:, :wide]).astype(bf16)
    for c in range(2):
        rows = slice(c * slots, (c + 1) * slots)
        kv = jnp.concatenate([part[rows] for part in kv_parts], axis=0)
        kv_ref[c] = kv
        query_ref[c] = query[rows]
        utt = utt_ref[first + c]
        utt_row = jnp.concatenate([utt[j : j + 1, :] for j in range(3)], axis=1)
        utt_col = column_of(utt[1:2, :])
        allowed = jnp.concatenate([utt_col] * 3, axis=1) == utt_row
        allowed = jnp.concatenate([allowed, allowed], axis=0)
        parts = []
        for p in range(pairs):
            sl = slice(2 * p * LANES, 2 * (p + 1) * LANES)
            sv = slice(wide + 2 * p * LANES, wide + 2 * (p + 1) * LANES)
            scores = dot_nt(split_pair(query[rows, sl]), kv[:, sl]) * score_scale
            probs = softmax_rows(scores, allowed)
            prob_ref[c, p] = probs
            parts.append(join_pair(dot(probs.astype(bf16), kv[:, sv]).astype(bf16)))
        attn = narrow_heads(jnp.concatenate(parts, axis=1))
        cols = attn.shape[1]
        attn_ref[0, :, c * cols : (c + 1) * cols] = attn


def backward_kernel(
    info_ref, a0, a1, a2, a3, wout_hbm, frames_ref, goal_ref, pick_ref,
    prob_hbm, query_hbm, kv_hbm, *refs, base, coef, final,
):
    earlier, refs = (refs[:4], refs[4:]) if final else (None, refs)
    if final:
        qk_ref, v_ref, go_ref = refs[:3]
        refs = refs[3:]
    else:
        gq_ref, gk_ref, gv_ref, go_ref = refs[:4]
        refs = refs[4:]
    (
        wout_scr, prob_scr, query_scr, kv_scr, stack_scr, full_scr, sum_scr, goal_scr,
        grad_scr, ng_scr, ag_scr, dq_scr, dkv_scr, sems,
    ) = refs
    members, pairs = prob_scr.shape[:2]
    slots = query_scr.shape[1]
    wide = query_scr.shape[2]
    tok, width = frames_ref.shape
    groups = stack_scr.shape[0]
    cols = a0.shape[2] // 2
    place = info_ref[1]

    copies = [
        pltpu.make_async_copy(src, dst, sems.at[n])
        for n, (src, dst) in enumerate(
            (
                (wout_hbm.at[pl.ds(3 * width, width), :], wout_scr),
                (kv_hbm, kv_scr),
                (prob_hbm, prob_scr),
                (query_hbm, query_scr),
            )
        )
    ]
    for copy in copies:
        copy.start()

    for k, ref in enumerate((a0, a1, a2, a3)):
        stack_scr[lax.rem(place + k, groups)] = ref[...]
    for g in range(groups):
        for m in range(members):
            half = m % 2
            full_scr[m * slots : (m + 1) * slots, g * cols : (g + 1) * cols] = stack_scr[
                g, m // 2, :, half * cols : (half + 1) * cols
            ]
    pick = jnp.concatenate(
        [select_rows(pick_ref[base + m, 1:2, :], tok) for m in range(members)], axis=0
    )
    goal_scr[...] = dot(pick, goal_ref[...])
    sum_scr[...] = dot(pick, frames_ref[...])
    copies[0].wait()
    sum_scr[...] += dot(full_scr[...], wout_scr[...])
    block = 32

    def norm_rows(n, carry):
        here = pl.ds(pl.multiple_of(n * block, block), block)
        summed = sum_scr[here, :]
        centre = summed - jnp.mean(summed, axis=-1, keepdims=True)
        factor = lax.rsqrt(jnp.mean(centre * centre, axis=-1, keepdims=True) + norm_eps)
        normed = centre * factor
        upstream = (normed - goal_scr[here, :]) * coef
        part = upstream - jnp.mean(upstream, axis=-1, keepdims=True)
        part = part - normed * jnp.mean(upstream * normed, axis=-1, keepdims=True)
        grad_scr[here, :] = (part * factor).astype(bf16)
        return carry

    lax.fori_loop(0, members * slots // block, norm_rows, 0, unroll=4)
    for m in range(members):
        rows = slice(m * slots, (m + 1) * slots)
        live = column_of(pick_ref[base + m, 1:2, :]) >= 0
        live = jnp.concatenate([live] * (width // LANES), axis=1)
        grad_scr[rows, :] = jnp.where(live, grad_scr[rows, :], jnp.zeros((), bf16))
    grad = grad_scr[...]
    for g in range(groups):
        @pl.when(place == g)
        def _():
            ng_scr[...] = grad_scr[:, g * cols : (g + 1) * cols]

    own_rows = wout_scr[pl.ds(pl.multiple_of(place * cols, LANES // 2), cols), :]
    ag_scr[...] = widen_heads(dot_nt(grad, own_rows).astype(bf16))
    for copy in copies[1:]:
        copy.wait()
    for m in range(members):
        rows = slice(m * slots, (m + 1) * slots)
        for p in range(pairs):
            sl = slice(2 * p * LANES, 2 * (p + 1) * LANES)
            sv = slice(wide + 2 * p * LANES, wide + 2 * (p + 1) * LANES)
            probs = prob_scr[m, p]
            grads = split_pair(ag_scr[rows, sl])
            prob_grad = dot_nt(grads, kv_scr[m, :, sv])
            inner = jnp.sum(probs * prob_grad, axis=-1, keepdims=True)
            score_grad = (probs * (prob_grad - inner) * score_scale).astype(bf16)
            dq_scr[rows, sl] = join_pair(dot(score_grad, kv_scr[m, :, sl]).astype(bf16))
            dk = dot_tn(score_grad, split_pair(query_scr[m, :, sl])).astype(bf16)
            dv = dot_tn(probs.astype(bf16), grads).astype(bf16)
            for j in range(3):
                dkv_scr[j, rows, sl] = dk[j * slots : (j + 1) * slots]
                dkv_scr[j, rows, sv] = dv[j * slots : (j + 1) * slots]

    keys, values, query = [], [], None
    for j in range(3):
        row = jnp.concatenate([pick_ref[base + m, j : j + 1, :] for m in range(members)], axis=1)
        pick_t = select_rows_t(row, tok)
        total = dot(pick_t, dkv_scr[j])
        keys.append(narrow_heads(total[:, :wide]))
        values.append(narrow_heads(total[:, wide:]))
        if j == 1:
            query = narrow_heads(dot(pick_t, dq_scr[...]))
    keys, values = jnp.concatenate(keys, axis=0), jnp.concatenate(values, axis=0)
    out = dot_tn(full_scr[...], ng_scr[...])
    if not final:
        gq_ref[...], gk_ref[...], gv_ref[...], go_ref[...] = query, keys, values, out
        return
    query = query + earlier[0][...]
    keys = keys + earlier[1][...]
    values = values + earlier[2][...]
    go_ref[...] = out + earlier[3][...]
    gap = jnp.zeros((tok, cols), f32)
    both = jnp.concatenate([jnp.concatenate([gap, query, gap], axis=0), keys], axis=1)
    for ref, full in ((qk_ref, both), (v_ref, values)):
        wide_cols = full.shape[1]
        top = full.astype(bf16)
        ref[:, :wide_cols] = top
        ref[:, wide_cols:] = (full - top.astype(f32)).astype(bf16)


def weights_kernel(half_ref, left_ref, own_ref, right_ref, qk_in, v_in, go_ref, qk_ref, vo_ref):
    cols = go_ref.shape[1]
    lhs = jnp.concatenate([left_ref[...], own_ref[...], right_ref[...]], axis=0)
    both = dot_tn(lhs, qk_in[...])
    qk_ref[...] = both[:, : 2 * cols] + both[:, 2 * cols :]
    value = dot_tn(lhs, v_in[...])
    vo_ref[:, :cols] = value[:, :cols] + value[:, cols:]
    vo_ref[:, cols:] = go_ref[...]


def weight_grads(half, left, own, right, qk, v, go, name):
    tok, width = own.shape
    cols = go.shape[1]
    part = width // CORES
    whole = lambda a: pl.BlockSpec(a.shape, lambda k, half: (0, 0))
    return pl.pallas_call(
        weights_kernel,
        grid_spec=pltpu.PrefetchScalarGridSpec(
            num_scalar_prefetch=1,
            grid=(1,),
            in_specs=[pl.BlockSpec((tok, part), lambda k, half: (0, half[0]))] * 3
            + [whole(qk), whole(v), pl.BlockSpec((part, cols), lambda k, half: (half[0], 0))],
            out_specs=[pl.BlockSpec((part, 2 * cols), lambda k, half: (0, 0))] * 2,
        ),
        out_shape=[jax.ShapeDtypeStruct((part, 2 * cols), f32)] * 2,
        compiler_params=params(),
        cost_estimate=pl.CostEstimate(
            flops=2 * 6 * tok * part * 3 * cols, bytes_accessed=8 << 20, transcendentals=0
        ),
        name=name,
    )(half, left, own, right, qk, v, go)


def pieces_kernel(spot_ref, *refs, terms, count):
    ins, outs, scr = refs[:terms], refs[terms : terms + count], refs[terms + count]
    total = ins[0][...]
    for ref in ins[1:]:
        total = total + ref[...]
    scr[...] = total
    rows = outs[0].shape[0]
    for k in range(count):
        at = pl.multiple_of(lax.rem(spot_ref[0] + k, count) * rows, 8)
        outs[k][...] = scr[pl.ds(at, rows), :]


def sum_pieces(parts, spot, count, name):
    rows, width = parts[0].shape
    return pl.pallas_call(
        functools.partial(pieces_kernel, terms=len(parts), count=count),
        in_specs=[SMEM] + [VMEM] * len(parts),
        out_specs=[VMEM] * count,
        out_shape=[jax.ShapeDtypeStruct((rows // count, width), f32)] * count,
        scratch_shapes=[pltpu.VMEM((rows, width), f32)],
        compiler_params=params(),
        name=name,
    )(spot.reshape(1), *parts)


def ring_send(pieces, pairs_of):
    order = [k for k in (2, 1, 3) if k < len(pieces)]
    return [pieces[0]] + [lax.ppermute(pieces[k], "seq", pairs_of(k)) for k in order]


def mats_kernel(spot_ref, *refs):
    qk, vo, outs, scr = refs[:4], refs[4:8], refs[8:12], refs[12]
    cols = outs[0].shape[1]
    for n, parts in enumerate((qk, vo)):
        total = parts[0][...]
        for ref in parts[1:]:
            total = total + ref[...]
        scr[2 * n] = total[:, :cols]
        scr[2 * n + 1] = total[:, cols:]
    for k in range(len(outs)):
        outs[k][...] = scr[lax.rem(spot_ref[0] + k, len(outs))]


def order_kernel(spot_ref, *refs):
    ins, out_ref, scr = refs[:4], refs[4], refs[5]
    cols = ins[0].shape[1]
    for k, ref in enumerate(ins):
        scr[k] = ref[...]
    for g in range(len(ins)):
        turn = lax.rem(spot_ref[0] - g + len(ins), len(ins))
        out_ref[:, g * cols : (g + 1) * cols] = scr[turn]


def utterance_of(positions, utt_ends):
    return jnp.sum((utt_ends <= positions[..., None]).astype(jnp.int32), axis=-1)


def per_device(
    frames, utt_lengths, vis_frames, vis_count, teacher_qkv, teacher_out, student_weights
):
    tok, width = frames.shape
    seq, seq_count = lax.axis_index("seq"), lax.axis_size("seq")
    place, groups = lax.axis_index("copy"), lax.axis_size("copy")
    cols = teacher_out.shape[0]
    heads = cols // HEAD_DIM
    wide = heads * LANES
    first_frame = seq * tok
    here = vis_frames.shape[0]
    copies = here * groups
    slots = vis_frames.shape[2]
    members = copies // CHUNKS
    core = lax.rem(seq, CORES)
    swap = [(n, n ^ 1) for n in range(seq_count)]

    up = [(n, n + 1) for n in range(seq_count - 1)]
    left = lax.ppermute(frames, "seq", up)
    right = lax.ppermute(frames, "seq", [(j, n) for n, j in up])

    def from_group(value):
        spread = lambda k: [(n, (n - k) % groups) for n in range(groups)]
        return [value] + [lax.ppermute(value, "copy", spread(k)) for k in (2, 1, 3)]

    def by_turn(parts):
        return [parts[0], parts[2], parts[1], parts[3]]

    utt_ends = jnp.cumsum(utt_lengths)
    near = seq - 1 + jnp.arange(3, dtype=jnp.int32)
    inside = (near >= 0) & (near < seq_count)
    near_ids = jnp.clip(near, 0, seq_count - 1)
    near_lists = jnp.take(vis_frames, near_ids, axis=1)
    near_counts = jnp.where(inside, jnp.take(vis_count, near_ids, axis=1), 0)
    near_live = jnp.arange(slots, dtype=jnp.int32) < near_counts[..., None]
    slot_utt = utterance_of((near * tok)[None, :, None] + near_lists, utt_ends)
    marks = jnp.stack([jnp.where(near_live, near_lists, -1), jnp.where(near_live, slot_utt, -1)], 1)
    marks = jnp.stack(by_turn(from_group(marks)))
    marks = jnp.take(marks, lax.rem(jnp.arange(groups) - place + groups, groups), axis=0)
    marks = marks.reshape(copies, 2, 3, slots)
    picks, utts = marks[:, 0], marks[:, 1]

    half_rows = cols // CORES
    out_mine = lax.all_gather(
        lax.dynamic_slice_in_dim(teacher_out, core * half_rows, half_rows, 0), "copy", axis=0
    )
    out_other = lax.ppermute(out_mine, "seq", swap)

    reach_pos = first_frame - tok + jnp.arange(3 * tok, dtype=jnp.int32)
    reach_in = (reach_pos >= 0) & (reach_pos < seq_count * tok)
    reach_utt = jnp.where(reach_in, utterance_of(reach_pos, utt_ends), -1)

    spot = jnp.stack([place * cols // LANES, lax.rem(place, 2)])
    own_student, own_teacher = project(spot, [frames], student_weights, teacher_qkv, 0, "project_own")
    side_student, side_teacher = project(
        spot, [left, right], student_weights, teacher_qkv, 1, "project_side"
    )

    teacher_attn = pl.pallas_call(
        teacher_kernel,
        in_specs=[VMEM] * 4,
        out_specs=VMEM,
        out_shape=jax.ShapeDtypeStruct((tok // 2, 2 * cols), bf16),
        compiler_params=params(),
        cost_estimate=pl.CostEstimate(
            flops=4 * heads * tok * 3 * tok * LANES,
            bytes_accessed=2 << 20,
            transcendentals=heads * tok * 3 * tok,
        ),
        name="teacher_attn",
    )(own_teacher, side_teacher, reach_utt[tok : 2 * tok].reshape(tok, 1), reach_utt.reshape(1, 3 * tok))
    teacher_all = by_turn(from_group(teacher_attn))

    saved, gathered = [], []
    whole = lambda a: pl.BlockSpec(a.shape, lambda c, n=a.ndim: (0,) * n)
    two = lambda shape: pl.BlockSpec((2,) + shape, lambda c, n=len(shape): (c,) + (0,) * n)
    prob_shape = (heads // 2, 2 * slots, 3 * slots)
    for chunk in range(CHUNKS):
        attn, probs, query, kv = pl.pallas_call(
            functools.partial(forward_kernel, base=chunk * members),
            grid=(members // 2,),
            in_specs=[whole(own_student), whole(side_student), whole(picks), whole(utts)],
            out_specs=[
                pl.BlockSpec((1, slots, 2 * cols), lambda c: (c, 0, 0)),
                two(prob_shape),
                two((slots, wide)),
                two((3 * slots, 2 * wide)),
            ],
            out_shape=[
                jax.ShapeDtypeStruct((members // 2, slots, 2 * cols), bf16),
                jax.ShapeDtypeStruct((members,) + prob_shape, f32),
                jax.ShapeDtypeStruct((members, slots, wide), bf16),
                jax.ShapeDtypeStruct((members, 3 * slots, 2 * wide), bf16),
            ],
            compiler_params=params(),
            cost_estimate=pl.CostEstimate(
                flops=members * (4 * heads * slots * 3 * slots * LANES + 2 * slots * tok * 7 * wide),
                bytes_accessed=8 << 20,
                transcendentals=members * heads * slots * 3 * slots,
            ),
            name=f"student_forward{chunk}",
        )(own_student, side_student, picks, utts)
        gathered.append(by_turn(from_group(attn)))
        saved.append((probs, query, kv))

    info = jnp.stack([core, place])
    targets = pl.pallas_call(
        targets_kernel,
        in_specs=[SMEM] + [VMEM] * 7,
        out_specs=VMEM,
        out_shape=jax.ShapeDtypeStruct((tok, width), bf16),
        scratch_shapes=[pltpu.VMEM((groups, tok // 2, 2 * cols), bf16)],
        compiler_params=params(),
        cost_estimate=pl.CostEstimate(
            flops=2 * tok * width * width, bytes_accessed=5 << 20, transcendentals=0
        ),
        name="teacher_targets",
    )(info, *teacher_all, out_mine, out_other, frames)

    coef = 2.0 / (width**0.5 * copies)
    rows = members * slots
    carried = ()
    for chunk in range(CHUNKS):
        final = chunk == CHUNKS - 1
        probs, query, kv = saved[chunk]
        side_f32 = lambda n: jax.ShapeDtypeStruct((n * tok, cols), f32)
        out_o = jax.ShapeDtypeStruct((width, cols), f32)
        if final:
            outs = [
                jax.ShapeDtypeStruct((3 * tok, 4 * cols), bf16),
                jax.ShapeDtypeStruct((3 * tok, 2 * cols), bf16),
                out_o,
            ]
        else:
            outs = [side_f32(1), side_f32(3), side_f32(3), out_o]
        carried = pl.pallas_call(
            functools.partial(backward_kernel, base=chunk * members, coef=coef, final=final),
            in_specs=[SMEM] + [VMEM] * 4 + [HBM] + [VMEM] * 3 + [HBM] * 3 + [VMEM] * len(carried),
            out_specs=[VMEM] * len(outs),
            out_shape=outs,
            scratch_shapes=[
                pltpu.VMEM((width, width), bf16),
                pltpu.VMEM(probs.shape, f32),
                pltpu.VMEM(query.shape, bf16),
                pltpu.VMEM(kv.shape, bf16),
                pltpu.VMEM((groups, members // 2, slots, 2 * cols), bf16),
                pltpu.VMEM((rows, width), bf16),
                pltpu.VMEM((rows, width), f32),
                pltpu.VMEM((rows, width), f32),
                pltpu.VMEM((rows, width), bf16),
                pltpu.VMEM((rows, cols), bf16),
                pltpu.VMEM((rows, wide), bf16),
                pltpu.VMEM((rows, wide), bf16),
                pltpu.VMEM((3, rows, 2 * wide), bf16),
                pltpu.SemaphoreType.DMA((4,)),
            ],
            compiler_params=params(),
            cost_estimate=pl.CostEstimate(
                flops=members * slots * width * width * 6, bytes_accessed=16 << 20, transcendentals=0
            ),
            name=f"student_backward{chunk}",
        )(
            info, *gathered[chunk], student_weights, frames, targets, picks,
            probs, query, kv, *carried,
        )

    away = weight_grads((1 - core).reshape(1), left, frames, right, *carried, "weights_away")
    arrived = [lax.ppermute(a, "seq", swap) for a in away]
    kept = weight_grads(core.reshape(1), left, frames, right, *carried, "weights_kept")

    ring = RING
    far = seq_count // CORES // ring
    z_place = lax.rem(seq // CORES, ring)
    y_place = seq // (CORES * ring)

    def z_pairs(k):
        span = CORES * ring
        return [
            (n, n // span * span + ((n // CORES + k) % ring) * CORES + n % CORES)
            for n in range(seq_count)
        ]

    def y_pairs(k):
        return [(n, (n + k * CORES * ring) % seq_count) for n in range(seq_count)]

    qk = ring_send(sum_pieces([kept[0], arrived[0]], z_place, ring, "pieces_qk"), z_pairs)
    vo = ring_send(sum_pieces([kept[1], arrived[1]], y_place, far, "pieces_vo"), y_pairs)
    qk = ring_send(sum_pieces(qk, y_place, far, "pieces_qk2"), y_pairs)
    vo = ring_send(sum_pieces(vo, z_place, ring, "pieces_vo2"), z_pairs)

    out_rows = width // seq_count
    mats = groups
    parts = pl.pallas_call(
        mats_kernel,
        in_specs=[SMEM] + [VMEM] * 8,
        out_specs=[VMEM] * mats,
        out_shape=[jax.ShapeDtypeStruct((out_rows, cols), f32)] * mats,
        scratch_shapes=[pltpu.VMEM((mats, out_rows, cols), f32)],
        compiler_params=params(),
        name="matrix_rows",
    )(place.reshape(1), *qk, *vo)

    def row_block(s, mat):
        c, z, y = s % CORES, s // CORES % ring, s // (CORES * ring)
        return (c * ring + z) * far + y if mat < 2 else (c * far + y) * ring + z

    received = []
    for turn in range(mats):
        pairs = [
            (s * groups + g, (g + turn) % mats * seq_count + row_block(s, (g + turn) % mats))
            for s in range(seq_count)
            for g in range(groups)
        ]
        received.append(lax.ppermute(parts[turn], ("seq", "copy"), pairs))
    own_mat = (seq * groups + place) // seq_count
    return pl.pallas_call(
        order_kernel,
        in_specs=[SMEM] + [VMEM] * groups,
        out_specs=VMEM,
        out_shape=jax.ShapeDtypeStruct((out_rows, groups * cols), f32),
        scratch_shapes=[pltpu.VMEM((groups, out_rows, cols), f32)],
        compiler_params=params(),
        name="order_columns",
    )(own_mat.reshape(1), *received)


def solution(mesh):
    placed = (
        P("seq", None),
        P(),
        P("copy", None, None),
        P("copy", None),
        P(None, None, "copy"),
        P("copy", None),
        P(),
    )
    return jax.shard_map(
        per_device, mesh=mesh, in_specs=placed, out_specs=P(("seq", "copy"), None), check_vma=False
    )
```

```python
import functools

import jax
import jax.numpy as jnp
from jax import lax
from jax.experimental import pallas as pl
from jax.experimental.pallas import tpu as pltpu
from jax.sharding import PartitionSpec as P

HEADS = 16
HEAD_DIM = 80
LANES = 128
CHUNKS = 2
CORES = 2
RING = 4

norm_eps = 1e-05
mask_fill = -1e30
score_scale = HEAD_DIM ** (-0.5)
bf16 = jnp.bfloat16
f32 = jnp.float32
VMEM = pl.BlockSpec(memory_space=pltpu.VMEM)
SMEM = pl.BlockSpec(memory_space=pltpu.SMEM)
HBM = pl.BlockSpec(memory_space=pl.ANY)


def dot(a, b):
    return lax.dot_general(a, b, (((1,), (0,)), ((), ())), preferred_element_type=f32)


def dot_nt(a, b):
    return lax.dot_general(a, b, (((1,), (1,)), ((), ())), preferred_element_type=f32)


def dot_tn(a, b):
    return lax.dot_general(a, b, (((0,), (0,)), ((), ())), preferred_element_type=f32)


def widen_heads(x):
    rows, cols = x.shape
    gap = jnp.zeros((rows, LANES - HEAD_DIM), x.dtype)
    parts = []
    for h in range(cols // HEAD_DIM):
        parts += [x[:, h * HEAD_DIM : (h + 1) * HEAD_DIM], gap]
    return jnp.concatenate(parts, axis=1)


def narrow_heads(x):
    return jnp.concatenate(
        [x[:, h * LANES : h * LANES + HEAD_DIM] for h in range(x.shape[1] // LANES)], axis=1
    )


def softmax_rows(scores, allowed):
    masked = jnp.where(allowed, scores, mask_fill)
    expo = jnp.exp(masked - jnp.max(masked, axis=-1, keepdims=True))
    return expo * (1.0 / jnp.sum(expo, axis=-1, keepdims=True))


def layer_norm(values):
    centre = values - jnp.mean(values, axis=-1, keepdims=True)
    spread = jnp.mean(centre * centre, axis=-1, keepdims=True)
    return centre * lax.rsqrt(spread + norm_eps)


def params(mib):
    return pltpu.CompilerParams(vmem_limit_bytes=mib << 20)


def column_of(row):
    count = row.shape[1]
    return jnp.transpose(jnp.broadcast_to(row, (count, count)))


def select_rows(row, count):
    slots = row.shape[1]
    column = column_of(row)
    column = jnp.concatenate([column] * (count // slots), axis=1)
    return (lax.broadcasted_iota(jnp.int32, (slots, count), 1) == column).astype(bf16)


def select_rows_t(row, count):
    slots = row.shape[1]
    return (lax.broadcasted_iota(jnp.int32, (count, slots), 0) == row).astype(bf16)


def split_pair(x):
    gap = jnp.zeros((x.shape[0], LANES), x.dtype)
    top = jnp.concatenate([x[:, :LANES], gap], axis=1)
    low = jnp.concatenate([gap, x[:, LANES:]], axis=1)
    return jnp.concatenate([top, low], axis=0)


def join_pair(x):
    rows = x.shape[0] // 2
    return jnp.concatenate([x[:rows, :LANES], x[rows:, LANES:]], axis=1)


def project_kernel(spot_ref, *refs, sides):
    rows_refs, (w0, w1, w2, wt, student_ref, teacher_ref) = refs[:sides], refs[sides:]
    cols = wt.shape[1]
    rows = jnp.concatenate([r[...] for r in rows_refs], axis=0)
    weights = jnp.concatenate([w0[...], w1[...], w2[...]], axis=1)
    student = dot(rows, weights).astype(bf16)
    teacher_ref[...] = widen_heads(dot_nt(rows, wt[0]).astype(bf16))
    shift = LANES // 2
    for odd in range(2):
        @pl.when(spot_ref[1] == odd)
        def _():
            student_ref[...] = widen_heads(student[:, odd * shift : odd * shift + cols])


def project(spot, rows, student_weights, teacher_qkv, first, name):
    count = len(rows)
    tok, width = rows[0].shape
    cols = teacher_qkv.shape[1]
    wide = cols // HEAD_DIM * LANES
    mats = 3 - first
    window = lambda j: pl.BlockSpec((width, LANES), lambda m, spot, j=j: (m + first, spot[0] + j))
    out = jax.ShapeDtypeStruct((count * tok, mats * wide), bf16)
    return pl.pallas_call(
        functools.partial(project_kernel, sides=count),
        grid_spec=pltpu.PrefetchScalarGridSpec(
            num_scalar_prefetch=1,
            grid=(mats,),
            in_specs=[pl.BlockSpec((tok, width), lambda m, spot: (0, 0))] * count
            + [window(j) for j in range(3)]
            + [pl.BlockSpec((1, cols, width), lambda m, spot: (m + first, 0, 0))],
            out_specs=[pl.BlockSpec((count * tok, wide), lambda m, spot: (0, m))] * 2,
        ),
        out_shape=[out, out],
        compiler_params=params(20),
        cost_estimate=pl.CostEstimate(
            flops=2 * count * tok * width * 768 * mats, bytes_accessed=6 << 20, transcendentals=0
        ),
        name=name,
    )(spot, *rows, student_weights, student_weights, student_weights, teacher_qkv)


def teacher_heads(own_ref, side_ref, utt_col_ref, utt_row_ref):
    rows = own_ref.shape[0]
    wide = own_ref.shape[1] // 3
    allowed = utt_col_ref[...] == utt_row_ref[...]
    parts = []
    for h in range(wide // LANES):
        sl = slice(h * LANES, (h + 1) * LANES)
        sk = slice(wide + h * LANES, wide + (h + 1) * LANES)
        sv = slice(2 * wide + h * LANES, 2 * wide + (h + 1) * LANES)
        keys = jnp.concatenate([side_ref[:rows, sl], own_ref[:, sk], side_ref[rows:, sl]], axis=0)
        vals = jnp.concatenate([side_ref[:rows, sk], own_ref[:, sv], side_ref[rows:, sk]], axis=0)
        probs = softmax_rows(dot_nt(own_ref[:, sl], keys) * score_scale, allowed).astype(bf16)
        parts.append(dot(probs, vals).astype(bf16)[:, :HEAD_DIM])
    attn = jnp.concatenate(parts, axis=1)
    return jnp.concatenate([attn[: rows // 2], attn[rows // 2 :]], axis=1)


def targets_kernel(info_ref, a0, a1, a2, a3, mine_ref, other_ref, frames_ref, out_ref, attn_scr):
    groups = len((a0, a1, a2, a3))
    cols = a0.shape[2] // 2
    part = cols // 2
    even = info_ref[0] == 0
    for k, ref in enumerate((a0, a1, a2, a3)):
        attn_scr[lax.rem(info_ref[1] + k, groups)] = ref[0]
    low, high = [], []
    for g in range(groups):
        block = attn_scr[g]
        rows = jnp.concatenate([block[:, :cols], block[:, cols:]], axis=0)
        low.append(rows[:, :part])
        high.append(rows[:, part:])
    low, high = jnp.concatenate(low, axis=1), jnp.concatenate(high, axis=1)
    depth, width = groups * part, mine_ref.shape[-1]
    mine = mine_ref[...].reshape(depth, width)
    other = other_ref[...].reshape(depth, width)
    lhs_mine = jnp.where(even, low, high)
    lhs_other = jnp.where(even, high, low)
    wide_frames = frames_ref[...].astype(f32)
    mixing = dot(lhs_mine, mine) + dot(lhs_other, other)
    out_ref[...] = layer_norm(0.5 * (wide_frames + layer_norm(wide_frames + mixing))).astype(bf16)


def forward_first_kernel(
    own_ref, side_ref, pick_ref, utt_ref, town_ref, tside_ref, utt_col_ref, utt_row_ref,
    attn_ref, prob_ref, query_ref, kv_ref,
):
    step = pl.program_id(0)

    @pl.when(step == 0)
    def _():
        attn_ref[0] = teacher_heads(town_ref, tside_ref, utt_col_ref, utt_row_ref)

    @pl.when(step > 0)
    def _():
        forward_pair(
            own_ref, side_ref, pick_ref, utt_ref, attn_ref, prob_ref, query_ref, kv_ref, 2 * step - 2
        )


def forward_next_kernel(
    own_ref, side_ref, pick_ref, utt_ref, left_ref, frames_ref, right_ref,
    attn_ref, prob_ref, query_ref, kv_ref, turned_ref, *, base,
):
    step = pl.program_id(0)

    @pl.when(step == 0)
    def _():
        tok = frames_ref.shape[0]
        for j, ref in enumerate((left_ref, frames_ref, right_ref)):
            turned_ref[:, j * tok : (j + 1) * tok] = jnp.transpose(ref[...])

    forward_pair(
        own_ref, side_ref, pick_ref, utt_ref, attn_ref, prob_ref, query_ref, kv_ref, base + 2 * step
    )


def forward_pair(
    own_ref, side_ref, pick_ref, utt_ref, attn_ref, prob_ref, query_ref, kv_ref, first
):
    tok = own_ref.shape[0]
    wide = own_ref.shape[1] // 3
    pairs = wide // (2 * LANES)
    slots = pick_ref.shape[2]
    tables = [side_ref[:tok, :], own_ref[:, wide:], side_ref[tok:, :]]
    kv_parts, query = [], None
    for j in range(3):
        pick = jnp.concatenate(
            [select_rows(pick_ref[first + c, j : j + 1, :], tok) for c in range(2)], axis=0
        )
        kv_parts.append(dot(pick, tables[j]).astype(bf16))
        if j == 1:
            query = dot(pick, own_ref[:, :wide]).astype(bf16)
    for c in range(2):
        rows = slice(c * slots, (c + 1) * slots)
        kv = jnp.concatenate([part[rows] for part in kv_parts], axis=0)
        kv_ref[c] = kv
        query_ref[c] = query[rows]
        utt = utt_ref[first + c]
        utt_row = jnp.concatenate([utt[j : j + 1, :] for j in range(3)], axis=1)
        utt_col = column_of(utt[1:2, :])
        allowed = jnp.concatenate([utt_col] * 3, axis=1) == utt_row
        allowed = jnp.concatenate([allowed, allowed], axis=0)
        parts = []
        for p in range(pairs):
            sl = slice(2 * p * LANES, 2 * (p + 1) * LANES)
            sv = slice(wide + 2 * p * LANES, wide + 2 * (p + 1) * LANES)
            scores = dot_nt(split_pair(query[rows, sl]), kv[:, sl]) * score_scale
            probs = softmax_rows(scores, allowed)
            prob_ref[c, p] = probs
            parts.append(join_pair(dot(probs.astype(bf16), kv[:, sv]).astype(bf16)))
        attn = narrow_heads(jnp.concatenate(parts, axis=1))
        cols = attn.shape[1]
        attn_ref[0, :, c * cols : (c + 1) * cols] = attn


def backward_kernel(
    info_ref, a0, a1, a2, a3, wout_hbm, frames_ref, goal_ref, pick_ref,
    prob_hbm, query_hbm, kv_hbm, *refs, base, coef, final, skip,
):
    earlier, refs = (refs[:4], refs[4:]) if final else (None, refs)
    if final:
        qk_ref, v_ref, go_ref = refs[:3]
        refs = refs[3:]
    else:
        gq_ref, gk_ref, gv_ref, go_ref = refs[:4]
        refs = refs[4:]
    (
        wout_scr, prob_scr, query_scr, kv_scr, stack_scr, full_scr, sum_scr, goal_scr,
        grad_scr, ng_scr, ag_scr, dq_scr, dkv_scr, sems,
    ) = refs
    members, pairs = prob_scr.shape[:2]
    slots = query_scr.shape[1]
    wide = query_scr.shape[2]
    tok, width = frames_ref.shape
    groups = stack_scr.shape[0]
    cols = a0.shape[2] // 2
    place = info_ref[1]

    copies = [
        pltpu.make_async_copy(src, dst, sems.at[n])
        for n, (src, dst) in enumerate(
            (
                (wout_hbm.at[pl.ds(3 * width, width), :], wout_scr),
                (kv_hbm, kv_scr),
                (prob_hbm, prob_scr),
                (query_hbm, query_scr),
            )
        )
    ]
    for copy in copies:
        copy.start()

    for k, ref in enumerate((a0, a1, a2, a3)):
        stack_scr[lax.rem(place + k, groups)] = ref[skip:]
    for g in range(groups):
        for m in range(members):
            half = m % 2
            full_scr[m * slots : (m + 1) * slots, g * cols : (g + 1) * cols] = stack_scr[
                g, m // 2, :, half * cols : (half + 1) * cols
            ]
    pick = jnp.concatenate(
        [select_rows(pick_ref[base + m, 1:2, :], tok) for m in range(members)], axis=0
    )
    goal_scr[...] = dot(pick, goal_ref[...])
    sum_scr[...] = dot(pick, frames_ref[...])
    copies[0].wait()
    sum_scr[...] += dot(full_scr[...], wout_scr[...])
    block = 32

    def norm_rows(n, carry):
        here = pl.ds(pl.multiple_of(n * block, block), block)
        summed = sum_scr[here, :]
        centre = summed - jnp.mean(summed, axis=-1, keepdims=True)
        factor = lax.rsqrt(jnp.mean(centre * centre, axis=-1, keepdims=True) + norm_eps)
        normed = centre * factor
        upstream = (normed - goal_scr[here, :]) * coef
        part = upstream - jnp.mean(upstream, axis=-1, keepdims=True)
        part = part - normed * jnp.mean(upstream * normed, axis=-1, keepdims=True)
        grad_scr[here, :] = (part * factor).astype(bf16)
        return carry

    lax.fori_loop(0, members * slots // block, norm_rows, 0, unroll=4)
    for m in range(members):
        rows = slice(m * slots, (m + 1) * slots)
        live = column_of(pick_ref[base + m, 1:2, :]) >= 0
        live = jnp.concatenate([live] * (width // LANES), axis=1)
        grad_scr[rows, :] = jnp.where(live, grad_scr[rows, :], jnp.zeros((), bf16))
    grad = grad_scr[...]
    for g in range(groups):
        @pl.when(place == g)
        def _():
            ng_scr[...] = grad_scr[:, g * cols : (g + 1) * cols]

    own_rows = wout_scr[pl.ds(pl.multiple_of(place * cols, LANES // 2), cols), :]
    ag_scr[...] = widen_heads(dot_nt(grad, own_rows).astype(bf16))
    for copy in copies[1:]:
        copy.wait()
    for m in range(members):
        rows = slice(m * slots, (m + 1) * slots)
        for p in range(pairs):
            sl = slice(2 * p * LANES, 2 * (p + 1) * LANES)
            sv = slice(wide + 2 * p * LANES, wide + 2 * (p + 1) * LANES)
            probs = prob_scr[m, p]
            grads = split_pair(ag_scr[rows, sl])
            prob_grad = dot_nt(grads, kv_scr[m, :, sv])
            inner = jnp.sum(probs * prob_grad, axis=-1, keepdims=True)
            score_grad = (probs * (prob_grad - inner) * score_scale).astype(bf16)
            dq_scr[rows, sl] = join_pair(dot(score_grad, kv_scr[m, :, sl]).astype(bf16))
            dk = dot_tn(score_grad, split_pair(query_scr[m, :, sl])).astype(bf16)
            dv = dot_tn(probs.astype(bf16), grads).astype(bf16)
            for j in range(3):
                dkv_scr[j, rows, sl] = dk[j * slots : (j + 1) * slots]
                dkv_scr[j, rows, sv] = dv[j * slots : (j + 1) * slots]

    keys, values, query = [], [], None
    for j in range(3):
        row = jnp.concatenate([pick_ref[base + m, j : j + 1, :] for m in range(members)], axis=1)
        pick_t = select_rows_t(row, tok)
        total = dot(pick_t, dkv_scr[j])
        keys.append(narrow_heads(total[:, :wide]))
        values.append(narrow_heads(total[:, wide:]))
        if j == 1:
            query = narrow_heads(dot(pick_t, dq_scr[...]))
    keys, values = jnp.concatenate(keys, axis=0), jnp.concatenate(values, axis=0)
    out = dot_tn(full_scr[...], ng_scr[...])
    if not final:
        gq_ref[...], gk_ref[...], gv_ref[...], go_ref[...] = query, keys, values, out
        return
    query = query + earlier[0][...]
    keys = keys + earlier[1][...]
    values = values + earlier[2][...]
    go_ref[...] = out + earlier[3][...]
    gap = jnp.zeros((tok, cols), f32)
    both = jnp.concatenate([jnp.concatenate([gap, query, gap], axis=0), keys], axis=1)
    for ref, full in ((qk_ref, both), (v_ref, values)):
        wide_cols = full.shape[1]
        top = full.astype(bf16)
        ref[:, :wide_cols] = top
        ref[:, wide_cols:] = (full - top.astype(f32)).astype(bf16)


def weights_kernel(half_ref, turned_ref, qk_in, v_in, go_ref, out_ref):
    count, _, rows, reach = turned_ref.shape
    cols = go_ref.shape[3]
    part = rows // 2
    lhs = turned_ref[...].reshape(count * rows, reach)
    both = dot(lhs, qk_in[...])
    both = both[:, : 2 * cols] + both[:, 2 * cols :]
    value = dot(lhs, v_in[...])
    value = value[:, :cols] + value[:, cols:]
    for z in range(count):
        top = slice(z * rows, z * rows + part)
        low = slice(z * rows + part, (z + 1) * rows)
        out_ref[z * part : (z + 1) * part, : 2 * cols] = both[top]
        out_ref[z * part : (z + 1) * part, 2 * cols : 3 * cols] = value[top]
        out_ref[z * part : (z + 1) * part, 3 * cols :] = go_ref[z, 0, :part, :]
        here = slice(z * cols, (z + 1) * cols)
        for m, full in enumerate((both[low, :cols], both[low, cols:], value[low], go_ref[z, 0, part:, :])):
            at = (count + m) * part
            out_ref[at : at + part, here] = full


def weight_grads(half, turned, qk, v, go, name):
    width, reach = turned.shape
    cols = go.shape[1]
    rows = width // RING // CORES
    whole = lambda a: pl.BlockSpec(a.shape, lambda k, half: (0, 0))
    mine = lambda n: pl.BlockSpec((RING, 1, rows, n), lambda k, half: (0, half[0], 0, 0))
    return pl.pallas_call(
        weights_kernel,
        grid_spec=pltpu.PrefetchScalarGridSpec(
            num_scalar_prefetch=1,
            grid=(1,),
            in_specs=[mine(reach), whole(qk), whole(v), mine(cols)],
            out_specs=pl.BlockSpec((RING * rows, 4 * cols), lambda k, half: (0, 0)),
        ),
        out_shape=jax.ShapeDtypeStruct((RING * rows, 4 * cols), f32),
        compiler_params=params(28),
        cost_estimate=pl.CostEstimate(
            flops=2 * width * reach * 3 * cols, bytes_accessed=8 << 20, transcendentals=0
        ),
        name=name,
    )(
        half,
        turned.reshape(RING, CORES, rows, reach),
        qk,
        v,
        go.reshape(RING, CORES, rows, cols),
    )


def first_pieces_kernel(spot_ref, kept_ref, arrived_ref, *refs):
    outs, scr = refs[:-1], refs[-1]
    scr[...] = kept_ref[...] + arrived_ref[...]
    rows = outs[0].shape[0]
    count = len(outs) // 2
    for n in range(2):
        for k in range(count):
            at = n * count + lax.rem(spot_ref[n] + k, count)
            outs[n * count + k][...] = scr[pl.ds(pl.multiple_of(at * rows, 8), rows), :]


def second_pieces_kernel(spot_ref, *refs):
    count = 4
    ins, outs, scr = refs[: 2 * count], refs[2 * count : 4 * count], refs[4 * count]
    rows, wide = outs[0].shape
    cols = wide // 2
    for n in range(2):
        total = ins[n * count][...]
        for k in range(1, count):
            total = total + ins[n * count + k][...]
        for m in range(count):
            for x in range(2):
                scr[m, :, x * cols : (x + 1) * cols] = total[
                    x * rows : (x + 1) * rows, m * cols : (m + 1) * cols
                ]
        for k in range(count):
            outs[n * count + k][...] = scr[lax.rem(spot_ref[1 - n] + k, count)]


def third_pieces_kernel(spot_ref, *refs):
    count = 4
    ins, outs, scr = refs[: 2 * count], refs[2 * count : 3 * count], refs[3 * count]
    cols = outs[0].shape[1]
    for n in range(2):
        total = ins[n * count][...]
        for k in range(1, count):
            total = total + ins[n * count + k][...]
        for x in range(2):
            scr[2 * n + x] = total[:, x * cols : (x + 1) * cols]
    for k in range(count):
        outs[k][...] = scr[lax.rem(spot_ref[2] + k, count)]


def last_pieces_kernel(spot_ref, *refs):
    ins, out_ref, scr = refs[:4], refs[4], refs[5]
    count = len(ins)
    cols = ins[0].shape[1]
    for k, ref in enumerate(ins):
        scr[lax.rem(spot_ref[2] - k + count, count)] = ref[...]
    for g in range(count):
        out_ref[:, g * cols : (g + 1) * cols] = scr[g]


def small_call(kernel, outs, scratch, name, spot, parts):
    return pl.pallas_call(
        kernel,
        in_specs=[SMEM] + [VMEM] * len(parts),
        out_specs=[VMEM] * len(outs),
        out_shape=[jax.ShapeDtypeStruct(shape, f32) for shape in outs],
        scratch_shapes=[pltpu.VMEM(scratch, f32)],
        compiler_params=params(16),
        name=name,
    )(spot, *parts)


def utterance_of(positions, utt_ends):
    return jnp.sum((utt_ends <= positions[..., None]).astype(jnp.int32), axis=-1)


def per_device(
    frames, utt_lengths, vis_frames, vis_count, teacher_qkv, teacher_out, student_weights
):
    tok, width = frames.shape
    seq, seq_count = lax.axis_index("seq"), lax.axis_size("seq")
    place, groups = lax.axis_index("copy"), lax.axis_size("copy")
    cols = teacher_out.shape[0]
    heads = cols // HEAD_DIM
    wide = heads * LANES
    first_frame = seq * tok
    here = vis_frames.shape[0]
    copies = here * groups
    slots = vis_frames.shape[2]
    members = copies // CHUNKS
    core = lax.rem(seq, CORES)
    swap = [(n, n ^ 1) for n in range(seq_count)]

    up = [(n, n + 1) for n in range(seq_count - 1)]
    left = lax.ppermute(frames, "seq", up)
    right = lax.ppermute(frames, "seq", [(j, n) for n, j in up])

    def from_group(value):
        spread = lambda k: [(n, (n - k) % groups) for n in range(groups)]
        return [value] + [lax.ppermute(value, "copy", spread(k)) for k in (2, 1, 3)]

    def by_turn(parts):
        return [parts[0], parts[2], parts[1], parts[3]]

    utt_ends = jnp.cumsum(utt_lengths)
    near = seq - 1 + jnp.arange(3, dtype=jnp.int32)
    inside = (near >= 0) & (near < seq_count)
    near_ids = jnp.clip(near, 0, seq_count - 1)
    near_lists = jnp.take(vis_frames, near_ids, axis=1)
    near_counts = jnp.where(inside, jnp.take(vis_count, near_ids, axis=1), 0)
    near_live = jnp.arange(slots, dtype=jnp.int32) < near_counts[..., None]
    slot_utt = utterance_of((near * tok)[None, :, None] + near_lists, utt_ends)
    marks = jnp.stack([jnp.where(near_live, near_lists, -1), jnp.where(near_live, slot_utt, -1)], 1)
    marks = jnp.stack(by_turn(from_group(marks)))
    marks = jnp.take(marks, lax.rem(jnp.arange(groups) - place + groups, groups), axis=0)
    marks = marks.reshape(copies, 2, 3, slots)
    picks, utts = marks[:, 0], marks[:, 1]

    half_rows = cols // CORES
    out_mine = lax.all_gather(
        lax.dynamic_slice_in_dim(teacher_out, core * half_rows, half_rows, 0), "copy", axis=0
    )

    reach_pos = first_frame - tok + jnp.arange(3 * tok, dtype=jnp.int32)
    reach_in = (reach_pos >= 0) & (reach_pos < seq_count * tok)
    reach_utt = jnp.where(reach_in, utterance_of(reach_pos, utt_ends), -1)
    reach_col = reach_utt[tok : 2 * tok].reshape(tok, 1)
    reach_row = reach_utt.reshape(1, 3 * tok)

    spot = jnp.stack([place * cols // LANES, lax.rem(place, 2)])
    teacher_in = jnp.swapaxes(teacher_qkv, 1, 2)
    own_student, own_teacher = project(spot, [frames], student_weights, teacher_in, 0, "project_own")
    side_student, side_teacher = project(
        spot, [left, right], student_weights, teacher_in, 1, "project_side"
    )

    saved, gathered = [], []
    whole = lambda a: pl.BlockSpec(a.shape, lambda c, n=a.ndim: (0,) * n)
    prob_shape = (heads // 2, 2 * slots, 3 * slots)
    for chunk in range(CHUNKS):
        extra = 1 if chunk == 0 else 0
        lag = lambda c, extra=extra: jnp.maximum(c - extra, 0)
        two = lambda shape: pl.BlockSpec(
            (2,) + shape, lambda c, lag=lag, n=len(shape): (lag(c),) + (0,) * n
        )
        ins = [own_student, side_student, picks, utts]
        out_specs = [
            pl.BlockSpec((1, slots, 2 * cols), lambda c: (c, 0, 0)),
            two(prob_shape),
            two((slots, wide)),
            two((3 * slots, 2 * wide)),
        ]
        out_shape = [
            jax.ShapeDtypeStruct((members // 2 + extra, slots, 2 * cols), bf16),
            jax.ShapeDtypeStruct((members,) + prob_shape, f32),
            jax.ShapeDtypeStruct((members, slots, wide), bf16),
            jax.ShapeDtypeStruct((members, 3 * slots, 2 * wide), bf16),
        ]
        if chunk == 0:
            kernel = forward_first_kernel
            ins += [own_teacher, side_teacher, reach_col, reach_row]
        else:
            kernel = functools.partial(forward_next_kernel, base=chunk * members)
            ins += [left, frames, right]
            out_specs.append(pl.BlockSpec((width, 3 * tok), lambda c: (0, 0)))
            out_shape.append(jax.ShapeDtypeStruct((width, 3 * tok), bf16))
        attn, probs, query, kv, *rest = pl.pallas_call(
            kernel,
            grid=(members // 2 + extra,),
            in_specs=[whole(a) for a in ins],
            out_specs=out_specs,
            out_shape=out_shape,
            compiler_params=params(32),
            cost_estimate=pl.CostEstimate(
                flops=members * (4 * heads * slots * 3 * slots * LANES + 2 * slots * tok * 7 * wide),
                bytes_accessed=8 << 20,
                transcendentals=members * heads * slots * 3 * slots,
            ),
            name=f"student_forward{chunk}",
        )(*ins)
        gathered.append(by_turn(from_group(attn)))
        saved.append((probs, query, kv))
        turned = rest[0] if rest else None
        if chunk == 0:
            out_late, _ = lax.optimization_barrier((out_mine, attn))
            out_other = lax.ppermute(out_late, "seq", swap)

    info = jnp.stack([core, place])
    targets = pl.pallas_call(
        targets_kernel,
        in_specs=[SMEM] + [VMEM] * 7,
        out_specs=VMEM,
        out_shape=jax.ShapeDtypeStruct((tok, width), bf16),
        scratch_shapes=[pltpu.VMEM((groups, tok // 2, 2 * cols), bf16)],
        compiler_params=params(20),
        cost_estimate=pl.CostEstimate(
            flops=2 * tok * width * width, bytes_accessed=5 << 20, transcendentals=0
        ),
        name="teacher_targets",
    )(info, *gathered[0], out_mine, out_other, frames)

    coef = 2.0 / (width**0.5 * copies)
    rows = members * slots
    carried = ()
    for chunk in range(CHUNKS):
        final = chunk == CHUNKS - 1
        probs, query, kv = saved[chunk]
        side_f32 = lambda n: jax.ShapeDtypeStruct((n * tok, cols), f32)
        out_o = jax.ShapeDtypeStruct((width, cols), f32)
        if final:
            outs = [
                jax.ShapeDtypeStruct((3 * tok, 4 * cols), bf16),
                jax.ShapeDtypeStruct((3 * tok, 2 * cols), bf16),
                out_o,
            ]
        else:
            outs = [side_f32(1), side_f32(3), side_f32(3), out_o]
        carried = pl.pallas_call(
            functools.partial(backward_kernel, base=chunk * members, coef=coef, final=final, skip=1 - min(chunk, 1)),
            in_specs=[SMEM] + [VMEM] * 4 + [HBM] + [VMEM] * 3 + [HBM] * 3 + [VMEM] * len(carried),
            out_specs=[VMEM] * len(outs),
            out_shape=outs,
            scratch_shapes=[
                pltpu.VMEM((width, width), bf16),
                pltpu.VMEM(probs.shape, f32),
                pltpu.VMEM(query.shape, bf16),
                pltpu.VMEM(kv.shape, bf16),
                pltpu.VMEM((groups, members // 2, slots, 2 * cols), bf16),
                pltpu.VMEM((rows, width), bf16),
                pltpu.VMEM((rows, width), f32),
                pltpu.VMEM((rows, width), f32),
                pltpu.VMEM((rows, width), bf16),
                pltpu.VMEM((rows, cols), bf16),
                pltpu.VMEM((rows, wide), bf16),
                pltpu.VMEM((rows, wide), bf16),
                pltpu.VMEM((3, rows, 2 * wide), bf16),
                pltpu.SemaphoreType.DMA((4,)),
            ],
            compiler_params=params(44),
            cost_estimate=pl.CostEstimate(
                flops=members * slots * width * width * 6, bytes_accessed=16 << 20, transcendentals=0
            ),
            name=f"student_backward{chunk}",
        )(
            info, *gathered[chunk], student_weights, frames, targets, picks,
            probs, query, kv, *carried,
        )

    away = weight_grads((1 - core).reshape(1), turned, *carried, "weights_away")
    arrived = lax.ppermute(away, "seq", swap)
    kept = weight_grads(core.reshape(1), turned, *carried, "weights_kept")

    ring = RING
    span = CORES * ring
    spot = jnp.stack([lax.rem(seq // CORES, ring), seq // span, place])

    def z_pairs(k):
        return [
            (n, n // span * span + ((n // CORES + k) % ring) * CORES + n % CORES)
            for n in range(seq_count)
        ]

    def y_pairs(k):
        return [(n, (n + k * span) % seq_count) for n in range(seq_count)]

    def exchange(pieces, firsts, seconds):
        order = (2, 1, 3)
        lead = [lax.ppermute(pieces[k], "seq", firsts(k)) for k in order]
        rest = [lax.ppermute(pieces[ring + k], "seq", seconds(k)) for k in order]
        return [pieces[0]] + lead + [pieces[ring]] + rest

    out_rows = width // seq_count
    pieces = small_call(
        first_pieces_kernel, [(2 * out_rows, 4 * cols)] * 8, kept.shape, "pieces1", spot, [kept, arrived]
    )
    pieces = exchange(pieces, z_pairs, y_pairs)
    pieces = small_call(
        second_pieces_kernel, [(out_rows, 2 * cols)] * 8, (4, out_rows, 2 * cols), "pieces2", spot, pieces
    )
    pieces = exchange(pieces, y_pairs, z_pairs)
    pieces = small_call(
        third_pieces_kernel, [(out_rows, cols)] * 4, (4, out_rows, cols), "pieces3", spot, pieces
    )
    forward = lambda k: [(n, (n + k) % groups) for n in range(groups)]
    pieces = [pieces[0]] + [lax.ppermute(pieces[k], "copy", forward(k)) for k in (1, 2, 3)]
    return small_call(
        last_pieces_kernel, [(out_rows, 4 * cols)], (4, out_rows, cols), "pieces4", spot, pieces
    )[0]


def solution(mesh):
    placed = (
        P("seq", None),
        P(),
        P("copy", None, None),
        P("copy", None),
        P(None, None, "copy"),
        P("copy", None),
        P(),
    )
    return jax.shard_map(
        per_device, mesh=mesh, in_specs=placed, out_specs=P(("seq", "copy"), None), check_vma=False
    )
```

```python
import functools

import jax
import jax.numpy as jnp
from jax import lax
from jax.experimental import pallas as pl
from jax.experimental.pallas import tpu as pltpu
from jax.sharding import PartitionSpec as P

HEADS = 16
HEAD_DIM = 80
LANES = 128
CHUNKS = (2, 4, 2)
CORES = 2
RING = 4

norm_eps = 1e-05
mask_fill = -1e30
score_scale = HEAD_DIM ** (-0.5)
bf16 = jnp.bfloat16
f32 = jnp.float32
VMEM = pl.BlockSpec(memory_space=pltpu.VMEM)
SMEM = pl.BlockSpec(memory_space=pltpu.SMEM)
HBM = pl.BlockSpec(memory_space=pl.ANY)


def dot(a, b):
    return lax.dot_general(a, b, (((1,), (0,)), ((), ())), preferred_element_type=f32)


def dot_nt(a, b):
    return lax.dot_general(a, b, (((1,), (1,)), ((), ())), preferred_element_type=f32)


def dot_tn(a, b):
    return lax.dot_general(a, b, (((0,), (0,)), ((), ())), preferred_element_type=f32)


def widen_heads(x):
    rows, cols = x.shape
    gap = jnp.zeros((rows, LANES - HEAD_DIM), x.dtype)
    parts = []
    for h in range(cols // HEAD_DIM):
        parts += [x[:, h * HEAD_DIM : (h + 1) * HEAD_DIM], gap]
    return jnp.concatenate(parts, axis=1)


def narrow_heads(x):
    return jnp.concatenate(
        [x[:, h * LANES : h * LANES + HEAD_DIM] for h in range(x.shape[1] // LANES)], axis=1
    )


def softmax_rows(scores, allowed):
    masked = jnp.where(allowed, scores, mask_fill)
    expo = jnp.exp(masked - jnp.max(masked, axis=-1, keepdims=True))
    return expo * (1.0 / jnp.sum(expo, axis=-1, keepdims=True))


def layer_norm(values):
    centre = values - jnp.mean(values, axis=-1, keepdims=True)
    spread = jnp.mean(centre * centre, axis=-1, keepdims=True)
    return centre * lax.rsqrt(spread + norm_eps)


def params(mib):
    return pltpu.CompilerParams(vmem_limit_bytes=mib << 20)


def column_of(row):
    count = row.shape[1]
    return jnp.transpose(jnp.broadcast_to(row, (count, count)))


def select_rows(row, count):
    slots = row.shape[1]
    column = column_of(row)
    column = jnp.concatenate([column] * (count // slots), axis=1)
    return (lax.broadcasted_iota(jnp.int32, (slots, count), 1) == column).astype(bf16)


def select_rows_t(row, count):
    slots = row.shape[1]
    return (lax.broadcasted_iota(jnp.int32, (count, slots), 0) == row).astype(bf16)


def split_pair(x):
    gap = jnp.zeros((x.shape[0], LANES), x.dtype)
    top = jnp.concatenate([x[:, :LANES], gap], axis=1)
    low = jnp.concatenate([gap, x[:, LANES:]], axis=1)
    return jnp.concatenate([top, low], axis=0)


def join_pair(x):
    rows = x.shape[0] // 2
    return jnp.concatenate([x[:rows, :LANES], x[rows:, LANES:]], axis=1)


def project_kernel(spot_ref, *refs, sides):
    rows_refs, (w0, w1, w2, wt, student_ref, teacher_ref) = refs[:sides], refs[sides:]
    cols = wt.shape[1]
    rows = jnp.concatenate([r[...] for r in rows_refs], axis=0)
    weights = jnp.concatenate([w0[...], w1[...], w2[...]], axis=1)
    student = dot(rows, weights).astype(bf16)
    teacher_ref[...] = widen_heads(dot_nt(rows, wt[0]).astype(bf16))
    shift = LANES // 2
    for odd in range(2):
        @pl.when(spot_ref[1] == odd)
        def _():
            student_ref[...] = widen_heads(student[:, odd * shift : odd * shift + cols])


def project(spot, rows, student_weights, teacher_qkv, first, name):
    count = len(rows)
    tok, width = rows[0].shape
    cols = teacher_qkv.shape[1]
    wide = cols // HEAD_DIM * LANES
    mats = 3 - first
    window = lambda j: pl.BlockSpec((width, LANES), lambda m, spot, j=j: (m + first, spot[0] + j))
    out = jax.ShapeDtypeStruct((count * tok, mats * wide), bf16)
    return pl.pallas_call(
        functools.partial(project_kernel, sides=count),
        grid_spec=pltpu.PrefetchScalarGridSpec(
            num_scalar_prefetch=1,
            grid=(mats,),
            in_specs=[pl.BlockSpec((tok, width), lambda m, spot: (0, 0))] * count
            + [window(j) for j in range(3)]
            + [pl.BlockSpec((1, cols, width), lambda m, spot: (m + first, 0, 0))],
            out_specs=[pl.BlockSpec((count * tok, wide), lambda m, spot: (0, m))] * 2,
        ),
        out_shape=[out, out],
        compiler_params=params(52),
        cost_estimate=pl.CostEstimate(
            flops=2 * count * tok * width * 768 * mats, bytes_accessed=6 << 20, transcendentals=0
        ),
        name=name,
    )(spot, *rows, student_weights, student_weights, student_weights, teacher_qkv)


def teacher_heads(own_ref, side_ref, reach_ref):
    rows = own_ref.shape[0]
    wide = own_ref.shape[1] // 3
    spans = reach_ref.shape[0]
    reach = [reach_ref[n : n + 1, :] for n in range(spans)]
    column = jnp.concatenate([column_of(reach[n]) for n in (2, 3)], axis=0)
    allowed = jnp.concatenate([column] * spans, axis=1) == jnp.concatenate(reach, axis=1)
    parts = []
    for h in range(wide // LANES):
        sl = slice(h * LANES, (h + 1) * LANES)
        sk = slice(wide + h * LANES, wide + (h + 1) * LANES)
        sv = slice(2 * wide + h * LANES, 2 * wide + (h + 1) * LANES)
        keys = jnp.concatenate([side_ref[:rows, sl], own_ref[:, sk], side_ref[rows:, sl]], axis=0)
        vals = jnp.concatenate([side_ref[:rows, sk], own_ref[:, sv], side_ref[rows:, sk]], axis=0)
        probs = softmax_rows(dot_nt(own_ref[:, sl], keys) * score_scale, allowed).astype(bf16)
        parts.append(dot(probs, vals).astype(bf16)[:, :HEAD_DIM])
    attn = jnp.concatenate(parts, axis=1)
    return jnp.concatenate([attn[: rows // 2], attn[rows // 2 :]], axis=1)


def targets_kernel(a0, a1, a2, a3, mine_ref, other_ref, frames_ref, out_ref, attn_scr):
    groups = len((a0, a1, a2, a3))
    cols = a0.shape[2] // 2
    part = cols // 2
    even = lax.rem(lax.axis_index("seq"), CORES) == 0
    place = lax.axis_index("copy")
    for k, ref in enumerate((a0, a1, a2, a3)):
        attn_scr[lax.rem(place + k, groups)] = ref[0]
    low, high = [], []
    for g in range(groups):
        block = attn_scr[g]
        rows = jnp.concatenate([block[:, :cols], block[:, cols:]], axis=0)
        low.append(rows[:, :part])
        high.append(rows[:, part:])
    low, high = jnp.concatenate(low, axis=1), jnp.concatenate(high, axis=1)
    depth, width = groups * part, mine_ref.shape[-1]
    mine = mine_ref[...].reshape(depth, width)
    other = other_ref[...].reshape(depth, width)
    lhs_mine = jnp.where(even, low, high)
    lhs_other = jnp.where(even, high, low)
    wide_frames = frames_ref[...].astype(f32)
    mixing = dot(lhs_mine, mine) + dot(lhs_other, other)
    out_ref[...] = layer_norm(0.5 * (wide_frames + layer_norm(wide_frames + mixing))).astype(bf16)


def marks_kernel(lengths_ref, counts_ref, lists_ref, marks_ref, reach_ref, *, tok, blocks):
    seq = lax.axis_index("seq")
    copies, _, slots = lists_ref.shape
    lane = lax.broadcasted_iota(jnp.int32, (1, slots), 1)
    picks, places = [], []
    for c in range(copies):
        for j in range(3):
            near = seq - 1 + j
            block = jnp.clip(near, 0, blocks - 1)
            row = lists_ref[c, pl.ds(block, 1), :]
            count = jnp.where(near == block, counts_ref[c, block], 0)
            live = lane < count
            picks.append(jnp.where(live, row, -1))
            places.append(jnp.where(live, near * tok + row, -1))
    spans = reach_ref.shape[0]
    for n in range(spans):
        place = (seq - 1) * tok + n * slots + lane
        places.append(jnp.where((place >= 0) & (place < blocks * tok), place, -1))
    places = jnp.concatenate(places, axis=0)

    def passed(u, carry):
        end, utt = carry
        end = end + lengths_ref[u]
        return end, utt + jnp.where(end <= places, 1, 0)

    start = (jnp.int32(0), jnp.zeros(places.shape, jnp.int32))
    _, utt = lax.fori_loop(0, lengths_ref.shape[0], passed, start, unroll=8)
    utt = jnp.where(places >= 0, utt, -1)
    for c in range(copies):
        for j in range(3):
            n = 3 * c + j
            marks_ref[c, 0, j : j + 1, :] = picks[n]
            marks_ref[c, 1, j : j + 1, :] = utt[n : n + 1, :]
    reach_ref[...] = utt[3 * copies :, :]


def forward_first_kernel(
    own_ref, side_ref, town_ref, tside_ref, reach_ref, m0, m1, m2, m3,
    attn_ref, prob_ref, query_ref, kv_ref, pick_ref, utt_ref,
):
    step = pl.program_id(0)

    @pl.when(step == 0)
    def _():
        place = lax.axis_index("copy")
        marks = (m0, m1, m2, m3)
        here = m0.shape[0]
        for k, ref in enumerate(marks):
            group = lax.rem(place + k, len(marks))
            for c in range(here):
                pick_ref[group * here + c] = ref[c, 0]
                utt_ref[group * here + c] = ref[c, 1]
        attn_ref[0] = teacher_heads(town_ref, tside_ref, reach_ref)

    @pl.when(step > 0)
    def _():
        forward_pair(
            own_ref, side_ref, pick_ref, utt_ref, attn_ref, prob_ref, query_ref, kv_ref, 2 * step - 2
        )


def forward_middle_kernel(own_ref, side_ref, pick_ref, utt_ref, *outs, base):
    forward_pair(own_ref, side_ref, pick_ref, utt_ref, *outs, base + 2 * pl.program_id(0))


def forward_last_kernel(
    own_ref, side_ref, pick_ref, utt_ref, left_ref, frames_ref, right_ref,
    attn_ref, prob_ref, query_ref, kv_ref, turned_ref, *, base,
):
    step = pl.program_id(0)

    @pl.when(step == 0)
    def _():
        tok = frames_ref.shape[0]
        for j, ref in enumerate((left_ref, frames_ref, right_ref)):
            turned_ref[:, j * tok : (j + 1) * tok] = jnp.transpose(ref[...])

    forward_pair(
        own_ref, side_ref, pick_ref, utt_ref, attn_ref, prob_ref, query_ref, kv_ref, base + 2 * step
    )


def forward_pair(
    own_ref, side_ref, pick_ref, utt_ref, attn_ref, prob_ref, query_ref, kv_ref, first
):
    tok = own_ref.shape[0]
    wide = own_ref.shape[1] // 3
    pairs = wide // (2 * LANES)
    slots = pick_ref.shape[2]
    tables = [side_ref[:tok, :], own_ref[:, wide:], side_ref[tok:, :]]
    kv_parts, query = [], None
    for j in range(3):
        pick = jnp.concatenate(
            [select_rows(pick_ref[first + c, j : j + 1, :], tok) for c in range(2)], axis=0
        )
        kv_parts.append(dot(pick, tables[j]).astype(bf16))
        if j == 1:
            query = dot(pick, own_ref[:, :wide]).astype(bf16)
    for c in range(2):
        rows = slice(c * slots, (c + 1) * slots)
        kv = jnp.concatenate([part[rows] for part in kv_parts], axis=0)
        kv_ref[c] = kv
        query_ref[c] = query[rows]
        utt = utt_ref[first + c]
        utt_row = jnp.concatenate([utt[j : j + 1, :] for j in range(3)], axis=1)
        utt_col = column_of(utt[1:2, :])
        allowed = jnp.concatenate([utt_col] * 3, axis=1) == utt_row
        allowed = jnp.concatenate([allowed, allowed], axis=0)
        parts = []
        for p in range(pairs):
            sl = slice(2 * p * LANES, 2 * (p + 1) * LANES)
            sv = slice(wide + 2 * p * LANES, wide + 2 * (p + 1) * LANES)
            scores = dot_nt(split_pair(query[rows, sl]), kv[:, sl]) * score_scale
            probs = softmax_rows(scores, allowed)
            prob_ref[c, p] = probs
            parts.append(join_pair(dot(probs.astype(bf16), kv[:, sv]).astype(bf16)))
        attn = narrow_heads(jnp.concatenate(parts, axis=1))
        cols = attn.shape[1]
        attn_ref[0, :, c * cols : (c + 1) * cols] = attn


def backward_kernel(
    a0, a1, a2, a3, wout_hbm, frames_ref, goal_ref, pick_ref,
    prob_hbm, query_hbm, kv_hbm, *refs, base, coef, final, skip,
):
    earlier, refs = (refs[:4], refs[4:]) if base else (None, refs)
    if final:
        turned_ref, away_ref, qk_ref, v_ref, go_ref = refs[:5]
        refs = refs[5:]
    else:
        gq_ref, gk_ref, gv_ref, go_ref = refs[:4]
        refs = refs[4:]
    (
        wout_scr, prob_scr, query_scr, kv_scr, stack_scr, full_scr, sum_scr, goal_scr,
        grad_scr, ng_scr, ag_scr, dq_scr, dkv_scr, sems,
    ) = refs
    members, pairs = prob_scr.shape[:2]
    slots = query_scr.shape[1]
    wide = query_scr.shape[2]
    tok, width = frames_ref.shape
    groups = stack_scr.shape[0]
    cols = a0.shape[2] // 2
    place = lax.axis_index("copy")

    copies = [
        pltpu.make_async_copy(src, dst, sems.at[n])
        for n, (src, dst) in enumerate(
            (
                (wout_hbm.at[pl.ds(3 * width, width), :], wout_scr),
                (kv_hbm, kv_scr),
                (prob_hbm, prob_scr),
                (query_hbm, query_scr),
            )
        )
    ]
    for copy in copies:
        copy.start()

    for k, ref in enumerate((a0, a1, a2, a3)):
        stack_scr[lax.rem(place + k, groups)] = ref[skip:]
    for g in range(groups):
        for m in range(members):
            half = m % 2
            full_scr[m * slots : (m + 1) * slots, g * cols : (g + 1) * cols] = stack_scr[
                g, m // 2, :, half * cols : (half + 1) * cols
            ]
    pick = jnp.concatenate(
        [select_rows(pick_ref[base + m, 1:2, :], tok) for m in range(members)], axis=0
    )
    goal_scr[...] = dot(pick, goal_ref[...])
    sum_scr[...] = dot(pick, frames_ref[...])
    copies[0].wait()
    sum_scr[...] += dot(full_scr[...], wout_scr[...])
    block = 32

    def norm_rows(n, carry):
        here = pl.ds(pl.multiple_of(n * block, block), block)
        summed = sum_scr[here, :]
        centre = summed - jnp.mean(summed, axis=-1, keepdims=True)
        factor = lax.rsqrt(jnp.mean(centre * centre, axis=-1, keepdims=True) + norm_eps)
        normed = centre * factor
        upstream = (normed - goal_scr[here, :]) * coef
        part = upstream - jnp.mean(upstream, axis=-1, keepdims=True)
        part = part - normed * jnp.mean(upstream * normed, axis=-1, keepdims=True)
        grad_scr[here, :] = (part * factor).astype(bf16)
        return carry

    lax.fori_loop(0, members * slots // block, norm_rows, 0, unroll=4)
    for m in range(members):
        rows = slice(m * slots, (m + 1) * slots)
        live = column_of(pick_ref[base + m, 1:2, :]) >= 0
        live = jnp.concatenate([live] * (width // LANES), axis=1)
        grad_scr[rows, :] = jnp.where(live, grad_scr[rows, :], jnp.zeros((), bf16))
    grad = grad_scr[...]
    for g in range(groups):
        @pl.when(place == g)
        def _():
            ng_scr[...] = grad_scr[:, g * cols : (g + 1) * cols]

    own_rows = wout_scr[pl.ds(pl.multiple_of(place * cols, LANES // 2), cols), :]
    ag_scr[...] = widen_heads(dot_nt(grad, own_rows).astype(bf16))
    for copy in copies[1:]:
        copy.wait()
    for m in range(members):
        rows = slice(m * slots, (m + 1) * slots)
        for p in range(pairs):
            sl = slice(2 * p * LANES, 2 * (p + 1) * LANES)
            sv = slice(wide + 2 * p * LANES, wide + 2 * (p + 1) * LANES)
            probs = prob_scr[m, p]
            grads = split_pair(ag_scr[rows, sl])
            prob_grad = dot_nt(grads, kv_scr[m, :, sv])
            inner = jnp.sum(probs * prob_grad, axis=-1, keepdims=True)
            score_grad = (probs * (prob_grad - inner) * score_scale).astype(bf16)
            dq_scr[rows, sl] = join_pair(dot(score_grad, kv_scr[m, :, sl]).astype(bf16))
            dk = dot_tn(score_grad, split_pair(query_scr[m, :, sl])).astype(bf16)
            dv = dot_tn(probs.astype(bf16), grads).astype(bf16)
            for j in range(3):
                dkv_scr[j, rows, sl] = dk[j * slots : (j + 1) * slots]
                dkv_scr[j, rows, sv] = dv[j * slots : (j + 1) * slots]

    keys, values, query = [], [], None
    for j in range(3):
        row = jnp.concatenate([pick_ref[base + m, j : j + 1, :] for m in range(members)], axis=1)
        pick_t = select_rows_t(row, tok)
        total = dot(pick_t, dkv_scr[j])
        keys.append(narrow_heads(total[:, :wide]))
        values.append(narrow_heads(total[:, wide:]))
        if j == 1:
            query = narrow_heads(dot(pick_t, dq_scr[...]))
    keys, values = jnp.concatenate(keys, axis=0), jnp.concatenate(values, axis=0)
    out = dot_tn(full_scr[...], ng_scr[...])
    if base:
        query = query + earlier[0][...]
        keys = keys + earlier[1][...]
        values = values + earlier[2][...]
        out = out + earlier[3][...]
    if not final:
        gq_ref[...], gk_ref[...], gv_ref[...], go_ref[...] = query, keys, values, out
        return
    gap = jnp.zeros((tok, cols), f32)
    both = jnp.concatenate([jnp.concatenate([gap, query, gap], axis=0), keys], axis=1)
    for ref, full in ((qk_ref, both), (v_ref, values)):
        wide_cols = full.shape[1]
        top = full.astype(bf16)
        ref[:, :wide_cols] = top
        ref[:, wide_cols:] = (full - top.astype(f32)).astype(bf16)
    go_ref[...] = out.reshape(go_ref.shape)
    other = 1 - lax.rem(lax.axis_index("seq"), CORES)
    weight_rows(
        turned_ref[:, other], qk_ref[...], v_ref[...], lambda z: go_ref[z, other], away_ref
    )


def weight_rows(turned, qk, v, out_rows, out_ref):
    count, rows, reach = turned.shape
    cols = v.shape[1] // 2
    part = rows // 2
    lhs = turned.reshape(count * rows, reach)
    both = dot(lhs, qk)
    both = both[:, : 2 * cols] + both[:, 2 * cols :]
    value = dot(lhs, v)
    value = value[:, :cols] + value[:, cols:]
    for z in range(count):
        top = slice(z * rows, z * rows + part)
        low = slice(z * rows + part, (z + 1) * rows)
        last = out_rows(z)
        out_ref[z * part : (z + 1) * part, : 2 * cols] = both[top]
        out_ref[z * part : (z + 1) * part, 2 * cols : 3 * cols] = value[top]
        out_ref[z * part : (z + 1) * part, 3 * cols :] = last[:part]
        here = slice(z * cols, (z + 1) * cols)
        for m, full in enumerate((both[low, :cols], both[low, cols:], value[low], last[part:])):
            at = (count + m) * part
            out_ref[at : at + part, here] = full


def weights_kernel(turned_ref, qk_ref, v_ref, go_ref, out_ref):
    half = lax.rem(lax.axis_index("seq"), CORES)
    weight_rows(turned_ref[:, half], qk_ref[...], v_ref[...], lambda z: go_ref[z, half], out_ref)


def torus_place():
    seq = lax.axis_index("seq")
    return lax.rem(seq // CORES, RING), seq // (CORES * RING), lax.axis_index("copy")


def first_pieces_kernel(kept_ref, arrived_ref, *refs):
    outs, scr = refs[:-1], refs[-1]
    scr[...] = kept_ref[...] + arrived_ref[...]
    spot = torus_place()
    rows = outs[0].shape[0]
    count = len(outs) // 2
    for n in range(2):
        for k in range(count):
            at = n * count + lax.rem(spot[n] + k, count)
            outs[n * count + k][...] = scr[pl.ds(pl.multiple_of(at * rows, 8), rows), :]


def second_pieces_kernel(*refs):
    count = 4
    ins, outs, scr = refs[: 2 * count], refs[2 * count : 4 * count], refs[4 * count]
    rows, wide = outs[0].shape
    cols = wide // 2
    spot = torus_place()
    for n in range(2):
        total = ins[n * count][...]
        for k in range(1, count):
            total = total + ins[n * count + k][...]
        for m in range(count):
            for x in range(2):
                scr[m, :, x * cols : (x + 1) * cols] = total[
                    x * rows : (x + 1) * rows, m * cols : (m + 1) * cols
                ]
        for k in range(count):
            outs[n * count + k][...] = scr[lax.rem(spot[1 - n] + k, count)]


def third_pieces_kernel(*refs):
    count = 4
    ins, outs, scr = refs[: 2 * count], refs[2 * count : 3 * count], refs[3 * count]
    cols = outs[0].shape[1]
    for n in range(2):
        total = ins[n * count][...]
        for k in range(1, count):
            total = total + ins[n * count + k][...]
        for x in range(2):
            scr[2 * n + x] = total[:, x * cols : (x + 1) * cols]
    for k in range(count):
        outs[k][...] = scr[lax.rem(torus_place()[2] + k, count)]


def last_pieces_kernel(*refs):
    ins, out_ref, scr = refs[:4], refs[4], refs[5]
    count = len(ins)
    cols = ins[0].shape[1]
    for k, ref in enumerate(ins):
        scr[lax.rem(torus_place()[2] - k + count, count)] = ref[...]
    for g in range(count):
        out_ref[:, g * cols : (g + 1) * cols] = scr[g]


def small_call(kernel, outs, scratch, name, parts):
    return pl.pallas_call(
        kernel,
        in_specs=[VMEM] * len(parts),
        out_specs=[VMEM] * len(outs),
        out_shape=[jax.ShapeDtypeStruct(shape, f32) for shape in outs],
        scratch_shapes=[pltpu.VMEM(scratch, f32)],
        compiler_params=params(16),
        name=name,
    )(*parts)


def per_device(
    frames, utt_lengths, vis_frames, vis_count, teacher_qkv, teacher_out, student_weights
):
    tok, width = frames.shape
    seq, seq_count = lax.axis_index("seq"), lax.axis_size("seq")
    place, groups = lax.axis_index("copy"), lax.axis_size("copy")
    cols = teacher_out.shape[0]
    heads = cols // HEAD_DIM
    wide = heads * LANES
    here = vis_frames.shape[0]
    copies = here * groups
    slots = vis_frames.shape[2]
    core = lax.rem(seq, CORES)
    swap = [(n, n ^ 1) for n in range(seq_count)]

    up = [(n, n + 1) for n in range(seq_count - 1)]
    left = lax.ppermute(frames, "seq", up)
    right = lax.ppermute(frames, "seq", [(j, n) for n, j in up])

    def from_group(value):
        spread = lambda k: [(n, (n - k) % groups) for n in range(groups)]
        return [value] + [lax.ppermute(value, "copy", spread(k)) for k in (2, 1, 3)]

    def by_turn(parts):
        return [parts[0], parts[2], parts[1], parts[3]]

    marks, reach = pl.pallas_call(
        functools.partial(marks_kernel, tok=tok, blocks=seq_count),
        in_specs=[SMEM, SMEM, VMEM],
        out_specs=[VMEM, VMEM],
        out_shape=[
            jax.ShapeDtypeStruct((here, 2, 3, slots), jnp.int32),
            jax.ShapeDtypeStruct((3 * tok // slots, slots), jnp.int32),
        ],
        compiler_params=params(8),
        name="visible_marks",
    )(utt_lengths, vis_count, vis_frames)
    marks = by_turn(from_group(marks))

    half_rows = cols // CORES
    out_mine = lax.all_gather(
        lax.dynamic_slice_in_dim(teacher_out, core * half_rows, half_rows, 0), "copy", axis=0
    )

    spot = jnp.stack([place * cols // LANES, lax.rem(place, 2)])
    teacher_in = jnp.swapaxes(teacher_qkv, 1, 2)
    own_student, own_teacher = project(spot, [frames], student_weights, teacher_in, 0, "project_own")
    side_student, side_teacher = project(
        spot, [left, right], student_weights, teacher_in, 1, "project_side"
    )

    saved, gathered = [], []
    whole = lambda a: pl.BlockSpec(a.shape, lambda c, n=a.ndim: (0,) * n)
    prob_shape = (heads // 2, 2 * slots, 3 * slots)
    bases = [sum(CHUNKS[:n]) for n in range(len(CHUNKS))]
    for chunk, members in enumerate(CHUNKS):
        extra = 1 if chunk == 0 else 0
        lag = lambda c, extra=extra: jnp.maximum(c - extra, 0)
        two = lambda shape: pl.BlockSpec(
            (2,) + shape, lambda c, lag=lag, n=len(shape): (lag(c),) + (0,) * n
        )
        ins = [own_student, side_student]
        out_specs = [
            pl.BlockSpec((1, slots, 2 * cols), lambda c: (c, 0, 0)),
            two(prob_shape),
            two((slots, wide)),
            two((3 * slots, 2 * wide)),
        ]
        out_shape = [
            jax.ShapeDtypeStruct((members // 2 + extra, slots, 2 * cols), bf16),
            jax.ShapeDtypeStruct((members,) + prob_shape, f32),
            jax.ShapeDtypeStruct((members, slots, wide), bf16),
            jax.ShapeDtypeStruct((members, 3 * slots, 2 * wide), bf16),
        ]
        if chunk == 0:
            kernel = forward_first_kernel
            ins += [own_teacher, side_teacher, reach, *marks]
            out_specs += [pl.BlockSpec((copies, 3, slots), lambda c: (0, 0, 0))] * 2
            out_shape += [jax.ShapeDtypeStruct((copies, 3, slots), jnp.int32)] * 2
        elif chunk < len(CHUNKS) - 1:
            kernel = functools.partial(forward_middle_kernel, base=bases[chunk])
            ins += [picks, utts]
        else:
            kernel = functools.partial(forward_last_kernel, base=bases[chunk])
            ins += [picks, utts, left, frames, right]
            out_specs.append(pl.BlockSpec((width, 3 * tok), lambda c: (0, 0)))
            out_shape.append(jax.ShapeDtypeStruct((width, 3 * tok), bf16))
        attn, probs, query, kv, *rest = pl.pallas_call(
            kernel,
            grid=(members // 2 + extra,),
            in_specs=[whole(a) for a in ins],
            out_specs=out_specs,
            out_shape=out_shape,
            compiler_params=params(56),
            cost_estimate=pl.CostEstimate(
                flops=members * (4 * heads * slots * 3 * slots * LANES + 2 * slots * tok * 7 * wide),
                bytes_accessed=8 << 20,
                transcendentals=members * heads * slots * 3 * slots,
            ),
            name=f"student_forward{chunk}",
        )(*ins)
        gathered.append(by_turn(from_group(attn)))
        saved.append((probs, query, kv))
        if chunk == len(CHUNKS) - 1:
            turned = rest[0]
        if chunk == 0:
            picks, utts = rest
            out_late, _ = lax.optimization_barrier((out_mine, attn))
            out_other = lax.ppermute(out_late, "seq", swap)

    targets = pl.pallas_call(
        targets_kernel,
        in_specs=[VMEM] * 7,
        out_specs=VMEM,
        out_shape=jax.ShapeDtypeStruct((tok, width), bf16),
        scratch_shapes=[pltpu.VMEM((groups, tok // 2, 2 * cols), bf16)],
        compiler_params=params(20),
        cost_estimate=pl.CostEstimate(
            flops=2 * tok * width * width, bytes_accessed=5 << 20, transcendentals=0
        ),
        name="teacher_targets",
    )(*gathered[0], out_mine, out_other, frames)

    coef = 2.0 / (width**0.5 * copies)
    carried = ()
    for chunk, members in enumerate(CHUNKS):
        rows = members * slots
        final = chunk == len(CHUNKS) - 1
        probs, query, kv = saved[chunk]
        side_f32 = lambda n: jax.ShapeDtypeStruct((n * tok, cols), f32)
        out_o = jax.ShapeDtypeStruct((width, cols), f32)
        if final:
            outs = [
                jax.ShapeDtypeStruct((width // CORES, 4 * cols), f32),
                jax.ShapeDtypeStruct((3 * tok, 4 * cols), bf16),
                jax.ShapeDtypeStruct((3 * tok, 2 * cols), bf16),
                jax.ShapeDtypeStruct((RING, CORES, width // RING // CORES, cols), f32),
            ]
            carried = (*carried, turned.reshape(RING, CORES, width // RING // CORES, 3 * tok))
        else:
            outs = [side_f32(1), side_f32(3), side_f32(3), out_o]
        carried = pl.pallas_call(
            functools.partial(backward_kernel, base=bases[chunk], coef=coef, final=final, skip=1 - min(chunk, 1)),
            in_specs=[VMEM] * 4 + [HBM] + [VMEM] * 3 + [HBM] * 3 + [VMEM] * len(carried),
            out_specs=[VMEM] * len(outs),
            out_shape=outs,
            scratch_shapes=[
                pltpu.VMEM((width, width), bf16),
                pltpu.VMEM(probs.shape, f32),
                pltpu.VMEM(query.shape, bf16),
                pltpu.VMEM(kv.shape, bf16),
                pltpu.VMEM((groups, members // 2, slots, 2 * cols), bf16),
                pltpu.VMEM((rows, width), bf16),
                pltpu.VMEM((rows, width), f32),
                pltpu.VMEM((rows, width), f32),
                pltpu.VMEM((rows, width), bf16),
                pltpu.VMEM((rows, cols), bf16),
                pltpu.VMEM((rows, wide), bf16),
                pltpu.VMEM((rows, wide), bf16),
                pltpu.VMEM((3, rows, 2 * wide), bf16),
                pltpu.SemaphoreType.DMA((4,)),
            ],
            compiler_params=params(56),
            cost_estimate=pl.CostEstimate(
                flops=members * slots * width * width * 6, bytes_accessed=16 << 20, transcendentals=0
            ),
            name=f"student_backward{chunk}",
        )(
            *gathered[chunk], student_weights, frames, targets, picks,
            probs, query, kv, *carried,
        )

    away, *kept_ins = carried
    arrived = lax.ppermute(away, "seq", swap)
    kept = pl.pallas_call(
        weights_kernel,
        in_specs=[VMEM] * 4,
        out_specs=VMEM,
        out_shape=jax.ShapeDtypeStruct(away.shape, f32),
        compiler_params=params(28),
        cost_estimate=pl.CostEstimate(
            flops=2 * width * 3 * tok * 3 * cols, bytes_accessed=8 << 20, transcendentals=0
        ),
        name="weights_kept",
    )(turned.reshape(RING, CORES, width // RING // CORES, 3 * tok), *kept_ins)

    ring = RING
    span = CORES * ring

    def z_pairs(k):
        return [
            (n, n // span * span + ((n // CORES + k) % ring) * CORES + n % CORES)
            for n in range(seq_count)
        ]

    def y_pairs(k):
        return [(n, (n + k * span) % seq_count) for n in range(seq_count)]

    def exchange(pieces, firsts, seconds):
        order = (2, 1, 3)
        lead = [lax.ppermute(pieces[k], "seq", firsts(k)) for k in order]
        rest = [lax.ppermute(pieces[ring + k], "seq", seconds(k)) for k in order]
        return [pieces[0]] + lead + [pieces[ring]] + rest

    out_rows = width // seq_count
    pieces = small_call(
        first_pieces_kernel, [(2 * out_rows, 4 * cols)] * 8, kept.shape, "pieces1", [kept, arrived]
    )
    pieces = exchange(pieces, z_pairs, y_pairs)
    pieces = small_call(
        second_pieces_kernel, [(out_rows, 2 * cols)] * 8, (4, out_rows, 2 * cols), "pieces2", pieces
    )
    pieces = exchange(pieces, y_pairs, z_pairs)
    pieces = small_call(
        third_pieces_kernel, [(out_rows, cols)] * 4, (4, out_rows, cols), "pieces3", pieces
    )
    forward = lambda k: [(n, (n + k) % groups) for n in range(groups)]
    pieces = [pieces[0]] + [lax.ppermute(pieces[k], "copy", forward(k)) for k in (1, 2, 3)]
    return small_call(
        last_pieces_kernel, [(out_rows, 4 * cols)], (4, out_rows, cols), "pieces4", pieces
    )[0]


def solution(mesh):
    placed = (
        P("seq", None),
        P(),
        P("copy", None, None),
        P("copy", None),
        P(None, None, "copy"),
        P("copy", None),
        P(),
    )
    return jax.shard_map(
        per_device, mesh=mesh, in_specs=placed, out_specs=P(("seq", "copy"), None), check_vma=False
    )
```

```python
import functools

import jax
import jax.numpy as jnp
from jax import lax
from jax.experimental import pallas as pl
from jax.experimental.pallas import tpu as pltpu
from jax.sharding import PartitionSpec as P

HEADS = 16
HEAD_DIM = 80
LANES = 128
CHUNKS = (2, 4, 2)
CORES = 2
RING = 4
CODES = 256.0
OWN_MIB, FORWARD_MIB, BACKWARD_MIB, COMBINE_MIB, KEPT_MIB = 14, 10, 18, 18, 12

norm_eps = 1e-05
mask_fill = -1e30
score_scale = HEAD_DIM ** (-0.5)
bf16 = jnp.bfloat16
f32 = jnp.float32
VMEM = pl.BlockSpec(memory_space=pltpu.VMEM)
SMEM = pl.BlockSpec(memory_space=pltpu.SMEM)
HBM = pl.BlockSpec(memory_space=pltpu.HBM)


def dot(a, b):
    return lax.dot_general(a, b, (((1,), (0,)), ((), ())), preferred_element_type=f32)


def dot_nt(a, b):
    return lax.dot_general(a, b, (((1,), (1,)), ((), ())), preferred_element_type=f32)


def dot_tn(a, b):
    return lax.dot_general(a, b, (((0,), (0,)), ((), ())), preferred_element_type=f32)


def widen_heads(x):
    rows, cols = x.shape
    gap = jnp.zeros((rows, LANES - HEAD_DIM), x.dtype)
    parts = []
    for h in range(cols // HEAD_DIM):
        parts += [x[:, h * HEAD_DIM : (h + 1) * HEAD_DIM], gap]
    return jnp.concatenate(parts, axis=1)


def narrow_heads(x):
    return jnp.concatenate(
        [x[:, h * LANES : h * LANES + HEAD_DIM] for h in range(x.shape[1] // LANES)], axis=1
    )


def softmax_rows(scores, allowed):
    masked = jnp.where(allowed, scores, mask_fill)
    expo = jnp.exp(masked - jnp.max(masked, axis=-1, keepdims=True))
    return expo * (1.0 / jnp.sum(expo, axis=-1, keepdims=True))


def layer_norm(values):
    centre = values - jnp.mean(values, axis=-1, keepdims=True)
    spread = jnp.mean(centre * centre, axis=-1, keepdims=True)
    return centre * lax.rsqrt(spread + norm_eps)


def params(mib):
    return pltpu.CompilerParams(vmem_limit_bytes=mib << 20)


def estimate(micros):
    return pl.CostEstimate(flops=int(micros * 1e9), bytes_accessed=1 << 20, transcendentals=0)


def column_of(row):
    count = row.shape[1]
    return jnp.transpose(jnp.broadcast_to(row, (count, count)))


def select_rows(row, count):
    slots = row.shape[1]
    column = column_of(row)
    column = jnp.concatenate([column] * (count // slots), axis=1)
    return (lax.broadcasted_iota(jnp.int32, (slots, count), 1) == column).astype(bf16)


def select_rows_t(row, count):
    slots = row.shape[1]
    return (lax.broadcasted_iota(jnp.int32, (count, slots), 0) == row).astype(bf16)


def split_pair(x):
    gap = jnp.zeros((x.shape[0], LANES), x.dtype)
    top = jnp.concatenate([x[:, :LANES], gap], axis=1)
    low = jnp.concatenate([gap, x[:, LANES:]], axis=1)
    return jnp.concatenate([top, low], axis=0)


def join_pair(x):
    rows = x.shape[0] // 2
    return jnp.concatenate([x[:rows, :LANES], x[rows:, LANES:]], axis=1)


def project_part(rows, window, weights, student_ref, teacher_ref, side_ref, side_teacher_ref, n):
    cols = weights.shape[0]
    wide = cols // HEAD_DIM * LANES
    tok = student_ref.shape[0]
    here = slice(n * wide, (n + 1) * wide)
    side = slice((n - 1) * wide, n * wide)
    teacher = widen_heads(dot_nt(rows, weights).astype(bf16))
    teacher_ref[:, here] = teacher[:tok]
    if n:
        side_teacher_ref[:, side] = teacher[tok:]
    student = dot(rows, window).astype(bf16)
    shift = LANES // 2
    for odd in range(2):
        @pl.when(lax.rem(lax.axis_index("copy"), 2) == odd)
        def _():
            full = widen_heads(student[:, odd * shift : odd * shift + cols])
            student_ref[:, here] = full[:tok]
            if n:
                side_ref[:, side] = full[tok:]


def project_kernel(
    frames_ref, left_ref, right_ref, weights_hbm, teacher_hbm,
    student_ref, teacher_ref, side_student_ref, side_teacher_ref, wout_ref,
    window_scr, teach_scr, sems,
):
    tok, width = frames_ref.shape
    mats, cols = teach_scr.shape[:2]
    at = pl.multiple_of(lax.axis_index("copy") * cols // LANES * LANES, LANES)
    copies = []
    for m in range(mats):
        window = weights_hbm.at[pl.ds(m * width, width), pl.ds(at, window_scr.shape[2])]
        copies.append(pltpu.make_async_copy(teacher_hbm.at[m], teach_scr.at[m], sems.at[2 * m]))
        copies.append(pltpu.make_async_copy(window, window_scr.at[m], sems.at[2 * m + 1]))
    out = weights_hbm.at[pl.ds(mats * width, width), :]
    copies.append(pltpu.make_async_copy(out, wout_ref, sems.at[2 * mats]))
    for copy in copies:
        copy.start()
    own = frames_ref[...]
    rows = jnp.concatenate([own, left_ref[...], right_ref[...]], axis=0)
    for m in range(mats):
        copies[2 * m].wait()
        copies[2 * m + 1].wait()
        project_part(
            rows if m else own, window_scr[m], teach_scr[m],
            student_ref, teacher_ref, side_student_ref, side_teacher_ref, m,
        )
    copies[2 * mats].wait()


def teacher_heads(own_ref, side_ref, reach_ref):
    rows = own_ref.shape[0]
    wide = own_ref.shape[1] // 3
    spans = reach_ref.shape[0]
    reach = [reach_ref[n : n + 1, :] for n in range(spans)]
    column = jnp.concatenate([column_of(reach[n]) for n in (2, 3)], axis=0)
    allowed = jnp.concatenate([column] * spans, axis=1) == jnp.concatenate(reach, axis=1)
    parts = []
    for h in range(wide // LANES):
        sl = slice(h * LANES, (h + 1) * LANES)
        sk = slice(wide + h * LANES, wide + (h + 1) * LANES)
        sv = slice(2 * wide + h * LANES, 2 * wide + (h + 1) * LANES)
        keys = jnp.concatenate([side_ref[:rows, sl], own_ref[:, sk], side_ref[rows:, sl]], axis=0)
        vals = jnp.concatenate([side_ref[:rows, sk], own_ref[:, sv], side_ref[rows:, sk]], axis=0)
        probs = softmax_rows(dot_nt(own_ref[:, sl], keys) * score_scale, allowed).astype(bf16)
        parts.append(dot(probs, vals).astype(bf16)[:, :HEAD_DIM])
    attn = jnp.concatenate(parts, axis=1)
    return jnp.concatenate([attn[: rows // 2], attn[rows // 2 :]], axis=1)


def targets_kernel(a0, a1, a2, a3, mine_ref, other_ref, frames_ref, out_ref, attn_scr):
    groups = len((a0, a1, a2, a3))
    cols = a0.shape[2] // 2
    part = cols // 2
    even = lax.rem(lax.axis_index("seq"), CORES) == 0
    place = lax.axis_index("copy")
    for k, ref in enumerate((a0, a1, a2, a3)):
        attn_scr[lax.rem(place + k, groups)] = ref[0]
    low, high = [], []
    for g in range(groups):
        block = attn_scr[g]
        rows = jnp.concatenate([block[:, :cols], block[:, cols:]], axis=0)
        low.append(rows[:, :part])
        high.append(rows[:, part:])
    low, high = jnp.concatenate(low, axis=1), jnp.concatenate(high, axis=1)
    depth, width = groups * part, mine_ref.shape[-1]
    mine = mine_ref[...].reshape(depth, width)
    other = other_ref[...].reshape(depth, width)
    lhs_mine = jnp.where(even, low, high)
    lhs_other = jnp.where(even, high, low)
    wide_frames = frames_ref[...].astype(f32)
    mixing = dot(lhs_mine, mine) + dot(lhs_other, other)
    out_ref[...] = layer_norm(0.5 * (wide_frames + layer_norm(wide_frames + mixing))).astype(bf16)


def marks_kernel(lengths_ref, counts_ref, lists_ref, marks_ref, reach_ref, *, tok, blocks):
    seq = lax.axis_index("seq")
    copies, _, slots = lists_ref.shape
    lane = lax.broadcasted_iota(jnp.int32, (1, slots), 1)
    picks, places = [], []
    for c in range(copies):
        for j in range(3):
            near = seq - 1 + j
            block = jnp.clip(near, 0, blocks - 1)
            row = lists_ref[c, pl.ds(block, 1), :]
            count = jnp.where(near == block, counts_ref[c, block], 0)
            live = lane < count
            picks.append(jnp.where(live, row, -1))
            places.append(jnp.where(live, near * tok + row, -1))
    spans = reach_ref.shape[0]
    for n in range(spans):
        place = (seq - 1) * tok + n * slots + lane
        places.append(jnp.where((place >= 0) & (place < blocks * tok), place, -1))
    places = jnp.concatenate(places, axis=0)

    def passed(u, carry):
        end, utt = carry
        end = end + lengths_ref[u]
        return end, utt + jnp.where(end <= places, 1, 0)

    start = (jnp.int32(0), jnp.zeros(places.shape, jnp.int32))
    _, utt = lax.fori_loop(0, lengths_ref.shape[0], passed, start, unroll=8)
    utt = jnp.where(places >= 0, utt, -1)
    for c in range(copies):
        for j in range(3):
            n = 3 * c + j
            marks_ref[c, 0, j : j + 1, :] = picks[n]
            marks_ref[c, 1, j : j + 1, :] = utt[n : n + 1, :]
    reach_ref[...] = utt[3 * copies :, :]


def forward_first_kernel(
    own_ref, side_ref, town_ref, tside_ref, reach_ref, m0, m1, m2, m3,
    attn_ref, prob_ref, query_ref, kv_ref, pick_ref, utt_ref,
):
    place = lax.axis_index("copy")
    marks = (m0, m1, m2, m3)
    here = m0.shape[0]
    for k, ref in enumerate(marks):
        group = lax.rem(place + k, len(marks))
        for c in range(here):
            pick_ref[group * here + c] = ref[c, 0]
            utt_ref[group * here + c] = ref[c, 1]
    attn_ref[0] = teacher_heads(town_ref, tside_ref, reach_ref)
    forward_copies(
        own_ref, side_ref, pick_ref, utt_ref, attn_ref, prob_ref, query_ref, kv_ref, 0, 1
    )


def forward_middle_kernel(own_ref, side_ref, pick_ref, utt_ref, *outs, base):
    forward_copies(own_ref, side_ref, pick_ref, utt_ref, *outs, base, 0)


def forward_last_kernel(
    own_ref, side_ref, pick_ref, utt_ref, left_ref, frames_ref, right_ref,
    attn_ref, prob_ref, query_ref, kv_ref, turned_ref, *, base,
):
    forward_copies(
        own_ref, side_ref, pick_ref, utt_ref, attn_ref, prob_ref, query_ref, kv_ref, base, 0
    )
    tok = frames_ref.shape[0]
    for j, ref in enumerate((left_ref, frames_ref, right_ref)):
        turned_ref[:, j * tok : (j + 1) * tok] = jnp.transpose(ref[...])


def forward_copies(
    own_ref, side_ref, pick_ref, utt_ref, attn_ref, prob_ref, query_ref, kv_ref, base, lead
):
    tok = own_ref.shape[0]
    wide = own_ref.shape[1] // 3
    members, pairs = prob_ref.shape[:2]
    slots = pick_ref.shape[2]
    tables = [side_ref[:tok, :], own_ref[:, wide:], side_ref[tok:, :]]
    for j in range(3):
        pick = jnp.concatenate(
            [select_rows(pick_ref[base + c, j : j + 1, :], tok) for c in range(members)], axis=0
        )
        kv = dot(pick, tables[j]).astype(bf16)
        for c in range(members):
            kv_ref[c, j * slots : (j + 1) * slots, :] = kv[c * slots : (c + 1) * slots]
        if j == 1:
            query = dot(pick, own_ref[:, :wide]).astype(bf16)
            for c in range(members):
                query_ref[c] = query[c * slots : (c + 1) * slots]
    for c in range(members):
        utt = utt_ref[base + c]
        utt_row = jnp.concatenate([utt[j : j + 1, :] for j in range(3)], axis=1)
        utt_col = column_of(utt[1:2, :])
        allowed = jnp.concatenate([utt_col] * 3, axis=1) == utt_row
        allowed = jnp.concatenate([allowed, allowed], axis=0)
        parts = []
        for p in range(pairs):
            sl = slice(2 * p * LANES, 2 * (p + 1) * LANES)
            sv = slice(wide + 2 * p * LANES, wide + 2 * (p + 1) * LANES)
            scores = dot_nt(split_pair(query_ref[c, :, sl]), kv_ref[c, :, sl]) * score_scale
            probs = softmax_rows(scores, allowed)
            prob_ref[c, p] = probs
            parts.append(join_pair(dot(probs.astype(bf16), kv_ref[c, :, sv]).astype(bf16)))
        attn = narrow_heads(jnp.concatenate(parts, axis=1))
        cols = attn.shape[1]
        half = c % 2
        attn_ref[lead + c // 2, :, half * cols : (half + 1) * cols] = attn


def backward_kernel(
    a0, a1, a2, a3, wout_ref, frames_ref, goal_ref, pick_ref, prob_ref, query_ref, kv_ref,
    full_ref, ng_ref, dq_ref, dkv_ref, stack_scr, sum_scr, goal_scr, grad_scr, ag_scr,
    *, base, coef, skip,
):
    members, pairs = prob_ref.shape[:2]
    slots, wide = query_ref.shape[1:]
    tok, width = frames_ref.shape
    groups = stack_scr.shape[0]
    cols = a0.shape[2] // 2
    place = lax.axis_index("copy")
    for k, ref in enumerate((a0, a1, a2, a3)):
        stack_scr[lax.rem(place + k, groups)] = ref[skip:]
    for g in range(groups):
        for m in range(members):
            half = m % 2
            full_ref[m * slots : (m + 1) * slots, g * cols : (g + 1) * cols] = stack_scr[
                g, m // 2, :, half * cols : (half + 1) * cols
            ]
    pick = jnp.concatenate(
        [select_rows(pick_ref[base + m, 1:2, :], tok) for m in range(members)], axis=0
    )
    goal_scr[...] = dot(pick, goal_ref[...])
    sum_scr[...] = dot(pick, frames_ref[...])
    sum_scr[...] += dot(full_ref[...], wout_ref[...])
    block = 32

    def norm_rows(n, carry):
        here = pl.ds(pl.multiple_of(n * block, block), block)
        summed = sum_scr[here, :]
        centre = summed - jnp.mean(summed, axis=-1, keepdims=True)
        factor = lax.rsqrt(jnp.mean(centre * centre, axis=-1, keepdims=True) + norm_eps)
        normed = centre * factor
        upstream = (normed - goal_scr[here, :]) * coef
        part = upstream - jnp.mean(upstream, axis=-1, keepdims=True)
        part = part - normed * jnp.mean(upstream * normed, axis=-1, keepdims=True)
        grad_scr[here, :] = (part * factor).astype(bf16)
        return carry

    lax.fori_loop(0, members * slots // block, norm_rows, 0, unroll=4)
    for m in range(members):
        rows = slice(m * slots, (m + 1) * slots)
        live = column_of(pick_ref[base + m, 1:2, :]) >= 0
        live = jnp.concatenate([live] * (width // LANES), axis=1)
        grad_scr[rows, :] = jnp.where(live, grad_scr[rows, :], jnp.zeros((), bf16))
    grad = grad_scr[...]
    for g in range(groups):
        @pl.when(place == g)
        def _():
            ng_ref[...] = grad_scr[:, g * cols : (g + 1) * cols]

    own_rows = wout_ref[pl.ds(pl.multiple_of(place * cols, LANES // 2), cols), :]
    ag_scr[...] = widen_heads(dot_nt(grad, own_rows).astype(bf16))
    for m in range(members):
        rows = slice(m * slots, (m + 1) * slots)
        for p in range(pairs):
            sl = slice(2 * p * LANES, 2 * (p + 1) * LANES)
            sv = slice(wide + 2 * p * LANES, wide + 2 * (p + 1) * LANES)
            probs = prob_ref[m, p]
            grads = split_pair(ag_scr[rows, sl])
            prob_grad = dot_nt(grads, kv_ref[m, :, sv])
            inner = jnp.sum(probs * prob_grad, axis=-1, keepdims=True)
            score_grad = (probs * (prob_grad - inner) * score_scale).astype(bf16)
            dq_ref[rows, sl] = join_pair(dot(score_grad, kv_ref[m, :, sl]).astype(bf16))
            dk = dot_tn(score_grad, split_pair(query_ref[m, :, sl])).astype(bf16)
            dv = dot_tn(probs.astype(bf16), grads).astype(bf16)
            for j in range(3):
                dkv_ref[j, rows, sl] = dk[j * slots : (j + 1) * slots]
                dkv_ref[j, rows, sv] = dv[j * slots : (j + 1) * slots]


def combine_kernel(pick_ref, turned_ref, *refs):
    chunks = len(CHUNKS)
    fulls, ngs, dqs, dkvs = (refs[n * chunks : (n + 1) * chunks] for n in range(4))
    away_ref, qk_ref, v_ref, go_ref = refs[4 * chunks :]
    slots = pick_ref.shape[2]
    tok = turned_ref.shape[3] // 3
    wide = dqs[0].shape[1]
    cols = go_ref.shape[3]
    keys, values, query = [], [], None
    for j in range(3):
        total, base = None, 0
        for dq_ref, dkv_ref in zip(dqs, dkvs):
            members = dq_ref.shape[0] // slots
            row = jnp.concatenate(
                [pick_ref[base + m, j : j + 1, :] for m in range(members)], axis=1
            )
            pick_t = select_rows_t(row, tok)
            term = dot(pick_t, dkv_ref[j])
            total = term if total is None else total + term
            if j == 1:
                term = dot(pick_t, dq_ref[...])
                query = term if query is None else query + term
            base += members
        keys.append(narrow_heads(total[:, :wide]))
        values.append(narrow_heads(total[:, wide:]))
    query = narrow_heads(query)
    keys, values = jnp.concatenate(keys, axis=0), jnp.concatenate(values, axis=0)
    out = None
    for full_ref, ng_ref in zip(fulls, ngs):
        term = dot_tn(full_ref[...], ng_ref[...])
        out = term if out is None else out + term
    gap = jnp.zeros((tok, cols), f32)
    both = jnp.concatenate([jnp.concatenate([gap, query, gap], axis=0), keys], axis=1)
    for ref, whole in ((qk_ref, both), (v_ref, values)):
        wide_cols = whole.shape[1]
        top = whole.astype(bf16)
        ref[:, :wide_cols] = top
        ref[:, wide_cols:] = (whole - top.astype(f32)).astype(bf16)
    go_ref[...] = out.reshape(go_ref.shape)
    other = 1 - lax.rem(lax.axis_index("seq"), CORES)
    weight_rows(
        turned_ref[:, other], qk_ref[...], v_ref[...], lambda z: go_ref[z, other], away_ref
    )


def weight_rows(turned, qk, v, out_rows, out_ref):
    count, rows, reach = turned.shape
    cols = v.shape[1] // 2
    part = rows // 2
    lhs = turned.reshape(count * rows, reach)
    both = dot(lhs, qk)
    both = both[:, : 2 * cols] + both[:, 2 * cols :]
    value = dot(lhs, v)
    value = value[:, :cols] + value[:, cols:]
    for z in range(count):
        top = slice(z * rows, z * rows + part)
        low = slice(z * rows + part, (z + 1) * rows)
        last = out_rows(z)
        out_ref[z * part : (z + 1) * part, : 2 * cols] = both[top]
        out_ref[z * part : (z + 1) * part, 2 * cols : 3 * cols] = value[top]
        out_ref[z * part : (z + 1) * part, 3 * cols :] = last[:part]
        here = slice(z * cols, (z + 1) * cols)
        for m, full in enumerate((both[low, :cols], both[low, cols:], value[low], last[part:])):
            at = (count + m) * part
            out_ref[at : at + part, here] = full


def weights_kernel(turned_ref, qk_ref, v_ref, go_ref, out_ref):
    half = lax.rem(lax.axis_index("seq"), CORES)
    weight_rows(turned_ref[:, half], qk_ref[...], v_ref[...], lambda z: go_ref[z, half], out_ref)


def torus_place():
    seq = lax.axis_index("seq")
    return lax.rem(seq // CORES, RING), seq // (CORES * RING), lax.axis_index("copy")


def pack_rows(value):
    half = value.shape[1] // 2
    top = jnp.max(jnp.abs(value), axis=1, keepdims=True)
    code = jnp.ceil(jnp.log2(jnp.maximum(top, 1e-30)) * CODES).astype(jnp.int32)
    counts = jnp.round(value * (1.0 / row_step(code))).astype(jnp.int32)
    packed = (counts[:, :half] << 16) | (counts[:, half:] & 0xFFFF)
    return jnp.concatenate([packed, jnp.broadcast_to(code, (value.shape[0], LANES))], axis=1)


def row_step(code):
    return jnp.exp2(code.astype(f32) * (1.0 / CODES)) * (1.0 / 32000.0)


def unpack_rows(packed):
    half = packed.shape[1] - LANES
    step = row_step(packed[:, half : half + 1])
    pairs = packed[:, :half]
    high = (pairs >> 16).astype(f32) * step
    low = ((pairs << 16) >> 16).astype(f32) * step
    return jnp.concatenate([high, low], axis=1)


def first_pieces_kernel(kept_ref, arrived_ref, *refs):
    outs, scr = refs[:-1], refs[-1]
    scr[...] = kept_ref[...] + arrived_ref[...]
    spot = torus_place()
    rows = outs[0].shape[0]
    count = len(outs) // 2
    for n in range(2):
        for k in range(count):
            at = n * count + lax.rem(spot[n] + k, count)
            piece = scr[pl.ds(pl.multiple_of(at * rows, 8), rows), :]
            outs[n * count + k][...] = pack_rows(piece) if k else piece


def second_pieces_kernel(*refs):
    count = 4
    ins, outs, scr = refs[: 2 * count], refs[2 * count : 4 * count], refs[4 * count]
    rows, wide = outs[0].shape
    cols = wide // 2
    spot = torus_place()
    for n in range(2):
        total = ins[n * count][...]
        for k in range(1, count):
            total = total + unpack_rows(ins[n * count + k][...])
        for m in range(count):
            for x in range(2):
                scr[m, :, x * cols : (x + 1) * cols] = total[
                    x * rows : (x + 1) * rows, m * cols : (m + 1) * cols
                ]
        for k in range(count):
            outs[n * count + k][...] = scr[lax.rem(spot[1 - n] + k, count)]


def third_pieces_kernel(*refs):
    count = 4
    ins, outs, scr = refs[: 2 * count], refs[2 * count : 3 * count], refs[3 * count]
    cols = outs[0].shape[1]
    for n in range(2):
        total = ins[n * count][...]
        for k in range(1, count):
            total = total + ins[n * count + k][...]
        for x in range(2):
            scr[2 * n + x] = total[:, x * cols : (x + 1) * cols]
    for k in range(count):
        outs[k][...] = scr[lax.rem(torus_place()[2] + k, count)]


def last_pieces_kernel(*refs):
    ins, out_ref, scr = refs[:4], refs[4], refs[5]
    count = len(ins)
    cols = ins[0].shape[1]
    for k, ref in enumerate(ins):
        scr[lax.rem(torus_place()[2] - k + count, count)] = ref[...]
    for g in range(count):
        out_ref[:, g * cols : (g + 1) * cols] = scr[g]


def small_call(kernel, outs, scratch, name, parts):
    return pl.pallas_call(
        kernel,
        in_specs=[VMEM] * len(parts),
        out_specs=[VMEM] * len(outs),
        out_shape=outs,
        scratch_shapes=[pltpu.VMEM(scratch, f32)],
        compiler_params=params(16),
        name=name,
    )(*parts)


def per_device(
    frames, utt_lengths, vis_frames, vis_count, teacher_qkv, teacher_out, student_weights
):
    tok, width = frames.shape
    seq, seq_count = lax.axis_index("seq"), lax.axis_size("seq")
    place, groups = lax.axis_index("copy"), lax.axis_size("copy")
    cols = teacher_out.shape[0]
    heads = cols // HEAD_DIM
    wide = heads * LANES
    here = vis_frames.shape[0]
    copies = here * groups
    slots = vis_frames.shape[2]
    core = lax.rem(seq, CORES)
    swap = [(n, n ^ 1) for n in range(seq_count)]

    up = [(n, n + 1) for n in range(seq_count - 1)]
    left = lax.ppermute(frames, "seq", up)
    right = lax.ppermute(frames, "seq", [(j, n) for n, j in up])

    def from_group(value):
        spread = lambda k: [(n, (n - k) % groups) for n in range(groups)]
        return [value] + [lax.ppermute(value, "copy", spread(k)) for k in (2, 1, 3)]

    def by_turn(parts):
        return [parts[0], parts[2], parts[1], parts[3]]

    marks, reach = pl.pallas_call(
        functools.partial(marks_kernel, tok=tok, blocks=seq_count),
        in_specs=[SMEM, SMEM, VMEM],
        out_specs=[VMEM, VMEM],
        out_shape=[
            jax.ShapeDtypeStruct((here, 2, 3, slots), jnp.int32),
            jax.ShapeDtypeStruct((3 * tok // slots, slots), jnp.int32),
        ],
        compiler_params=params(8),
        cost_estimate=estimate(8),
        name="visible_marks",
    )(utt_lengths, vis_count, vis_frames)
    marks = by_turn(from_group(marks))

    half_rows = cols // CORES
    out_mine = lax.all_gather(
        lax.dynamic_slice_in_dim(teacher_out, core * half_rows, half_rows, 0), "copy", axis=0
    )

    teacher_in = jnp.swapaxes(teacher_qkv, 1, 2)
    own_out = jax.ShapeDtypeStruct((tok, 3 * wide), bf16)
    own_student, own_teacher, side_student, side_teacher, w_out = pl.pallas_call(
        project_kernel,
        in_specs=[VMEM] * 3 + [HBM] * 2,
        out_specs=[VMEM] * 5,
        out_shape=[own_out] * 2
        + [jax.ShapeDtypeStruct((2 * tok, 2 * wide), bf16)] * 2
        + [jax.ShapeDtypeStruct((width, width), bf16)],
        scratch_shapes=[
            pltpu.VMEM((3, width, 3 * LANES), bf16),
            pltpu.VMEM(teacher_in.shape, bf16),
            pltpu.SemaphoreType.DMA((7,)),
        ],
        compiler_params=params(OWN_MIB),
        cost_estimate=estimate(7),
        name="project_frames",
    )(frames, left, right, student_weights, teacher_in)

    saved, gathered = [], []
    prob_shape = (heads // 2, 2 * slots, 3 * slots)
    bases = [sum(CHUNKS[:n]) for n in range(len(CHUNKS))]
    for chunk, members in enumerate(CHUNKS):
        extra = 1 if chunk == 0 else 0
        ins = [own_student, side_student]
        out_shape = [
            jax.ShapeDtypeStruct((members // 2 + extra, slots, 2 * cols), bf16),
            jax.ShapeDtypeStruct((members,) + prob_shape, f32),
            jax.ShapeDtypeStruct((members, slots, wide), bf16),
            jax.ShapeDtypeStruct((members, 3 * slots, 2 * wide), bf16),
        ]
        if chunk == 0:
            kernel = forward_first_kernel
            ins += [own_teacher, side_teacher, reach, *marks]
            out_shape += [jax.ShapeDtypeStruct((copies, 3, slots), jnp.int32)] * 2
        elif chunk < len(CHUNKS) - 1:
            kernel = functools.partial(forward_middle_kernel, base=bases[chunk])
            ins += [picks, utts]
        else:
            kernel = functools.partial(forward_last_kernel, base=bases[chunk])
            ins += [picks, utts, left, frames, right]
            out_shape.append(jax.ShapeDtypeStruct((width, 3 * tok), bf16))
        attn, probs, query, kv, *rest = pl.pallas_call(
            kernel,
            in_specs=[VMEM] * len(ins),
            out_specs=[VMEM] * len(out_shape),
            out_shape=out_shape,
            compiler_params=params(FORWARD_MIB),
            cost_estimate=estimate(2.5 * extra + 0.9 * members),
            name=f"student_forward{chunk}",
        )(*ins)
        gathered.append(by_turn(from_group(attn)))
        saved.append((probs, query, kv))
        if chunk == len(CHUNKS) - 1:
            turned = rest[0]
        if chunk == 0:
            picks, utts = rest
            out_late, _ = lax.optimization_barrier((out_mine, attn))
            out_other = lax.ppermute(out_late, "seq", swap)

    targets = pl.pallas_call(
        targets_kernel,
        in_specs=[VMEM] * 7,
        out_specs=VMEM,
        out_shape=jax.ShapeDtypeStruct((tok, width), bf16),
        scratch_shapes=[pltpu.VMEM((groups, tok // 2, 2 * cols), bf16)],
        compiler_params=params(20),
        cost_estimate=estimate(2.5),
        name="teacher_targets",
    )(*gathered[0], out_mine, out_other, frames)

    coef = 2.0 / (width**0.5 * copies)
    results = []
    for chunk, members in enumerate(CHUNKS):
        rows = members * slots
        probs, query, kv = saved[chunk]
        results.append(
            pl.pallas_call(
                functools.partial(
                    backward_kernel, base=bases[chunk], coef=coef, skip=1 - min(chunk, 1)
                ),
                in_specs=[VMEM] * 11,
                out_specs=[VMEM] * 4,
                out_shape=[
                    jax.ShapeDtypeStruct((rows, width), bf16),
                    jax.ShapeDtypeStruct((rows, cols), bf16),
                    jax.ShapeDtypeStruct((rows, wide), bf16),
                    jax.ShapeDtypeStruct((3, rows, 2 * wide), bf16),
                ],
                scratch_shapes=[
                    pltpu.VMEM((groups, members // 2, slots, 2 * cols), bf16),
                    pltpu.VMEM((rows, width), f32),
                    pltpu.VMEM((rows, width), f32),
                    pltpu.VMEM((rows, width), bf16),
                    pltpu.VMEM((rows, wide), bf16),
                ],
                compiler_params=params(BACKWARD_MIB),
                cost_estimate=estimate(2.7 * members),
                name=f"student_backward{chunk}",
            )(*gathered[chunk], w_out, frames, targets, picks, probs, query, kv)
        )
    turned = turned.reshape(RING, CORES, width // RING // CORES, 3 * tok)
    carried = pl.pallas_call(
        combine_kernel,
        in_specs=[VMEM] * (2 + 4 * len(CHUNKS)),
        out_specs=[VMEM] * 4,
        out_shape=[
            jax.ShapeDtypeStruct((width // CORES, 4 * cols), f32),
            jax.ShapeDtypeStruct((3 * tok, 4 * cols), bf16),
            jax.ShapeDtypeStruct((3 * tok, 2 * cols), bf16),
            jax.ShapeDtypeStruct((RING, CORES, width // RING // CORES, cols), f32),
        ],
        compiler_params=params(COMBINE_MIB),
        cost_estimate=estimate(6),
        name="combine_terms",
    )(picks, turned, *[part[n] for n in range(4) for part in results])

    away, *kept_ins = carried
    arrived = lax.ppermute(away, "seq", swap)
    kept = pl.pallas_call(
        weights_kernel,
        in_specs=[VMEM] * 4,
        out_specs=VMEM,
        out_shape=jax.ShapeDtypeStruct(away.shape, f32),
        compiler_params=params(KEPT_MIB),
        cost_estimate=estimate(2.5),
        name="weights_kept",
    )(turned, *kept_ins)

    ring = RING
    span = CORES * ring

    def z_pairs(k):
        return [
            (n, n // span * span + ((n // CORES + k) % ring) * CORES + n % CORES)
            for n in range(seq_count)
        ]

    def y_pairs(k):
        return [(n, (n + k * span) % seq_count) for n in range(seq_count)]

    def exchange(pieces, firsts, seconds):
        order = (2, 1, 3)
        lead = [lax.ppermute(pieces[k], "seq", firsts(k)) for k in order]
        rest = [lax.ppermute(pieces[ring + k], "seq", seconds(k)) for k in order]
        return [pieces[0]] + lead + [pieces[ring]] + rest

    out_rows = width // seq_count
    sent = jax.ShapeDtypeStruct((2 * out_rows, 2 * cols + LANES), jnp.int32)
    shaped = lambda *shape: jax.ShapeDtypeStruct(shape, f32)
    outs = ([shaped(2 * out_rows, 4 * cols)] + [sent] * 3) * 2
    pieces = small_call(first_pieces_kernel, outs, kept.shape, "pieces1", [kept, arrived])
    pieces = exchange(pieces, z_pairs, y_pairs)
    pieces = small_call(
        second_pieces_kernel, [shaped(out_rows, 2 * cols)] * 8, (4, out_rows, 2 * cols), "pieces2", pieces
    )
    pieces = exchange(pieces, y_pairs, z_pairs)
    pieces = small_call(
        third_pieces_kernel, [shaped(out_rows, cols)] * 4, (4, out_rows, cols), "pieces3", pieces
    )
    forward = lambda k: [(n, (n + k) % groups) for n in range(groups)]
    pieces = [pieces[0]] + [lax.ppermute(pieces[k], "copy", forward(k)) for k in (1, 2, 3)]
    return small_call(
        last_pieces_kernel, [shaped(out_rows, 4 * cols)], (4, out_rows, cols), "pieces4", pieces
    )[0]


def solution(mesh):
    placed = (
        P("seq", None),
        P(),
        P("copy", None, None),
        P("copy", None),
        P(None, None, "copy"),
        P("copy", None),
        P(),
    )
    return jax.shard_map(
        per_device, mesh=mesh, in_specs=placed, out_specs=P(("seq", "copy"), None), check_vma=False
    )
```

```python
import functools

import jax
import jax.numpy as jnp
from jax import lax
from jax.experimental import pallas as pl
from jax.experimental.pallas import tpu as pltpu
from jax.sharding import PartitionSpec as P

HEADS = 16
HEAD_DIM = 80
LANES = 128
CHUNKS = (2, 4, 2)
CORES = 2
RING = 4
CODES = 256.0
OWN_MIB, FORWARD_MIB, BACKWARD_MIB, COMBINE_MIB, KEPT_MIB = 14, 10, 18, 18, 12

norm_eps = 1e-05
mask_fill = -1e30
score_scale = HEAD_DIM ** (-0.5)
bf16 = jnp.bfloat16
f32 = jnp.float32
VMEM = pl.BlockSpec(memory_space=pltpu.VMEM)
SMEM = pl.BlockSpec(memory_space=pltpu.SMEM)
HBM = pl.BlockSpec(memory_space=pltpu.HBM)


def dot(a, b):
    return lax.dot_general(a, b, (((1,), (0,)), ((), ())), preferred_element_type=f32)


def dot_nt(a, b):
    return lax.dot_general(a, b, (((1,), (1,)), ((), ())), preferred_element_type=f32)


def dot_tn(a, b):
    return lax.dot_general(a, b, (((0,), (0,)), ((), ())), preferred_element_type=f32)


def widen_heads(x):
    rows, cols = x.shape
    gap = jnp.zeros((rows, LANES - HEAD_DIM), x.dtype)
    parts = []
    for h in range(cols // HEAD_DIM):
        parts += [x[:, h * HEAD_DIM : (h + 1) * HEAD_DIM], gap]
    return jnp.concatenate(parts, axis=1)


def narrow_heads(x):
    return jnp.concatenate(
        [x[:, h * LANES : h * LANES + HEAD_DIM] for h in range(x.shape[1] // LANES)], axis=1
    )


def softmax_rows(scores, allowed):
    masked = jnp.where(allowed, scores, mask_fill)
    expo = jnp.exp(masked - jnp.max(masked, axis=-1, keepdims=True))
    return expo * (1.0 / jnp.sum(expo, axis=-1, keepdims=True))


def layer_norm(values):
    centre = values - jnp.mean(values, axis=-1, keepdims=True)
    spread = jnp.mean(centre * centre, axis=-1, keepdims=True)
    return centre * lax.rsqrt(spread + norm_eps)


def params(mib):
    return pltpu.CompilerParams(vmem_limit_bytes=mib << 20)


def estimate(micros):
    return pl.CostEstimate(flops=int(micros * 1e9), bytes_accessed=1 << 20, transcendentals=0)


def column_of(row):
    count = row.shape[1]
    return jnp.transpose(jnp.broadcast_to(row, (count, count)))


def select_rows(row, count):
    slots = row.shape[1]
    column = column_of(row)
    column = jnp.concatenate([column] * (count // slots), axis=1)
    return (lax.broadcasted_iota(jnp.int32, (slots, count), 1) == column).astype(bf16)


def select_rows_t(row, count):
    slots = row.shape[1]
    return (lax.broadcasted_iota(jnp.int32, (count, slots), 0) == row).astype(bf16)


def split_pair(x):
    gap = jnp.zeros((x.shape[0], LANES), x.dtype)
    top = jnp.concatenate([x[:, :LANES], gap], axis=1)
    low = jnp.concatenate([gap, x[:, LANES:]], axis=1)
    return jnp.concatenate([top, low], axis=0)


def join_pair(x):
    rows = x.shape[0] // 2
    return jnp.concatenate([x[:rows, :LANES], x[rows:, LANES:]], axis=1)


def project_part(rows, window, weights, student_ref, teacher_ref, side_ref, side_teacher_ref, n):
    cols = weights.shape[0]
    wide = cols // HEAD_DIM * LANES
    tok = student_ref.shape[0]
    here = slice(n * wide, (n + 1) * wide)
    side = slice((n - 1) * wide, n * wide)
    teacher = widen_heads(dot_nt(rows, weights).astype(bf16))
    teacher_ref[:, here] = teacher[:tok]
    if n:
        side_teacher_ref[:, side] = teacher[tok:]
    student = dot(rows, window).astype(bf16)
    shift = LANES // 2
    for odd in range(2):
        @pl.when(lax.rem(lax.axis_index("copy"), 2) == odd)
        def _():
            full = widen_heads(student[:, odd * shift : odd * shift + cols])
            student_ref[:, here] = full[:tok]
            if n:
                side_ref[:, side] = full[tok:]


def project_kernel(
    frames_ref, left_ref, right_ref, weights_hbm, teacher_hbm,
    student_ref, teacher_ref, side_student_ref, side_teacher_ref, wout_ref,
    window_scr, teach_scr, sems,
):
    tok, width = frames_ref.shape
    mats, cols = teach_scr.shape[:2]
    at = pl.multiple_of(lax.axis_index("copy") * cols // LANES * LANES, LANES)
    copies = []
    for m in range(mats):
        window = weights_hbm.at[pl.ds(m * width, width), pl.ds(at, window_scr.shape[2])]
        copies.append(pltpu.make_async_copy(teacher_hbm.at[m], teach_scr.at[m], sems.at[2 * m]))
        copies.append(pltpu.make_async_copy(window, window_scr.at[m], sems.at[2 * m + 1]))
    out = weights_hbm.at[pl.ds(mats * width, width), :]
    copies.append(pltpu.make_async_copy(out, wout_ref, sems.at[2 * mats]))
    for copy in copies:
        copy.start()
    own = frames_ref[...]
    rows = jnp.concatenate([own, left_ref[...], right_ref[...]], axis=0)
    for m in range(mats):
        copies[2 * m].wait()
        copies[2 * m + 1].wait()
        project_part(
            rows if m else own, window_scr[m], teach_scr[m],
            student_ref, teacher_ref, side_student_ref, side_teacher_ref, m,
        )
    copies[2 * mats].wait()


def teacher_heads(own_ref, side_ref, reach_ref):
    rows = own_ref.shape[0]
    wide = own_ref.shape[1] // 3
    spans = reach_ref.shape[0]
    reach = [reach_ref[n : n + 1, :] for n in range(spans)]
    column = jnp.concatenate([column_of(reach[n]) for n in (2, 3)], axis=0)
    allowed = jnp.concatenate([column] * spans, axis=1) == jnp.concatenate(reach, axis=1)
    parts = []
    for h in range(wide // LANES):
        sl = slice(h * LANES, (h + 1) * LANES)
        sk = slice(wide + h * LANES, wide + (h + 1) * LANES)
        sv = slice(2 * wide + h * LANES, 2 * wide + (h + 1) * LANES)
        keys = jnp.concatenate([side_ref[:rows, sl], own_ref[:, sk], side_ref[rows:, sl]], axis=0)
        vals = jnp.concatenate([side_ref[:rows, sk], own_ref[:, sv], side_ref[rows:, sk]], axis=0)
        probs = softmax_rows(dot_nt(own_ref[:, sl], keys) * score_scale, allowed).astype(bf16)
        parts.append(dot(probs, vals).astype(bf16)[:, :HEAD_DIM])
    attn = jnp.concatenate(parts, axis=1)
    return jnp.concatenate([attn[: rows // 2], attn[rows // 2 :]], axis=1)


def targets_kernel(a0, a1, a2, a3, mine_ref, other_ref, frames_ref, out_ref, attn_scr):
    groups = len((a0, a1, a2, a3))
    cols = a0.shape[2] // 2
    part = cols // 2
    even = lax.rem(lax.axis_index("seq"), CORES) == 0
    place = lax.axis_index("copy")
    for k, ref in enumerate((a0, a1, a2, a3)):
        attn_scr[lax.rem(place + k, groups)] = ref[0]
    low, high = [], []
    for g in range(groups):
        block = attn_scr[g]
        rows = jnp.concatenate([block[:, :cols], block[:, cols:]], axis=0)
        low.append(rows[:, :part])
        high.append(rows[:, part:])
    low, high = jnp.concatenate(low, axis=1), jnp.concatenate(high, axis=1)
    depth, width = groups * part, mine_ref.shape[-1]
    mine = mine_ref[...].reshape(depth, width)
    other = other_ref[...].reshape(depth, width)
    lhs_mine = jnp.where(even, low, high)
    lhs_other = jnp.where(even, high, low)
    wide_frames = frames_ref[...].astype(f32)
    mixing = dot(lhs_mine, mine) + dot(lhs_other, other)
    out_ref[...] = layer_norm(0.5 * (wide_frames + layer_norm(wide_frames + mixing))).astype(bf16)


def marks_kernel(lengths_ref, counts_ref, lists_ref, marks_ref, reach_ref, *, tok, blocks):
    seq = lax.axis_index("seq")
    copies, _, slots = lists_ref.shape
    lane = lax.broadcasted_iota(jnp.int32, (1, slots), 1)
    picks, places = [], []
    for c in range(copies):
        for j in range(3):
            near = seq - 1 + j
            block = jnp.clip(near, 0, blocks - 1)
            row = lists_ref[c, pl.ds(block, 1), :]
            count = jnp.where(near == block, counts_ref[c, block], 0)
            live = lane < count
            picks.append(jnp.where(live, row, -1))
            places.append(jnp.where(live, near * tok + row, -1))
    spans = reach_ref.shape[0]
    for n in range(spans):
        place = (seq - 1) * tok + n * slots + lane
        places.append(jnp.where((place >= 0) & (place < blocks * tok), place, -1))
    places = jnp.concatenate(places, axis=0)

    def passed(u, carry):
        end, utt = carry
        end = end + lengths_ref[u]
        return end, utt + jnp.where(end <= places, 1, 0)

    start = (jnp.int32(0), jnp.zeros(places.shape, jnp.int32))
    _, utt = lax.fori_loop(0, lengths_ref.shape[0], passed, start, unroll=8)
    utt = jnp.where(places >= 0, utt, -1)
    for c in range(copies):
        for j in range(3):
            n = 3 * c + j
            marks_ref[c, 0, j : j + 1, :] = picks[n]
            marks_ref[c, 1, j : j + 1, :] = utt[n : n + 1, :]
    reach_ref[...] = utt[3 * copies :, :]


def forward_first_kernel(
    own_ref, side_ref, town_ref, tside_ref, reach_ref, m0, m1, m2, m3,
    attn_ref, prob_ref, query_ref, kv_ref, pick_ref, utt_ref,
):
    place = lax.axis_index("copy")
    marks = (m0, m1, m2, m3)
    here = m0.shape[0]
    for k, ref in enumerate(marks):
        group = lax.rem(place + k, len(marks))
        for c in range(here):
            pick_ref[group * here + c] = ref[c, 0]
            utt_ref[group * here + c] = ref[c, 1]
    attn_ref[0] = teacher_heads(town_ref, tside_ref, reach_ref)
    forward_copies(
        own_ref, side_ref, pick_ref, utt_ref, attn_ref, prob_ref, query_ref, kv_ref, 0, 1
    )


def forward_middle_kernel(own_ref, side_ref, pick_ref, utt_ref, *outs, base):
    forward_copies(own_ref, side_ref, pick_ref, utt_ref, *outs, base, 0)


def forward_last_kernel(
    own_ref, side_ref, pick_ref, utt_ref, left_ref, frames_ref, right_ref,
    attn_ref, prob_ref, query_ref, kv_ref, turned_ref, *, base,
):
    forward_copies(
        own_ref, side_ref, pick_ref, utt_ref, attn_ref, prob_ref, query_ref, kv_ref, base, 0
    )
    tok = frames_ref.shape[0]
    for j, ref in enumerate((left_ref, frames_ref, right_ref)):
        turned_ref[:, j * tok : (j + 1) * tok] = jnp.transpose(ref[...])


def forward_copies(
    own_ref, side_ref, pick_ref, utt_ref, attn_ref, prob_ref, query_ref, kv_ref, base, lead
):
    tok = own_ref.shape[0]
    wide = own_ref.shape[1] // 3
    members, pairs = prob_ref.shape[:2]
    slots = pick_ref.shape[2]
    tables = [side_ref[:tok, :], own_ref[:, wide:], side_ref[tok:, :]]
    for j in range(3):
        pick = jnp.concatenate(
            [select_rows(pick_ref[base + c, j : j + 1, :], tok) for c in range(members)], axis=0
        )
        kv = dot(pick, tables[j]).astype(bf16)
        for c in range(members):
            kv_ref[c, j * slots : (j + 1) * slots, :] = kv[c * slots : (c + 1) * slots]
        if j == 1:
            query = dot(pick, own_ref[:, :wide]).astype(bf16)
            for c in range(members):
                query_ref[c] = query[c * slots : (c + 1) * slots]
    for c in range(members):
        utt = utt_ref[base + c]
        utt_row = jnp.concatenate([utt[j : j + 1, :] for j in range(3)], axis=1)
        utt_col = column_of(utt[1:2, :])
        allowed = jnp.concatenate([utt_col] * 3, axis=1) == utt_row
        allowed = jnp.concatenate([allowed, allowed], axis=0)
        parts = []
        for p in range(pairs):
            sl = slice(2 * p * LANES, 2 * (p + 1) * LANES)
            sv = slice(wide + 2 * p * LANES, wide + 2 * (p + 1) * LANES)
            scores = dot_nt(split_pair(query_ref[c, :, sl]), kv_ref[c, :, sl]) * score_scale
            probs = softmax_rows(scores, allowed)
            prob_ref[c, p] = probs
            parts.append(join_pair(dot(probs.astype(bf16), kv_ref[c, :, sv]).astype(bf16)))
        attn = narrow_heads(jnp.concatenate(parts, axis=1))
        cols = attn.shape[1]
        half = c % 2
        attn_ref[lead + c // 2, :, half * cols : (half + 1) * cols] = attn


def backward_kernel(
    a0, a1, a2, a3, wout_ref, frames_ref, goal_ref, pick_ref, prob_ref, query_ref, kv_ref,
    full_ref, ng_ref, dq_ref, dkv_ref, stack_scr, sum_scr, goal_scr, grad_scr, ag_scr,
    *, base, coef, skip,
):
    members, pairs = prob_ref.shape[:2]
    slots, wide = query_ref.shape[1:]
    tok, width = frames_ref.shape
    groups = stack_scr.shape[0]
    cols = a0.shape[2] // 2
    place = lax.axis_index("copy")
    for k, ref in enumerate((a0, a1, a2, a3)):
        stack_scr[lax.rem(place + k, groups)] = ref[skip:]
    for g in range(groups):
        for m in range(members):
            half = m % 2
            full_ref[m * slots : (m + 1) * slots, g * cols : (g + 1) * cols] = stack_scr[
                g, m // 2, :, half * cols : (half + 1) * cols
            ]
    pick = jnp.concatenate(
        [select_rows(pick_ref[base + m, 1:2, :], tok) for m in range(members)], axis=0
    )
    goal_scr[...] = dot(pick, goal_ref[...])
    sum_scr[...] = dot(pick, frames_ref[...])
    sum_scr[...] += dot(full_ref[...], wout_ref[...])
    block = 32

    def norm_rows(n, carry):
        here = pl.ds(pl.multiple_of(n * block, block), block)
        summed = sum_scr[here, :]
        centre = summed - jnp.mean(summed, axis=-1, keepdims=True)
        factor = lax.rsqrt(jnp.mean(centre * centre, axis=-1, keepdims=True) + norm_eps)
        normed = centre * factor
        upstream = (normed - goal_scr[here, :]) * coef
        part = upstream - jnp.mean(upstream, axis=-1, keepdims=True)
        part = part - normed * jnp.mean(upstream * normed, axis=-1, keepdims=True)
        grad_scr[here, :] = (part * factor).astype(bf16)
        return carry

    lax.fori_loop(0, members * slots // block, norm_rows, 0, unroll=4)
    for m in range(members):
        rows = slice(m * slots, (m + 1) * slots)
        live = column_of(pick_ref[base + m, 1:2, :]) >= 0
        live = jnp.concatenate([live] * (width // LANES), axis=1)
        grad_scr[rows, :] = jnp.where(live, grad_scr[rows, :], jnp.zeros((), bf16))
    grad = grad_scr[...]
    for g in range(groups):
        @pl.when(place == g)
        def _():
            ng_ref[...] = grad_scr[:, g * cols : (g + 1) * cols]

    own_rows = wout_ref[pl.ds(pl.multiple_of(place * cols, LANES // 2), cols), :]
    ag_scr[...] = widen_heads(dot_nt(grad, own_rows).astype(bf16))
    for m in range(members):
        rows = slice(m * slots, (m + 1) * slots)
        for p in range(pairs):
            sl = slice(2 * p * LANES, 2 * (p + 1) * LANES)
            sv = slice(wide + 2 * p * LANES, wide + 2 * (p + 1) * LANES)
            probs = prob_ref[m, p]
            grads = split_pair(ag_scr[rows, sl])
            prob_grad = dot_nt(grads, kv_ref[m, :, sv])
            inner = jnp.sum(probs * prob_grad, axis=-1, keepdims=True)
            score_grad = (probs * (prob_grad - inner) * score_scale).astype(bf16)
            dq_ref[rows, sl] = join_pair(dot(score_grad, kv_ref[m, :, sl]).astype(bf16))
            dk = dot_tn(score_grad, split_pair(query_ref[m, :, sl])).astype(bf16)
            dv = dot_tn(probs.astype(bf16), grads).astype(bf16)
            for j in range(3):
                dkv_ref[j, rows, sl] = dk[j * slots : (j + 1) * slots]
                dkv_ref[j, rows, sv] = dv[j * slots : (j + 1) * slots]


def combine_kernel(pick_ref, turned_ref, *refs):
    chunks = len(CHUNKS)
    fulls, ngs, dqs, dkvs = (refs[n * chunks : (n + 1) * chunks] for n in range(4))
    away_ref, qk_ref, v_ref, go_ref = refs[4 * chunks :]
    slots = pick_ref.shape[2]
    tok = turned_ref.shape[3] // 3
    wide = dqs[0].shape[1]
    cols = go_ref.shape[3]
    keys, values, query = [], [], None
    for j in range(3):
        total, base = None, 0
        for dq_ref, dkv_ref in zip(dqs, dkvs):
            members = dq_ref.shape[0] // slots
            row = jnp.concatenate(
                [pick_ref[base + m, j : j + 1, :] for m in range(members)], axis=1
            )
            pick_t = select_rows_t(row, tok)
            term = dot(pick_t, dkv_ref[j])
            total = term if total is None else total + term
            if j == 1:
                term = dot(pick_t, dq_ref[...])
                query = term if query is None else query + term
            base += members
        keys.append(narrow_heads(total[:, :wide]))
        values.append(narrow_heads(total[:, wide:]))
    query = narrow_heads(query)
    keys, values = jnp.concatenate(keys, axis=0), jnp.concatenate(values, axis=0)
    out = None
    for full_ref, ng_ref in zip(fulls, ngs):
        term = dot_tn(full_ref[...], ng_ref[...])
        out = term if out is None else out + term
    gap = jnp.zeros((tok, cols), f32)
    both = jnp.concatenate([jnp.concatenate([gap, query, gap], axis=0), keys], axis=1)
    for ref, whole in ((qk_ref, both), (v_ref, values)):
        wide_cols = whole.shape[1]
        top = whole.astype(bf16)
        ref[:, :wide_cols] = top
        ref[:, wide_cols:] = (whole - top.astype(f32)).astype(bf16)
    go_ref[...] = out.reshape(go_ref.shape)
    other = 1 - lax.rem(lax.axis_index("seq"), CORES)
    weight_rows(
        turned_ref[:, other], qk_ref[...], v_ref[...], lambda z: go_ref[z, other], away_ref
    )


def weight_rows(turned, qk, v, out_rows, out_ref):
    count, rows, reach = turned.shape
    cols = v.shape[1] // 2
    part = rows // 2
    lhs = turned.reshape(count * rows, reach)
    both = dot(lhs, qk)
    both = both[:, : 2 * cols] + both[:, 2 * cols :]
    value = dot(lhs, v)
    value = value[:, :cols] + value[:, cols:]
    for z in range(count):
        top = slice(z * rows, z * rows + part)
        low = slice(z * rows + part, (z + 1) * rows)
        last = out_rows(z)
        out_ref[z * part : (z + 1) * part, : 2 * cols] = both[top]
        out_ref[z * part : (z + 1) * part, 2 * cols : 3 * cols] = value[top]
        out_ref[z * part : (z + 1) * part, 3 * cols :] = last[:part]
        here = slice(z * cols, (z + 1) * cols)
        for m, full in enumerate((both[low, :cols], both[low, cols:], value[low], last[part:])):
            at = (count + m) * part
            out_ref[at : at + part, here] = full


def weights_kernel(turned_ref, qk_ref, v_ref, go_ref, out_ref):
    half = lax.rem(lax.axis_index("seq"), CORES)
    weight_rows(turned_ref[:, half], qk_ref[...], v_ref[...], lambda z: go_ref[z, half], out_ref)


def torus_place():
    seq = lax.axis_index("seq")
    return lax.rem(seq // CORES, RING), seq // (CORES * RING), lax.axis_index("copy")


def pack_rows(value):
    half = value.shape[1] // 2
    top = jnp.max(jnp.abs(value), axis=1, keepdims=True)
    code = jnp.ceil(jnp.log2(jnp.maximum(top, 1e-30)) * CODES).astype(jnp.int32)
    counts = jnp.round(value * (1.0 / row_step(code))).astype(jnp.int32)
    packed = (counts[:, :half] << 16) | (counts[:, half:] & 0xFFFF)
    return jnp.concatenate([packed, jnp.broadcast_to(code, (value.shape[0], LANES))], axis=1)


def row_step(code):
    return jnp.exp2(code.astype(f32) * (1.0 / CODES)) * (1.0 / 32000.0)


def unpack_rows(packed):
    half = packed.shape[1] - LANES
    step = row_step(packed[:, half : half + 1])
    pairs = packed[:, :half]
    high = (pairs >> 16).astype(f32) * step
    low = ((pairs << 16) >> 16).astype(f32) * step
    return jnp.concatenate([high, low], axis=1)


def first_pieces_kernel(kept_ref, arrived_ref, *refs):
    outs, scr = refs[:-1], refs[-1]
    scr[...] = kept_ref[...] + arrived_ref[...]
    spot = torus_place()
    rows = outs[0].shape[0]
    count = len(outs) // 2
    for n in range(2):
        for k in range(count):
            at = n * count + lax.rem(spot[n] + k, count)
            piece = scr[pl.ds(pl.multiple_of(at * rows, 8), rows), :]
            outs[n * count + k][...] = pack_rows(piece) if k else piece


def second_pieces_kernel(*refs, axis):
    ins, outs, scr = refs[:4], refs[4:8], refs[8]
    count = len(outs)
    rows, wide = outs[0].shape
    cols = wide // 2
    total = ins[0][...]
    for ref in ins[1:]:
        total = total + unpack_rows(ref[...])
    for m in range(count):
        for x in range(2):
            scr[m, :, x * cols : (x + 1) * cols] = total[
                x * rows : (x + 1) * rows, m * cols : (m + 1) * cols
            ]
    for k in range(count):
        outs[k][...] = scr[lax.rem(torus_place()[axis] + k, count)]


def third_pieces_kernel(*refs):
    count = 4
    ins, outs, scr = refs[: 2 * count], refs[2 * count : 3 * count], refs[3 * count]
    cols = outs[0].shape[1]
    for n in range(2):
        total = ins[n * count][...]
        for k in range(1, count):
            total = total + ins[n * count + k][...]
        for x in range(2):
            scr[2 * n + x] = total[:, x * cols : (x + 1) * cols]
    for k in range(count):
        outs[k][...] = scr[lax.rem(torus_place()[2] + k, count)]


def last_pieces_kernel(*refs):
    ins, out_ref, scr = refs[:4], refs[4], refs[5]
    count = len(ins)
    cols = ins[0].shape[1]
    for k, ref in enumerate(ins):
        scr[lax.rem(torus_place()[2] - k + count, count)] = ref[...]
    for g in range(count):
        out_ref[:, g * cols : (g + 1) * cols] = scr[g]


def small_call(kernel, outs, scratch, name, parts):
    return pl.pallas_call(
        kernel,
        in_specs=[VMEM] * len(parts),
        out_specs=[VMEM] * len(outs),
        out_shape=outs,
        scratch_shapes=[pltpu.VMEM(scratch, f32)],
        compiler_params=params(16),
        name=name,
    )(*parts)


def per_device(
    frames, utt_lengths, vis_frames, vis_count, teacher_qkv, teacher_out, student_weights
):
    tok, width = frames.shape
    seq, seq_count = lax.axis_index("seq"), lax.axis_size("seq")
    place, groups = lax.axis_index("copy"), lax.axis_size("copy")
    cols = teacher_out.shape[0]
    heads = cols // HEAD_DIM
    wide = heads * LANES
    here = vis_frames.shape[0]
    copies = here * groups
    slots = vis_frames.shape[2]
    core = lax.rem(seq, CORES)
    swap = [(n, n ^ 1) for n in range(seq_count)]

    up = [(n, n + 1) for n in range(seq_count - 1)]
    left = lax.ppermute(frames, "seq", up)
    right = lax.ppermute(frames, "seq", [(j, n) for n, j in up])

    def from_group(value):
        spread = lambda k: [(n, (n - k) % groups) for n in range(groups)]
        return [value] + [lax.ppermute(value, "copy", spread(k)) for k in (2, 1, 3)]

    def by_turn(parts):
        return [parts[0], parts[2], parts[1], parts[3]]

    marks, reach = pl.pallas_call(
        functools.partial(marks_kernel, tok=tok, blocks=seq_count),
        in_specs=[SMEM, SMEM, VMEM],
        out_specs=[VMEM, VMEM],
        out_shape=[
            jax.ShapeDtypeStruct((here, 2, 3, slots), jnp.int32),
            jax.ShapeDtypeStruct((3 * tok // slots, slots), jnp.int32),
        ],
        compiler_params=params(8),
        cost_estimate=estimate(8),
        name="visible_marks",
    )(utt_lengths, vis_count, vis_frames)
    marks = by_turn(from_group(marks))

    half_rows = cols // CORES
    out_mine = lax.all_gather(
        lax.dynamic_slice_in_dim(teacher_out, core * half_rows, half_rows, 0), "copy", axis=0
    )

    teacher_in = jnp.swapaxes(teacher_qkv, 1, 2)
    own_out = jax.ShapeDtypeStruct((tok, 3 * wide), bf16)
    own_student, own_teacher, side_student, side_teacher, w_out = pl.pallas_call(
        project_kernel,
        in_specs=[VMEM] * 3 + [HBM] * 2,
        out_specs=[VMEM] * 5,
        out_shape=[own_out] * 2
        + [jax.ShapeDtypeStruct((2 * tok, 2 * wide), bf16)] * 2
        + [jax.ShapeDtypeStruct((width, width), bf16)],
        scratch_shapes=[
            pltpu.VMEM((3, width, 3 * LANES), bf16),
            pltpu.VMEM(teacher_in.shape, bf16),
            pltpu.SemaphoreType.DMA((7,)),
        ],
        compiler_params=params(OWN_MIB),
        cost_estimate=estimate(7),
        name="project_frames",
    )(frames, left, right, student_weights, teacher_in)

    saved, gathered = [], []
    prob_shape = (heads // 2, 2 * slots, 3 * slots)
    bases = [sum(CHUNKS[:n]) for n in range(len(CHUNKS))]
    for chunk, members in enumerate(CHUNKS):
        extra = 1 if chunk == 0 else 0
        ins = [own_student, side_student]
        out_shape = [
            jax.ShapeDtypeStruct((members // 2 + extra, slots, 2 * cols), bf16),
            jax.ShapeDtypeStruct((members,) + prob_shape, f32),
            jax.ShapeDtypeStruct((members, slots, wide), bf16),
            jax.ShapeDtypeStruct((members, 3 * slots, 2 * wide), bf16),
        ]
        if chunk == 0:
            kernel = forward_first_kernel
            ins += [own_teacher, side_teacher, reach, *marks]
            out_shape += [jax.ShapeDtypeStruct((copies, 3, slots), jnp.int32)] * 2
        elif chunk < len(CHUNKS) - 1:
            kernel = functools.partial(forward_middle_kernel, base=bases[chunk])
            ins += [picks, utts]
        else:
            kernel = functools.partial(forward_last_kernel, base=bases[chunk])
            last_picks, _ = lax.optimization_barrier((picks, attn))
            ins += [last_picks, utts, left, frames, right]
            out_shape.append(jax.ShapeDtypeStruct((width, 3 * tok), bf16))
        attn, probs, query, kv, *rest = pl.pallas_call(
            kernel,
            in_specs=[VMEM] * len(ins),
            out_specs=[VMEM] * len(out_shape),
            out_shape=out_shape,
            compiler_params=params(FORWARD_MIB),
            cost_estimate=estimate(2.5 * extra + 0.9 * members),
            name=f"student_forward{chunk}",
        )(*ins)
        gathered.append(by_turn(from_group(attn)))
        saved.append((probs, query, kv))
        if chunk == len(CHUNKS) - 1:
            turned = rest[0]
        if chunk == 0:
            picks, utts = rest
            out_late, _ = lax.optimization_barrier((out_mine, attn))
            out_other = lax.ppermute(out_late, "seq", swap)

    targets = pl.pallas_call(
        targets_kernel,
        in_specs=[VMEM] * 7,
        out_specs=VMEM,
        out_shape=jax.ShapeDtypeStruct((tok, width), bf16),
        scratch_shapes=[pltpu.VMEM((groups, tok // 2, 2 * cols), bf16)],
        compiler_params=params(20),
        cost_estimate=estimate(2.5),
        name="teacher_targets",
    )(*gathered[0], out_mine, out_other, frames)

    coef = 2.0 / (width**0.5 * copies)
    results = []
    for chunk, members in enumerate(CHUNKS):
        rows = members * slots
        probs, query, kv = saved[chunk]
        if chunk:
            targets, _ = lax.optimization_barrier((targets, results[-1][1]))
        results.append(
            pl.pallas_call(
                functools.partial(
                    backward_kernel, base=bases[chunk], coef=coef, skip=1 - min(chunk, 1)
                ),
                in_specs=[VMEM] * 11,
                out_specs=[VMEM] * 4,
                out_shape=[
                    jax.ShapeDtypeStruct((rows, width), bf16),
                    jax.ShapeDtypeStruct((rows, cols), bf16),
                    jax.ShapeDtypeStruct((rows, wide), bf16),
                    jax.ShapeDtypeStruct((3, rows, 2 * wide), bf16),
                ],
                scratch_shapes=[
                    pltpu.VMEM((groups, members // 2, slots, 2 * cols), bf16),
                    pltpu.VMEM((rows, width), f32),
                    pltpu.VMEM((rows, width), f32),
                    pltpu.VMEM((rows, width), bf16),
                    pltpu.VMEM((rows, wide), bf16),
                ],
                compiler_params=params(BACKWARD_MIB),
                cost_estimate=estimate(2.7 * members),
                name=f"student_backward{chunk}",
            )(*gathered[chunk], w_out, frames, targets, picks, probs, query, kv)
        )
    turned = turned.reshape(RING, CORES, width // RING // CORES, 3 * tok)
    carried = pl.pallas_call(
        combine_kernel,
        in_specs=[VMEM] * (2 + 4 * len(CHUNKS)),
        out_specs=[VMEM] * 4,
        out_shape=[
            jax.ShapeDtypeStruct((width // CORES, 4 * cols), f32),
            jax.ShapeDtypeStruct((3 * tok, 4 * cols), bf16),
            jax.ShapeDtypeStruct((3 * tok, 2 * cols), bf16),
            jax.ShapeDtypeStruct((RING, CORES, width // RING // CORES, cols), f32),
        ],
        compiler_params=params(COMBINE_MIB),
        cost_estimate=estimate(6),
        name="combine_terms",
    )(picks, turned, *[part[n] for n in range(4) for part in results])

    away, *kept_ins = carried
    arrived = lax.ppermute(away, "seq", swap)
    kept = pl.pallas_call(
        weights_kernel,
        in_specs=[VMEM] * 4,
        out_specs=VMEM,
        out_shape=jax.ShapeDtypeStruct(away.shape, f32),
        compiler_params=params(KEPT_MIB),
        cost_estimate=estimate(2.5),
        name="weights_kept",
    )(turned, *kept_ins)

    ring = RING
    span = CORES * ring

    def z_pairs(k):
        return [
            (n, n // span * span + ((n // CORES + k) % ring) * CORES + n % CORES)
            for n in range(seq_count)
        ]

    def y_pairs(k):
        return [(n, (n + k * span) % seq_count) for n in range(seq_count)]

    def exchange(pieces, pairs_of):
        return [pieces[0]] + [lax.ppermute(pieces[k], "seq", pairs_of(k)) for k in (2, 3, 1)]

    out_rows = width // seq_count
    shaped = lambda *shape: jax.ShapeDtypeStruct(shape, f32)
    sent = jax.ShapeDtypeStruct((2 * out_rows, 2 * cols + LANES), jnp.int32)
    outs = ([shaped(2 * out_rows, 4 * cols)] + [sent] * 3) * 2
    pieces = small_call(first_pieces_kernel, outs, kept.shape, "pieces1", [kept, arrived])
    chains = []
    for n, (first, second) in enumerate(((z_pairs, y_pairs), (y_pairs, z_pairs))):
        part = exchange(pieces[n * ring : (n + 1) * ring], first)
        part = small_call(
            functools.partial(second_pieces_kernel, axis=1 - n),
            [shaped(out_rows, 2 * cols)] * 4,
            (4, out_rows, 2 * cols),
            f"pieces2_{n}",
            part,
        )
        chains += exchange(part, second)
    pieces = chains
    pieces = small_call(
        third_pieces_kernel, [shaped(out_rows, cols)] * 4, (4, out_rows, cols), "pieces3", pieces
    )
    forward = lambda k: [(n, (n + k) % groups) for n in range(groups)]
    pieces = [pieces[0]] + [lax.ppermute(pieces[k], "copy", forward(k)) for k in (1, 2, 3)]
    return small_call(
        last_pieces_kernel, [shaped(out_rows, 4 * cols)], (4, out_rows, cols), "pieces4", pieces
    )[0]


def solution(mesh):
    placed = (
        P("seq", None),
        P(),
        P("copy", None, None),
        P("copy", None),
        P(None, None, "copy"),
        P("copy", None),
        P(),
    )
    return jax.shard_map(
        per_device, mesh=mesh, in_specs=placed, out_specs=P(("seq", "copy"), None), check_vma=False
    )
```

```python
import functools

import jax
import jax.numpy as jnp
from jax import lax
from jax.experimental import pallas as pl
from jax.experimental.pallas import tpu as pltpu
from jax.sharding import PartitionSpec as P

HEADS = 16
HEAD_DIM = 80
LANES = 128
CHUNKS = (2, 4, 2)
CORES = 2
RING = 4
CODES = 256.0
OWN_MIB, FORWARD_MIB, LAST_MIB, BACKWARD_MIB, COMBINE_MIB, KEPT_MIB = 14, 10, 34, 18, 18, 12

norm_eps = 1e-05
mask_fill = -1e30
score_scale = HEAD_DIM ** (-0.5)
bf16 = jnp.bfloat16
f32 = jnp.float32
VMEM = pl.BlockSpec(memory_space=pltpu.VMEM)
SMEM = pl.BlockSpec(memory_space=pltpu.SMEM)
HBM = pl.BlockSpec(memory_space=pltpu.HBM)


def dot(a, b):
    return lax.dot_general(a, b, (((1,), (0,)), ((), ())), preferred_element_type=f32)


def dot_nt(a, b):
    return lax.dot_general(a, b, (((1,), (1,)), ((), ())), preferred_element_type=f32)


def dot_tn(a, b):
    return lax.dot_general(a, b, (((0,), (0,)), ((), ())), preferred_element_type=f32)


def widen_heads(x):
    rows, cols = x.shape
    gap = jnp.zeros((rows, LANES - HEAD_DIM), x.dtype)
    parts = []
    for h in range(cols // HEAD_DIM):
        parts += [x[:, h * HEAD_DIM : (h + 1) * HEAD_DIM], gap]
    return jnp.concatenate(parts, axis=1)


def narrow_heads(x):
    return jnp.concatenate(
        [x[:, h * LANES : h * LANES + HEAD_DIM] for h in range(x.shape[1] // LANES)], axis=1
    )


def softmax_rows(scores, allowed):
    masked = jnp.where(allowed, scores, mask_fill)
    expo = jnp.exp(masked - jnp.max(masked, axis=-1, keepdims=True))
    return expo * (1.0 / jnp.sum(expo, axis=-1, keepdims=True))


def layer_norm(values):
    centre = values - jnp.mean(values, axis=-1, keepdims=True)
    spread = jnp.mean(centre * centre, axis=-1, keepdims=True)
    return centre * lax.rsqrt(spread + norm_eps)


def params(mib):
    return pltpu.CompilerParams(vmem_limit_bytes=mib << 20)


def estimate(micros):
    return pl.CostEstimate(flops=int(micros * 1e9), bytes_accessed=1 << 20, transcendentals=0)


def column_of(row):
    count = row.shape[1]
    return jnp.transpose(jnp.broadcast_to(row, (count, count)))


def select_rows(row, count):
    slots = row.shape[1]
    column = column_of(row)
    column = jnp.concatenate([column] * (count // slots), axis=1)
    return (lax.broadcasted_iota(jnp.int32, (slots, count), 1) == column).astype(bf16)


def select_rows_t(row, count):
    slots = row.shape[1]
    return (lax.broadcasted_iota(jnp.int32, (count, slots), 0) == row).astype(bf16)


def split_pair(x):
    gap = jnp.zeros((x.shape[0], LANES), x.dtype)
    top = jnp.concatenate([x[:, :LANES], gap], axis=1)
    low = jnp.concatenate([gap, x[:, LANES:]], axis=1)
    return jnp.concatenate([top, low], axis=0)


def join_pair(x):
    rows = x.shape[0] // 2
    return jnp.concatenate([x[:rows, :LANES], x[rows:, LANES:]], axis=1)


def project_part(rows, window, weights, student_ref, teacher_ref, side_ref, side_teacher_ref, n):
    cols = weights.shape[0]
    wide = cols // HEAD_DIM * LANES
    tok = student_ref.shape[0]
    here = slice(n * wide, (n + 1) * wide)
    side = slice((n - 1) * wide, n * wide)
    teacher = widen_heads(dot_nt(rows, weights).astype(bf16))
    teacher_ref[:, here] = teacher[:tok]
    if n:
        side_teacher_ref[:, side] = teacher[tok:]
    student = dot(rows, window).astype(bf16)
    shift = LANES // 2
    for odd in range(2):
        @pl.when(lax.rem(lax.axis_index("copy"), 2) == odd)
        def _():
            full = widen_heads(student[:, odd * shift : odd * shift + cols])
            student_ref[:, here] = full[:tok]
            if n:
                side_ref[:, side] = full[tok:]


def project_kernel(
    frames_ref, left_ref, right_ref, weights_hbm, teacher_hbm,
    student_ref, teacher_ref, side_student_ref, side_teacher_ref,
    window_scr, teach_scr, sems,
):
    tok, width = frames_ref.shape
    mats, cols = teach_scr.shape[:2]
    at = pl.multiple_of(lax.axis_index("copy") * cols // LANES * LANES, LANES)
    copies = []
    for m in range(mats):
        window = weights_hbm.at[pl.ds(m * width, width), pl.ds(at, window_scr.shape[2])]
        copies.append(pltpu.make_async_copy(teacher_hbm.at[m], teach_scr.at[m], sems.at[2 * m]))
        copies.append(pltpu.make_async_copy(window, window_scr.at[m], sems.at[2 * m + 1]))
    for copy in copies:
        copy.start()
    own = frames_ref[...]
    rows = jnp.concatenate([own, left_ref[...], right_ref[...]], axis=0)
    for m in range(mats):
        copies[2 * m].wait()
        copies[2 * m + 1].wait()
        project_part(
            rows if m else own, window_scr[m], teach_scr[m],
            student_ref, teacher_ref, side_student_ref, side_teacher_ref, m,
        )


def teacher_heads(own_ref, side_ref, reach_ref):
    rows = own_ref.shape[0]
    wide = own_ref.shape[1] // 3
    spans = reach_ref.shape[0]
    reach = [reach_ref[n : n + 1, :] for n in range(spans)]
    column = jnp.concatenate([column_of(reach[n]) for n in (2, 3)], axis=0)
    allowed = jnp.concatenate([column] * spans, axis=1) == jnp.concatenate(reach, axis=1)
    parts = []
    for h in range(wide // LANES):
        sl = slice(h * LANES, (h + 1) * LANES)
        sk = slice(wide + h * LANES, wide + (h + 1) * LANES)
        sv = slice(2 * wide + h * LANES, 2 * wide + (h + 1) * LANES)
        keys = jnp.concatenate([side_ref[:rows, sl], own_ref[:, sk], side_ref[rows:, sl]], axis=0)
        vals = jnp.concatenate([side_ref[:rows, sk], own_ref[:, sv], side_ref[rows:, sk]], axis=0)
        probs = softmax_rows(dot_nt(own_ref[:, sl], keys) * score_scale, allowed).astype(bf16)
        parts.append(dot(probs, vals).astype(bf16)[:, :HEAD_DIM])
    attn = jnp.concatenate(parts, axis=1)
    return jnp.concatenate([attn[: rows // 2], attn[rows // 2 :]], axis=1)


def targets_kernel(a0, a1, a2, a3, mine_ref, other_ref, frames_ref, out_ref, attn_scr):
    groups = len((a0, a1, a2, a3))
    cols = a0.shape[2] // 2
    part = cols // 2
    even = lax.rem(lax.axis_index("seq"), CORES) == 0
    place = lax.axis_index("copy")
    for k, ref in enumerate((a0, a1, a2, a3)):
        attn_scr[lax.rem(place + k, groups)] = ref[0]
    low, high = [], []
    for g in range(groups):
        block = attn_scr[g]
        rows = jnp.concatenate([block[:, :cols], block[:, cols:]], axis=0)
        low.append(rows[:, :part])
        high.append(rows[:, part:])
    low, high = jnp.concatenate(low, axis=1), jnp.concatenate(high, axis=1)
    depth, width = groups * part, mine_ref.shape[-1]
    mine = mine_ref[...].reshape(depth, width)
    other = other_ref[...].reshape(depth, width)
    lhs_mine = jnp.where(even, low, high)
    lhs_other = jnp.where(even, high, low)
    wide_frames = frames_ref[...].astype(f32)
    mixing = dot(lhs_mine, mine) + dot(lhs_other, other)
    out_ref[...] = layer_norm(0.5 * (wide_frames + layer_norm(wide_frames + mixing))).astype(bf16)


def marks_kernel(lengths_ref, counts_ref, lists_ref, marks_ref, reach_ref, *, tok, blocks):
    seq = lax.axis_index("seq")
    copies, _, slots = lists_ref.shape
    lane = lax.broadcasted_iota(jnp.int32, (1, slots), 1)
    picks, places = [], []
    for c in range(copies):
        for j in range(3):
            near = seq - 1 + j
            block = jnp.clip(near, 0, blocks - 1)
            row = lists_ref[c, pl.ds(block, 1), :]
            count = jnp.where(near == block, counts_ref[c, block], 0)
            live = lane < count
            picks.append(jnp.where(live, row, -1))
            places.append(jnp.where(live, near * tok + row, -1))
    spans = reach_ref.shape[0]
    for n in range(spans):
        place = (seq - 1) * tok + n * slots + lane
        places.append(jnp.where((place >= 0) & (place < blocks * tok), place, -1))
    places = jnp.concatenate(places, axis=0)

    def passed(u, carry):
        end, utt = carry
        end = end + lengths_ref[u]
        return end, utt + jnp.where(end <= places, 1, 0)

    start = (jnp.int32(0), jnp.zeros(places.shape, jnp.int32))
    _, utt = lax.fori_loop(0, lengths_ref.shape[0], passed, start, unroll=8)
    utt = jnp.where(places >= 0, utt, -1)
    for c in range(copies):
        for j in range(3):
            n = 3 * c + j
            marks_ref[c, 0, j : j + 1, :] = picks[n]
            marks_ref[c, 1, j : j + 1, :] = utt[n : n + 1, :]
    reach_ref[...] = utt[3 * copies :, :]


def forward_first_kernel(
    own_ref, side_ref, town_ref, tside_ref, reach_ref, m0, m1, m2, m3,
    attn_ref, prob_ref, query_ref, kv_ref, pick_ref, utt_ref,
):
    place = lax.axis_index("copy")
    marks = (m0, m1, m2, m3)
    here = m0.shape[0]
    for k, ref in enumerate(marks):
        group = lax.rem(place + k, len(marks))
        for c in range(here):
            pick_ref[group * here + c] = ref[c, 0]
            utt_ref[group * here + c] = ref[c, 1]
    attn_ref[0] = teacher_heads(town_ref, tside_ref, reach_ref)
    forward_copies(
        own_ref, side_ref, pick_ref, utt_ref, attn_ref, prob_ref, query_ref, kv_ref, 0, 1
    )


def forward_middle_kernel(own_ref, side_ref, pick_ref, utt_ref, *outs, base):
    forward_copies(own_ref, side_ref, pick_ref, utt_ref, *outs, base, 0)


def forward_last_kernel(
    own_ref, side_ref, pick_ref, utt_ref, left_ref, frames_ref, right_ref, weights_hbm,
    attn_ref, prob_ref, query_ref, kv_ref, turned_ref, wout_ref, sem, *, base,
):
    width = wout_ref.shape[0]
    take = pltpu.make_async_copy(weights_hbm.at[pl.ds(3 * width, width), :], wout_ref, sem)
    take.start()
    forward_copies(
        own_ref, side_ref, pick_ref, utt_ref, attn_ref, prob_ref, query_ref, kv_ref, base, 0
    )
    tok = frames_ref.shape[0]
    for j, ref in enumerate((left_ref, frames_ref, right_ref)):
        turned_ref[:, j * tok : (j + 1) * tok] = jnp.transpose(ref[...])
    take.wait()


def forward_copies(
    own_ref, side_ref, pick_ref, utt_ref, attn_ref, prob_ref, query_ref, kv_ref, base, lead
):
    tok = own_ref.shape[0]
    wide = own_ref.shape[1] // 3
    members, pairs = prob_ref.shape[:2]
    slots = pick_ref.shape[2]
    tables = [side_ref[:tok, :], own_ref[:, wide:], side_ref[tok:, :]]
    for j in range(3):
        pick = jnp.concatenate(
            [select_rows(pick_ref[base + c, j : j + 1, :], tok) for c in range(members)], axis=0
        )
        kv = dot(pick, tables[j]).astype(bf16)
        for c in range(members):
            kv_ref[c, j * slots : (j + 1) * slots, :] = kv[c * slots : (c + 1) * slots]
        if j == 1:
            query = dot(pick, own_ref[:, :wide]).astype(bf16)
            for c in range(members):
                query_ref[c] = query[c * slots : (c + 1) * slots]
    for c in range(members):
        utt = utt_ref[base + c]
        utt_row = jnp.concatenate([utt[j : j + 1, :] for j in range(3)], axis=1)
        utt_col = column_of(utt[1:2, :])
        allowed = jnp.concatenate([utt_col] * 3, axis=1) == utt_row
        allowed = jnp.concatenate([allowed, allowed], axis=0)
        parts = []
        for p in range(pairs):
            sl = slice(2 * p * LANES, 2 * (p + 1) * LANES)
            sv = slice(wide + 2 * p * LANES, wide + 2 * (p + 1) * LANES)
            scores = dot_nt(split_pair(query_ref[c, :, sl]), kv_ref[c, :, sl]) * score_scale
            probs = softmax_rows(scores, allowed)
            prob_ref[c, p] = probs
            parts.append(join_pair(dot(probs.astype(bf16), kv_ref[c, :, sv]).astype(bf16)))
        attn = narrow_heads(jnp.concatenate(parts, axis=1))
        cols = attn.shape[1]
        half = c % 2
        attn_ref[lead + c // 2, :, half * cols : (half + 1) * cols] = attn


def backward_kernel(
    a0, a1, a2, a3, wout_ref, frames_ref, goal_ref, pick_ref, prob_ref, query_ref, kv_ref,
    full_ref, ng_ref, dq_ref, dkv_ref, stack_scr, sum_scr, goal_scr, grad_scr, ag_scr,
    *, base, coef, skip,
):
    members, pairs = prob_ref.shape[:2]
    slots, wide = query_ref.shape[1:]
    tok, width = frames_ref.shape
    groups = stack_scr.shape[0]
    cols = a0.shape[2] // 2
    place = lax.axis_index("copy")
    for k, ref in enumerate((a0, a1, a2, a3)):
        stack_scr[lax.rem(place + k, groups)] = ref[skip:]
    for g in range(groups):
        for m in range(members):
            half = m % 2
            full_ref[m * slots : (m + 1) * slots, g * cols : (g + 1) * cols] = stack_scr[
                g, m // 2, :, half * cols : (half + 1) * cols
            ]
    pick = jnp.concatenate(
        [select_rows(pick_ref[base + m, 1:2, :], tok) for m in range(members)], axis=0
    )
    goal_scr[...] = dot(pick, goal_ref[...])
    sum_scr[...] = dot(pick, frames_ref[...])
    sum_scr[...] += dot(full_ref[...], wout_ref[...])
    block = 32

    def norm_rows(n, carry):
        here = pl.ds(pl.multiple_of(n * block, block), block)
        summed = sum_scr[here, :]
        centre = summed - jnp.mean(summed, axis=-1, keepdims=True)
        factor = lax.rsqrt(jnp.mean(centre * centre, axis=-1, keepdims=True) + norm_eps)
        normed = centre * factor
        upstream = (normed - goal_scr[here, :]) * coef
        part = upstream - jnp.mean(upstream, axis=-1, keepdims=True)
        part = part - normed * jnp.mean(upstream * normed, axis=-1, keepdims=True)
        grad_scr[here, :] = (part * factor).astype(bf16)
        return carry

    lax.fori_loop(0, members * slots // block, norm_rows, 0, unroll=4)
    for m in range(members):
        rows = slice(m * slots, (m + 1) * slots)
        live = column_of(pick_ref[base + m, 1:2, :]) >= 0
        live = jnp.concatenate([live] * (width // LANES), axis=1)
        grad_scr[rows, :] = jnp.where(live, grad_scr[rows, :], jnp.zeros((), bf16))
    grad = grad_scr[...]
    for g in range(groups):
        @pl.when(place == g)
        def _():
            ng_ref[...] = grad_scr[:, g * cols : (g + 1) * cols]

    own_rows = wout_ref[pl.ds(pl.multiple_of(place * cols, LANES // 2), cols), :]
    ag_scr[...] = widen_heads(dot_nt(grad, own_rows).astype(bf16))
    for m in range(members):
        rows = slice(m * slots, (m + 1) * slots)
        for p in range(pairs):
            sl = slice(2 * p * LANES, 2 * (p + 1) * LANES)
            sv = slice(wide + 2 * p * LANES, wide + 2 * (p + 1) * LANES)
            probs = prob_ref[m, p]
            grads = split_pair(ag_scr[rows, sl])
            prob_grad = dot_nt(grads, kv_ref[m, :, sv])
            inner = jnp.sum(probs * prob_grad, axis=-1, keepdims=True)
            score_grad = (probs * (prob_grad - inner) * score_scale).astype(bf16)
            dq_ref[rows, sl] = join_pair(dot(score_grad, kv_ref[m, :, sl]).astype(bf16))
            dk = dot_tn(score_grad, split_pair(query_ref[m, :, sl])).astype(bf16)
            dv = dot_tn(probs.astype(bf16), grads).astype(bf16)
            for j in range(3):
                dkv_ref[j, rows, sl] = dk[j * slots : (j + 1) * slots]
                dkv_ref[j, rows, sv] = dv[j * slots : (j + 1) * slots]


def combine_kernel(pick_ref, turned_ref, *refs):
    chunks = len(CHUNKS)
    fulls, ngs, dqs, dkvs = (refs[n * chunks : (n + 1) * chunks] for n in range(4))
    away_ref, qk_ref, v_ref, go_ref = refs[4 * chunks :]
    slots = pick_ref.shape[2]
    tok = turned_ref.shape[3] // 3
    wide = dqs[0].shape[1]
    cols = go_ref.shape[3]
    keys, values, query = [], [], None
    for j in range(3):
        total, base = None, 0
        for dq_ref, dkv_ref in zip(dqs, dkvs):
            members = dq_ref.shape[0] // slots
            row = jnp.concatenate(
                [pick_ref[base + m, j : j + 1, :] for m in range(members)], axis=1
            )
            pick_t = select_rows_t(row, tok)
            term = dot(pick_t, dkv_ref[j])
            total = term if total is None else total + term
            if j == 1:
                term = dot(pick_t, dq_ref[...])
                query = term if query is None else query + term
            base += members
        keys.append(narrow_heads(total[:, :wide]))
        values.append(narrow_heads(total[:, wide:]))
    query = narrow_heads(query)
    keys, values = jnp.concatenate(keys, axis=0), jnp.concatenate(values, axis=0)
    out = None
    for full_ref, ng_ref in zip(fulls, ngs):
        term = dot_tn(full_ref[...], ng_ref[...])
        out = term if out is None else out + term
    gap = jnp.zeros((tok, cols), f32)
    both = jnp.concatenate([jnp.concatenate([gap, query, gap], axis=0), keys], axis=1)
    for ref, whole in ((qk_ref, both), (v_ref, values)):
        wide_cols = whole.shape[1]
        top = whole.astype(bf16)
        ref[:, :wide_cols] = top
        ref[:, wide_cols:] = (whole - top.astype(f32)).astype(bf16)
    go_ref[...] = out.reshape(go_ref.shape)
    other = 1 - lax.rem(lax.axis_index("seq"), CORES)
    weight_rows(
        turned_ref[:, other], qk_ref[...], v_ref[...], lambda z: go_ref[z, other], away_ref
    )


def weight_rows(turned, qk, v, out_rows, out_ref):
    count, rows, reach = turned.shape
    cols = v.shape[1] // 2
    part = rows // 2
    lhs = turned.reshape(count * rows, reach)
    both = dot(lhs, qk)
    both = both[:, : 2 * cols] + both[:, 2 * cols :]
    value = dot(lhs, v)
    value = value[:, :cols] + value[:, cols:]
    for z in range(count):
        top = slice(z * rows, z * rows + part)
        low = slice(z * rows + part, (z + 1) * rows)
        last = out_rows(z)
        out_ref[z * part : (z + 1) * part, : 2 * cols] = both[top]
        out_ref[z * part : (z + 1) * part, 2 * cols : 3 * cols] = value[top]
        out_ref[z * part : (z + 1) * part, 3 * cols :] = last[:part]
        here = slice(z * cols, (z + 1) * cols)
        for m, full in enumerate((both[low, :cols], both[low, cols:], value[low], last[part:])):
            at = (count + m) * part
            out_ref[at : at + part, here] = full


def weights_kernel(turned_ref, qk_ref, v_ref, go_ref, out_ref):
    half = lax.rem(lax.axis_index("seq"), CORES)
    weight_rows(turned_ref[:, half], qk_ref[...], v_ref[...], lambda z: go_ref[z, half], out_ref)


def torus_place():
    seq = lax.axis_index("seq")
    return lax.rem(seq // CORES, RING), seq // (CORES * RING), lax.axis_index("copy")


def pack_rows(value):
    half = value.shape[1] // 2
    top = jnp.max(jnp.abs(value), axis=1, keepdims=True)
    code = jnp.ceil(jnp.log2(jnp.maximum(top, 1e-30)) * CODES).astype(jnp.int32)
    counts = jnp.round(value * (1.0 / row_step(code))).astype(jnp.int32)
    packed = (counts[:, :half] << 16) | (counts[:, half:] & 0xFFFF)
    return jnp.concatenate([packed, jnp.broadcast_to(code, (value.shape[0], LANES))], axis=1)


def row_step(code):
    return jnp.exp2(code.astype(f32) * (1.0 / CODES)) * (1.0 / 32000.0)


def unpack_rows(packed):
    half = packed.shape[1] - LANES
    step = row_step(packed[:, half : half + 1])
    pairs = packed[:, :half]
    high = (pairs >> 16).astype(f32) * step
    low = ((pairs << 16) >> 16).astype(f32) * step
    return jnp.concatenate([high, low], axis=1)


def first_pieces_kernel(kept_ref, arrived_ref, *refs):
    outs, scr = refs[:-1], refs[-1]
    scr[...] = kept_ref[...] + arrived_ref[...]
    spot = torus_place()
    rows = outs[0].shape[0]
    count = len(outs) // 2
    for n in range(2):
        for k in range(count):
            at = n * count + lax.rem(spot[n] + k, count)
            piece = scr[pl.ds(pl.multiple_of(at * rows, 8), rows), :]
            outs[n * count + k][...] = pack_rows(piece) if k else piece


def second_pieces_kernel(*refs, axis):
    ins, outs, scr = refs[:4], refs[4:8], refs[8]
    count = len(outs)
    rows, wide = outs[0].shape
    cols = wide // 2
    total = ins[0][...]
    for ref in ins[1:]:
        total = total + unpack_rows(ref[...])
    for m in range(count):
        for x in range(2):
            scr[m, :, x * cols : (x + 1) * cols] = total[
                x * rows : (x + 1) * rows, m * cols : (m + 1) * cols
            ]
    for k in range(count):
        outs[k][...] = scr[lax.rem(torus_place()[axis] + k, count)]


def third_pieces_kernel(*refs):
    count = 4
    ins, outs, scr = refs[: 2 * count], refs[2 * count : 3 * count], refs[3 * count]
    cols = outs[0].shape[1]
    for n in range(2):
        total = ins[n * count][...]
        for k in range(1, count):
            total = total + ins[n * count + k][...]
        for x in range(2):
            scr[2 * n + x] = total[:, x * cols : (x + 1) * cols]
    for k in range(count):
        outs[k][...] = scr[lax.rem(torus_place()[2] + k, count)]


def last_pieces_kernel(*refs):
    ins, out_ref, scr = refs[:4], refs[4], refs[5]
    count = len(ins)
    cols = ins[0].shape[1]
    for k, ref in enumerate(ins):
        scr[lax.rem(torus_place()[2] - k + count, count)] = ref[...]
    for g in range(count):
        out_ref[:, g * cols : (g + 1) * cols] = scr[g]


def small_call(kernel, outs, scratch, name, parts):
    return pl.pallas_call(
        kernel,
        in_specs=[VMEM] * len(parts),
        out_specs=[VMEM] * len(outs),
        out_shape=outs,
        scratch_shapes=[pltpu.VMEM(scratch, f32)],
        compiler_params=params(16),
        name=name,
    )(*parts)


def per_device(
    frames, utt_lengths, vis_frames, vis_count, teacher_qkv, teacher_out, student_weights
):
    tok, width = frames.shape
    seq, seq_count = lax.axis_index("seq"), lax.axis_size("seq")
    place, groups = lax.axis_index("copy"), lax.axis_size("copy")
    cols = teacher_out.shape[0]
    heads = cols // HEAD_DIM
    wide = heads * LANES
    here = vis_frames.shape[0]
    copies = here * groups
    slots = vis_frames.shape[2]
    core = lax.rem(seq, CORES)
    swap = [(n, n ^ 1) for n in range(seq_count)]

    up = [(n, n + 1) for n in range(seq_count - 1)]
    left = lax.ppermute(frames, "seq", up)
    right = lax.ppermute(frames, "seq", [(j, n) for n, j in up])

    def from_group(value):
        spread = lambda k: [(n, (n - k) % groups) for n in range(groups)]
        return [value] + [lax.ppermute(value, "copy", spread(k)) for k in (2, 1, 3)]

    def by_turn(parts):
        return [parts[0], parts[2], parts[1], parts[3]]

    marks, reach = pl.pallas_call(
        functools.partial(marks_kernel, tok=tok, blocks=seq_count),
        in_specs=[SMEM, SMEM, VMEM],
        out_specs=[VMEM, VMEM],
        out_shape=[
            jax.ShapeDtypeStruct((here, 2, 3, slots), jnp.int32),
            jax.ShapeDtypeStruct((3 * tok // slots, slots), jnp.int32),
        ],
        compiler_params=params(8),
        cost_estimate=estimate(8),
        name="visible_marks",
    )(utt_lengths, vis_count, vis_frames)
    marks = by_turn(from_group(marks))

    half_rows = cols // CORES
    out_mine = lax.all_gather(
        lax.dynamic_slice_in_dim(teacher_out, core * half_rows, half_rows, 0), "copy", axis=0
    )

    teacher_in = jnp.swapaxes(teacher_qkv, 1, 2)
    own_out = jax.ShapeDtypeStruct((tok, 3 * wide), bf16)
    own_student, own_teacher, side_student, side_teacher = pl.pallas_call(
        project_kernel,
        in_specs=[VMEM] * 3 + [HBM] * 2,
        out_specs=[VMEM] * 4,
        out_shape=[own_out] * 2 + [jax.ShapeDtypeStruct((2 * tok, 2 * wide), bf16)] * 2,
        scratch_shapes=[
            pltpu.VMEM((3, width, 3 * LANES), bf16),
            pltpu.VMEM(teacher_in.shape, bf16),
            pltpu.SemaphoreType.DMA((6,)),
        ],
        compiler_params=params(OWN_MIB),
        cost_estimate=estimate(7),
        name="project_frames",
    )(frames, left, right, student_weights, teacher_in)

    saved, gathered = [], []
    prob_shape = (heads // 2, 2 * slots, 3 * slots)
    bases = [sum(CHUNKS[:n]) for n in range(len(CHUNKS))]
    for chunk, members in enumerate(CHUNKS):
        extra = 1 if chunk == 0 else 0
        ins = [own_student, side_student]
        out_shape = [
            jax.ShapeDtypeStruct((members // 2 + extra, slots, 2 * cols), bf16),
            jax.ShapeDtypeStruct((members,) + prob_shape, f32),
            jax.ShapeDtypeStruct((members, slots, wide), bf16),
            jax.ShapeDtypeStruct((members, 3 * slots, 2 * wide), bf16),
        ]
        if chunk == 0:
            kernel = forward_first_kernel
            ins += [own_teacher, side_teacher, reach, *marks]
            out_shape += [jax.ShapeDtypeStruct((copies, 3, slots), jnp.int32)] * 2
        elif chunk < len(CHUNKS) - 1:
            kernel = functools.partial(forward_middle_kernel, base=bases[chunk])
            ins += [picks, utts]
        else:
            kernel = functools.partial(forward_last_kernel, base=bases[chunk])
            last_picks, _ = lax.optimization_barrier((picks, attn))
            ins += [last_picks, utts, left, frames, right, student_weights]
            out_shape.append(jax.ShapeDtypeStruct((width, 3 * tok), bf16))
            out_shape.append(jax.ShapeDtypeStruct((width, width), bf16))
        attn, probs, query, kv, *rest = pl.pallas_call(
            kernel,
            in_specs=[HBM if a is student_weights else VMEM for a in ins],
            out_specs=[VMEM] * len(out_shape),
            out_shape=out_shape,
            scratch_shapes=[pltpu.SemaphoreType.DMA] * (chunk == len(CHUNKS) - 1),
            compiler_params=params(LAST_MIB if chunk == len(CHUNKS) - 1 else FORWARD_MIB),
            cost_estimate=estimate(2.5 * extra + 0.9 * members),
            name=f"student_forward{chunk}",
        )(*ins)
        gathered.append(by_turn(from_group(attn)))
        saved.append((probs, query, kv))
        if chunk == len(CHUNKS) - 1:
            turned, w_out = rest
        if chunk == 0:
            picks, utts = rest
            out_late, _ = lax.optimization_barrier((out_mine, attn))
            out_other = lax.ppermute(out_late, "seq", swap)

    targets = pl.pallas_call(
        targets_kernel,
        in_specs=[VMEM] * 7,
        out_specs=VMEM,
        out_shape=jax.ShapeDtypeStruct((tok, width), bf16),
        scratch_shapes=[pltpu.VMEM((groups, tok // 2, 2 * cols), bf16)],
        compiler_params=params(20),
        cost_estimate=estimate(2.5),
        name="teacher_targets",
    )(*gathered[0], out_mine, out_other, frames)

    coef = 2.0 / (width**0.5 * copies)
    results = []
    for chunk, members in enumerate(CHUNKS):
        rows = members * slots
        probs, query, kv = saved[chunk]
        if chunk:
            targets, _ = lax.optimization_barrier((targets, results[-1][1]))
        results.append(
            pl.pallas_call(
                functools.partial(
                    backward_kernel, base=bases[chunk], coef=coef, skip=1 - min(chunk, 1)
                ),
                in_specs=[VMEM] * 11,
                out_specs=[VMEM] * 4,
                out_shape=[
                    jax.ShapeDtypeStruct((rows, width), bf16),
                    jax.ShapeDtypeStruct((rows, cols), bf16),
                    jax.ShapeDtypeStruct((rows, wide), bf16),
                    jax.ShapeDtypeStruct((3, rows, 2 * wide), bf16),
                ],
                scratch_shapes=[
                    pltpu.VMEM((groups, members // 2, slots, 2 * cols), bf16),
                    pltpu.VMEM((rows, width), f32),
                    pltpu.VMEM((rows, width), f32),
                    pltpu.VMEM((rows, width), bf16),
                    pltpu.VMEM((rows, wide), bf16),
                ],
                compiler_params=params(BACKWARD_MIB),
                cost_estimate=estimate(2.7 * members),
                name=f"student_backward{chunk}",
            )(*gathered[chunk], w_out, frames, targets, picks, probs, query, kv)
        )
    turned = turned.reshape(RING, CORES, width // RING // CORES, 3 * tok)
    carried = pl.pallas_call(
        combine_kernel,
        in_specs=[VMEM] * (2 + 4 * len(CHUNKS)),
        out_specs=[VMEM] * 4,
        out_shape=[
            jax.ShapeDtypeStruct((width // CORES, 4 * cols), f32),
            jax.ShapeDtypeStruct((3 * tok, 4 * cols), bf16),
            jax.ShapeDtypeStruct((3 * tok, 2 * cols), bf16),
            jax.ShapeDtypeStruct((RING, CORES, width // RING // CORES, cols), f32),
        ],
        compiler_params=params(COMBINE_MIB),
        cost_estimate=estimate(6),
        name="combine_terms",
    )(picks, turned, *[part[n] for n in range(4) for part in results])

    away, *kept_ins = carried
    arrived = lax.ppermute(away, "seq", swap)
    kept = pl.pallas_call(
        weights_kernel,
        in_specs=[VMEM] * 4,
        out_specs=VMEM,
        out_shape=jax.ShapeDtypeStruct(away.shape, f32),
        compiler_params=params(KEPT_MIB),
        cost_estimate=estimate(2.5),
        name="weights_kept",
    )(turned, *kept_ins)

    ring = RING
    span = CORES * ring

    def z_pairs(k):
        return [
            (n, n // span * span + ((n // CORES + k) % ring) * CORES + n % CORES)
            for n in range(seq_count)
        ]

    def y_pairs(k):
        return [(n, (n + k * span) % seq_count) for n in range(seq_count)]

    def exchange(pieces, pairs_of):
        return [pieces[0]] + [lax.ppermute(pieces[k], "seq", pairs_of(k)) for k in (2, 3, 1)]

    out_rows = width // seq_count
    shaped = lambda *shape: jax.ShapeDtypeStruct(shape, f32)
    sent = jax.ShapeDtypeStruct((2 * out_rows, 2 * cols + LANES), jnp.int32)
    outs = ([shaped(2 * out_rows, 4 * cols)] + [sent] * 3) * 2
    pieces = small_call(first_pieces_kernel, outs, kept.shape, "pieces1", [kept, arrived])
    chains = []
    for n, (first, second) in enumerate(((z_pairs, y_pairs), (y_pairs, z_pairs))):
        part = exchange(pieces[n * ring : (n + 1) * ring], first)
        part = small_call(
            functools.partial(second_pieces_kernel, axis=1 - n),
            [shaped(out_rows, 2 * cols)] * 4,
            (4, out_rows, 2 * cols),
            f"pieces2_{n}",
            part,
        )
        chains += exchange(part, second)
    pieces = chains
    pieces = small_call(
        third_pieces_kernel, [shaped(out_rows, cols)] * 4, (4, out_rows, cols), "pieces3", pieces
    )
    forward = lambda k: [(n, (n + k) % groups) for n in range(groups)]
    pieces = [pieces[0]] + [lax.ppermute(pieces[k], "copy", forward(k)) for k in (1, 2, 3)]
    return small_call(
        last_pieces_kernel, [shaped(out_rows, 4 * cols)], (4, out_rows, cols), "pieces4", pieces
    )[0]


def solution(mesh):
    placed = (
        P("seq", None),
        P(),
        P("copy", None, None),
        P("copy", None),
        P(None, None, "copy"),
        P("copy", None),
        P(),
    )
    return jax.shard_map(
        per_device, mesh=mesh, in_specs=placed, out_specs=P(("seq", "copy"), None), check_vma=False
    )
```
